32 devices in a mesh: row: 4 (over z), kv: 8 (over y, x, core).
Axes of the slice: x: 2, y: 2, z: 4, core: 2. Of those that a mesh axis runs over, the one named last changes fastest.
Arguments:
- hidden: bfloat16 [64, 5120], P(None, 'kv'), may hold values from -6 to 6
- query_weight: bfloat16 [5120, 8192], P('kv', 'row'), may hold values from -0.078125 to 0.078125
- adapter_down_weight: bfloat16 [32, 5120, 16], P(None, 'kv'), may hold values from -0.078125 to 0.078125
- adapter_up_weight: float32 [32, 16, 8192], P(None, None, 'row'), may hold values from -1.5 to 1.5
- query_norm_gain: float32 [128], replicated, may hold values from 0.1 to 1.9
- paged_key_cache: bfloat16 [1024, 128, 8, 128], P('kv', None, 'row'), may hold values from -400 to 400
- paged_value_cache: bfloat16 [1024, 128, 8, 128], P('kv', None, 'row'), may hold values from -6 to 6
- output_weight: bfloat16 [8192, 5120], P('row', 'kv'), may hold values from -0.0625 to 0.0625
- holder: int32 [64, 32], P('kv'), may hold values from 0 to 7, as said below
- holder_block_index: int32 [64, 32], P('kv'), may hold values from 0 to 127
- block_used_length: int32 [64, 32], P('kv'), may hold values from 1 to 128
- tenant: int32 [64], replicated, may hold values from 0 to 63
- tenant_adapter: int32 [64], replicated, may hold values from 0 to 31
Outputs:
- projected: bfloat16 [64, 5120], P('row', 'kv')
The draws below stay inside these ranges and needn't reach their ends.
Inputs may be any that keep to these rules, and one draw needn't show every extreme that they name: At most 64 of the 8 x 32 slots of the rows of one index of kv name one holder; in every draw one holder is named exactly 64 times by the slots of every index.
All inputs are finite; a program needn't handle non-finite values.
Results may differ from the reference program's by a relative error of at most 0.0159.
The reference program's roundings to bfloat16 on the way count: a program that leaves them out, or rounds other values in their place, can miss the bound.
Values may be sent and summed in bfloat16 or wider, within the bound.
No kernel may reach another device: no remote copies, remote signals or barrier semaphores. Data moves between devices by JAX's collectives and lax.ppermute only.
A program may use at most 256 MiB of HBM per device.

```python
import math
import jax
import jax.numpy as jnp
from jax import lax

MODEL_WIDTH = 5120
QUERY_HEADS = 64
KVH = 8
HEAD_WIDTH = 128
ADAPTER_RANK = 16
ADAPTER_COUNT = 32
TENANTS = 64
BLOCK = 128
BPR = 32
ROWS_DEV = 8
BLK_DEV = 128
CAP = 64
ROWS = 64
BLOCKS = 1024
N_KV = 8


def draw_paged_key_cache(key, part):
    key = jax.random.fold_in(key, 5)
    noise_key = jax.random.fold_in(key, 0)
    values = jax.random.truncated_normal(noise_key, -6.0, 6.0, (BLOCKS, BLOCK, KVH, HEAD_WIDTH), jnp.float32)
    return values.astype(jnp.bfloat16)


def draw_holder(key, part):
    key = jax.random.fold_in(key, 7)
    hot_key, device_key = jax.random.split(key)
    hot_holder = jax.random.randint(hot_key, (), 0, N_KV)
    seat_owner = (jnp.arange(N_KV * CAP, dtype=jnp.int32) // CAP + hot_holder) % N_KV

    def one_device(device_seed):
        order_key, place_key = jax.random.split(device_seed)
        remaining = jax.random.permutation(order_key, N_KV * CAP - CAP) + CAP
        seats = jnp.concatenate([jnp.arange(CAP, dtype=jnp.int32), remaining.astype(jnp.int32)])[:ROWS_DEV * BPR]
        chosen = seat_owner[seats]
        return jax.random.permutation(place_key, chosen).reshape(ROWS_DEV, BPR)
    drawn = jax.vmap(one_device)(jax.random.split(device_key, N_KV))
    return drawn.reshape(ROWS, BPR).astype(jnp.int32)


def plant(entries, key, least, top_value):
    spot = [jax.random.randint(jax.random.fold_in(key, axis), (), 0, length) for axis, length in enumerate(entries.shape)]
    widest = entries.shape.index(max(entries.shape))
    neighbour = spot[:widest] + [(spot[widest] + 1) % entries.shape[widest]] + spot[widest + 1:]
    return entries.at[tuple(spot)].set(least).at[tuple(neighbour)].set(top_value)


def levels(rng, dims, cuts, low, largest):
    def one(dim, parts):
        steps = jax.random.uniform(jax.random.fold_in(jax.random.fold_in(rng, 6), dim), (parts,), jnp.float32, low / len(cuts), largest / len(cuts))
        return jnp.repeat(jnp.exp(steps), dims[dim] // parts).reshape((-1,) + (1,) * (len(dims) - dim - 1))

    loudness = one(*cuts[0])
    for cut in cuts[1:]:
        loudness = loudness * one(*cut)
    return loudness


def gaussian(stream_key, extent, width, reach, cuts=(), kind=jnp.bfloat16):
    gain = levels(stream_key, extent, cuts, -0.22, 0.18) if cuts else 1.0
    array = jax.random.normal(stream_key, extent, jnp.float32) * width * gain
    return jnp.minimum(jnp.maximum(array, -reach), reach).astype(kind)


def setup_inputs(seed: int = 0) -> dict:
    key_of = jax.random.split(jax.random.key(seed), 14)
    return {
        "hidden": gaussian(key_of[0], (ROWS, MODEL_WIDTH), 1.0, 6.0, ((1, 8),)),
        "query_weight": gaussian(key_of[1], (MODEL_WIDTH, QUERY_HEADS * HEAD_WIDTH), MODEL_WIDTH ** -0.5, 0.078125, ((0, 8), (1, 4))),
        "adapter_down_weight": gaussian(key_of[2], (ADAPTER_COUNT, MODEL_WIDTH, ADAPTER_RANK), MODEL_WIDTH ** -0.5, 0.078125, ((1, 8),)),
        "adapter_up_weight": gaussian(key_of[3], (ADAPTER_COUNT, ADAPTER_RANK, QUERY_HEADS * HEAD_WIDTH), ADAPTER_RANK ** -0.5, 1.5, ((2, 4),), jnp.float32),
        "query_norm_gain": jnp.clip(1.0 + 0.18 * jax.random.normal(key_of[4], (HEAD_WIDTH,), jnp.float32), 0.1, 1.9),
        "paged_key_cache": draw_paged_key_cache(jax.random.fold_in(key_of[13], 71), 0),
        "paged_value_cache": gaussian(key_of[6], (BLOCKS, BLOCK, KVH, HEAD_WIDTH), 1.0, 6.0, ((0, 8), (2, 4))),
        "output_weight": gaussian(key_of[7], (QUERY_HEADS * HEAD_WIDTH, MODEL_WIDTH), (QUERY_HEADS * HEAD_WIDTH) ** -0.5, 0.0625, ((0, 4), (1, 8))),
        "holder": draw_holder(jax.random.fold_in(key_of[13], 71), 0),
        "holder_block_index": plant(jax.random.randint(key_of[9], (ROWS, BPR), 0, BLK_DEV), jax.random.fold_in(key_of[9], 1), 0, BLK_DEV - 1).astype(jnp.int32),
        "block_used_length": plant(jax.random.randint(key_of[10], (ROWS, BPR), 1, BLOCK + 1), jax.random.fold_in(key_of[10], 1), 1, BLOCK).astype(jnp.int32),
        "tenant": plant(jax.random.randint(key_of[11], (ROWS,), 0, TENANTS), jax.random.fold_in(key_of[11], 1), 0, TENANTS - 1).astype(jnp.int32),
        "tenant_adapter": plant(jax.random.randint(key_of[12], (TENANTS,), 0, ADAPTER_COUNT), jax.random.fold_in(key_of[12], 1), 0, ADAPTER_COUNT - 1).astype(jnp.int32),
    }


ADAPTER_SCALE = 0.5
ROPE_BASE = 1000000.0
EPSILON = 1e-06
NEG_FILL = -1e+30

def rotate_half(query, position):
    half_width = query.shape[-1] // 2
    frequency = ROPE_BASE ** (-(jnp.arange(half_width, dtype=jnp.float32) * 2.0) / query.shape[-1])
    angles = position[:, None] * frequency[None, :]
    cosine = jnp.concatenate([jnp.cos(angles), jnp.cos(angles)], axis=-1)[:, None, :]
    sine_part = jnp.concatenate([jnp.sin(angles), jnp.sin(angles)], axis=-1)[:, None, :]
    first_half = query[..., :half_width]
    second_half = query[..., half_width:]
    turned = jnp.concatenate([-second_half, first_half], axis=-1)
    return query * cosine + turned * sine_part

def prepare_queries(query_linear, query_norm_gain, block_used_length):
    row_count = query_linear.shape[0]
    head_size = query_norm_gain.shape[0]
    query = query_linear.reshape(row_count, query_linear.shape[1] // head_size, head_size)
    squares = lax.optimization_barrier(jnp.mean(query * query, axis=-1, keepdims=True))
    query = query * lax.rsqrt(squares + EPSILON) * query_norm_gain
    position = (lax.optimization_barrier(jnp.sum(block_used_length, axis=1)) - 1).astype(jnp.float32)
    return rotate_half(query, position).astype(jnp.bfloat16)

def merge_blocks(block_out, block_top, block_total, axis):
    overall = lax.optimization_barrier(jnp.max(block_top, axis=axis, keepdims=True))
    factors = jnp.exp(block_top - overall)
    numerator = lax.optimization_barrier(jnp.sum(factors[..., None] * block_out, axis=axis))
    denominator = lax.optimization_barrier(jnp.sum(factors * block_total, axis=axis))
    return numerator / denominator[..., None]

def reference(hidden, query_weight, adapter_down_weight, adapter_up_weight, query_norm_gain, paged_key_cache, paged_value_cache, output_weight, holder, holder_block_index, block_used_length, tenant, tenant_adapter):
    adapter_per_row = tenant_adapter[tenant]
    base_product = jnp.dot(hidden, query_weight, preferred_element_type=jnp.float32)
    down_projected_rows = adapter_down_weight[adapter_per_row]
    reduced_rank_rows = jnp.einsum('rd,rdk->rk', hidden.astype(jnp.float32), down_projected_rows.astype(jnp.float32))
    up_projected_rows = adapter_up_weight[adapter_per_row]
    adapter_product = jnp.einsum('wi,wio->wo', reduced_rank_rows, up_projected_rows, precision=lax.Precision.HIGHEST)
    query_linear = base_product + ADAPTER_SCALE * adapter_product
    queries = lax.optimization_barrier(prepare_queries(query_linear, query_norm_gain, block_used_length))
    global_blocks = (holder * BLK_DEV + holder_block_index).astype(jnp.int32)

    def attend_row(operands):
        query, blocks, lengths = operands
        keys = paged_key_cache[blocks].astype(jnp.float32)
        values = paged_value_cache[blocks].astype(jnp.float32)
        grouped = query.astype(jnp.float32).reshape(KVH, QUERY_HEADS // KVH, HEAD_WIDTH)
        scores = jnp.einsum('agd,btad->bagt', grouped, keys) * (1.0 / math.sqrt(HEAD_WIDTH))
        token_mask = (jnp.arange(BLOCK, dtype=jnp.int32)[None, :] < lengths[:, None])[:, None, None, :]
        block_top = lax.optimization_barrier(jnp.max(jnp.where(token_mask, scores, NEG_FILL), axis=-1))
        weights = jnp.where(token_mask, jnp.exp(scores - block_top[..., None]), 0.0)
        block_total = lax.optimization_barrier(jnp.sum(weights, axis=-1))
        rounded = lax.optimization_barrier(weights.astype(jnp.bfloat16))
        block_out = jnp.einsum('bagt,btad->bagd', rounded.astype(jnp.float32), values)
        return merge_blocks(block_out, block_top, block_total, 0).reshape(QUERY_HEADS * HEAD_WIDTH)
    attention = lax.map(attend_row, (queries, global_blocks, block_used_length)).astype(jnp.bfloat16)
    return jnp.dot(attention, output_weight, preferred_element_type=jnp.float32).astype(jnp.bfloat16)
```

```python
import functools
import math

import jax
import jax.numpy as jnp
from jax import lax
from jax.experimental import pallas as pl
from jax.experimental.pallas import tpu as pltpu
from jax.sharding import PartitionSpec as P

ADAPTER_SCALE = 0.5
ROPE_BASE = 1000000.0
EPSILON = 1e-06
NEG_FILL = -1e30
LANES = 128
COLUMN_TILE = 256
UNROLL = 8
LOG2E = math.log2(math.e)
MIB = 1024 * 1024


def params(mib):
    return pltpu.CompilerParams(vmem_limit_bytes=mib * MIB)


def vmem_spec():
    return pl.BlockSpec(memory_space=pltpu.VMEM)


def smem_spec():
    return pl.BlockSpec(memory_space=pltpu.SMEM)


def split2(x):
    high = x.astype(jnp.bfloat16)
    return high, (x - high.astype(jnp.float32)).astype(jnp.bfloat16)


def split3(x):
    high = x.astype(jnp.bfloat16).astype(jnp.float32)
    rest = x - high
    middle = rest.astype(jnp.bfloat16).astype(jnp.float32)
    return high, middle, (rest - middle).astype(jnp.bfloat16).astype(jnp.float32)


def to_column(row, count):
    shape = (count, count)
    eye = lax.broadcasted_iota(jnp.int32, shape, 0) == lax.broadcasted_iota(jnp.int32, shape, 1)
    return jnp.sum(jnp.where(eye, row.astype(jnp.float32), 0.0), axis=1, keepdims=True)


def project_kernel(
    rank, tenant_ref, adapter_ref, slots_ref, hidden_ref, weight_ref, down_ref, up_ref, out_ref, high_ref, low_ref
):
    step = pl.program_id(0)
    rows = hidden_ref.shape[0]
    width = pl.num_programs(0) * weight_ref.shape[1]
    nt = (((1,), (1,)), ((), ()))

    @pl.when(step == 0)
    def _():
        tenants = adapter_ref.shape[1]
        tenant = to_column(tenant_ref[...], rows)
        pick = lax.broadcasted_iota(jnp.int32, (rows, tenants), 1).astype(jnp.float32) == tenant
        adapter = jnp.sum(
            jnp.where(pick, adapter_ref[...].astype(jnp.float32), 0.0), axis=1, keepdims=True
        ).astype(jnp.int32)
        low = lax.dot_general(hidden_ref[...], down_ref[...], nt, preferred_element_type=jnp.float32)
        column = lax.broadcasted_iota(jnp.int32, low.shape, 1)
        match = (column >= adapter * rank) & (column < adapter * rank + rank)
        high_part, low_part = split2(jnp.where(match, ADAPTER_SCALE * low, 0.0))
        high_ref[...] = high_part
        low_ref[...] = low_part
        own = slots_ref.shape[0]
        for start in range(0, rows, own):
            out_ref[start : start + own, width:] = slots_ref[...]

    up_high, up_low = split2(up_ref[...])
    total = jnp.dot(hidden_ref[...], weight_ref[...], preferred_element_type=jnp.float32)
    total += jnp.dot(low_ref[...], up_high, preferred_element_type=jnp.float32)
    total += jnp.dot(high_ref[...], up_low, preferred_element_type=jnp.float32)
    total += jnp.dot(high_ref[...], up_high, preferred_element_type=jnp.float32)
    tile = weight_ref.shape[1]
    out_ref[:, pl.ds(pl.multiple_of(step * tile, tile), tile)] = total


def project(hidden, query_weight, down, up, tenant, tenant_adapter, slots, rank):
    rows, depth = hidden.shape
    width = query_weight.shape[1]
    low_width = down.shape[0]
    whole = lambda shape: pl.BlockSpec(shape, lambda i: (0,) * len(shape))
    return pl.pallas_call(
        functools.partial(project_kernel, rank),
        grid=(width // COLUMN_TILE,),
        in_specs=[
            whole(tenant.shape),
            whole(tenant_adapter.shape),
            whole(slots.shape),
            whole(hidden.shape),
            pl.BlockSpec((depth, COLUMN_TILE), lambda i: (0, i)),
            whole(down.shape),
            pl.BlockSpec((low_width, COLUMN_TILE), lambda i: (0, i)),
        ],
        out_specs=whole((rows, width + LANES)),
        out_shape=jax.ShapeDtypeStruct((rows, width + LANES), jnp.float32),
        scratch_shapes=[
            pltpu.VMEM((rows, low_width), jnp.bfloat16),
            pltpu.VMEM((rows, low_width), jnp.bfloat16),
        ],
        compiler_params=params(16),
        cost_estimate=pl.CostEstimate(
            flops=2 * rows * width * (depth + 3 * low_width),
            bytes_accessed=2 * depth * width + 4 * low_width * width,
            transcendentals=0,
        ),
        name="project",
    )(tenant, tenant_adapter, slots, hidden, query_weight, down, up)


def queries_kernel(parts_ref, cosine_ref, sine_ref, gain_ref, out_ref, turned_ref):
    heads = turned_ref.shape[1]
    copies = out_ref.shape[0]
    cosine, sine, gain = cosine_ref[...], sine_ref[...], gain_ref[...]
    for h in range(heads):
        columns = slice(h * LANES, (h + 1) * LANES)
        query = parts_ref[0, :, columns]
        for s in range(1, parts_ref.shape[0]):
            query = query + parts_ref[s, :, columns]
        square = jnp.mean(query * query, axis=-1, keepdims=True)
        query = query * lax.rsqrt(square + EPSILON) * gain
        turned_ref[:, h, :] = query * cosine + pltpu.roll(query, LANES // 2, 1) * sine
    result = turned_ref[...].astype(jnp.bfloat16)
    for c in range(copies):
        out_ref[c] = result


def make_queries(parts, cosine, sine, gain, heads):
    count, own, _ = parts.shape
    return pl.pallas_call(
        queries_kernel,
        in_specs=[vmem_spec()] * 4,
        out_specs=vmem_spec(),
        out_shape=jax.ShapeDtypeStruct((count, own, heads, LANES), jnp.bfloat16),
        scratch_shapes=[pltpu.VMEM((own, heads, LANES), jnp.float32)],
        compiler_params=params(16),
        name="queries",
    )(parts, cosine, sine, gain)


def list_kernel(block_size, slots, packed_ref, list_ref, count_ref):
    total = packed_ref.shape[0]
    capacity = list_ref.shape[0]
    rows = total // slots
    shift = block_size * LANES

    def step(i, position):
        for j in range(UNROLL):
            entry = i * UNROLL + j
            value = packed_ref[entry]
            list_ref[position] = value + (entry // slots) * shift
            position = position + (value >= 0).astype(jnp.int32)
        return position

    count = lax.fori_loop(0, total // UNROLL, step, jnp.int32(0))
    count_ref[0] = count

    def fill(i, carry):
        list_ref[count + i] = rows * shift
        return carry

    lax.fori_loop(0, UNROLL, fill, 0)


def make_list(packed, capacity, block_size, slots):
    return pl.pallas_call(
        functools.partial(list_kernel, block_size, slots),
        in_specs=[smem_spec()],
        out_specs=[smem_spec(), smem_spec()],
        out_shape=[
            jax.ShapeDtypeStruct((capacity,), jnp.int32),
            jax.ShapeDtypeStruct((1,), jnp.int32),
        ],
        compiler_params=params(16),
        cost_estimate=pl.CostEstimate(flops=10**8, bytes_accessed=10**7, transcendentals=0),
        name="slot_list",
    )(packed)


def attend_kernel(
    scale, group, kv_local, list_ref, count_ref, query_ref, key_ref, value_ref, out_ref, top_ref, total_ref, sum_ref
):
    rows, heads, _ = query_ref.shape
    tokens = key_ref.shape[1]
    block_size = tokens // kv_local
    shift = block_size * LANES
    factor = scale * LOG2E
    top_ref[...] = jnp.full(top_ref.shape, NEG_FILL, jnp.float32)
    total_ref[...] = jnp.zeros(total_ref.shape, jnp.float32)
    sum_ref[...] = jnp.zeros(sum_ref.shape, jnp.float32)
    head = lax.broadcasted_iota(jnp.int32, (heads, tokens), 0) // group
    place = lax.broadcasted_iota(jnp.int32, (heads, tokens), 1)
    token = jnp.where(place % kv_local == head, place // kv_local, block_size)
    nt = (((1,), (1,)), ((), ()))

    def chunk(i, carry):
        before, top, total, acc = carry
        row, block, length = [], [], []
        for j in range(UNROLL):
            entry = list_ref[i * UNROLL + j]
            row.append(entry // shift)
            block.append((entry // block_size) % LANES)
            length.append(entry % block_size + 1)
        scores = [
            lax.dot_general(
                query_ref[jnp.minimum(row[j], rows - 1)], key_ref[block[j]], nt, preferred_element_type=jnp.float32
            )
            for j in range(UNROLL)
        ]
        scores = [jnp.where(token < length[j], scores[j], NEG_FILL) for j in range(UNROLL)]
        tops = [jnp.max(s, axis=1, keepdims=True) for s in scores]
        weights = [jnp.exp2((scores[j] - tops[j]) * factor) for j in range(UNROLL)]
        totals = [jnp.sum(w, axis=1, keepdims=True) for w in weights]
        outs = [
            jnp.dot(weights[j].astype(jnp.bfloat16), value_ref[block[j]], preferred_element_type=jnp.float32)
            for j in range(UNROLL)
        ]
        for j in range(UNROLL):
            fresh = row[j] != before
            top = jnp.where(fresh, NEG_FILL, top)
            total = jnp.where(fresh, 0.0, total)
            acc = jnp.where(fresh, 0.0, acc)
            high = jnp.maximum(top, tops[j])
            old = jnp.exp2((top - high) * factor)
            new = jnp.exp2((tops[j] - high) * factor)
            total = total * old + totals[j] * new
            acc = acc * old + outs[j] * new
            top = high
            before = row[j]
            top_ref[row[j]] = top
            total_ref[row[j]] = total
            sum_ref[row[j]] = acc
        return before, top, total, acc

    wide = jnp.zeros((heads, LANES), jnp.float32)
    count = count_ref[0]
    lax.fori_loop(0, (count + UNROLL - 1) // UNROLL, chunk, (jnp.int32(-1), wide, wide, wide))

    copies, sections, _, _ = out_ref.shape
    own = sections - 1
    square = (own * heads, LANES)
    eye = lax.broadcasted_iota(jnp.int32, square, 0) == lax.broadcasted_iota(jnp.int32, square, 1)
    line = lax.broadcasted_iota(jnp.int32, (heads, LANES), 0)
    for c in range(copies):
        stats = jnp.zeros((heads, LANES), jnp.float32)
        position = 0
        for ref in (top_ref, total_ref):
            flat = jnp.sum(
                jnp.where(eye, ref[c * own : (c + 1) * own].reshape(square), 0.0), axis=0, keepdims=True
            )
            for piece in split3(flat):
                stats = jnp.where(line == position, piece, stats)
                position += 1
        for r in range(own):
            out_ref[c, r] = sum_ref[c * own + r].astype(jnp.bfloat16)
        out_ref[c, own] = stats.astype(jnp.bfloat16)


def attend(items, count, queries, keys, values, copies, kv_local, scale):
    rows, heads, _ = queries.shape
    own = rows // copies
    keys = pltpu.with_memory_space_constraint(keys, pltpu.VMEM)
    values = pltpu.with_memory_space_constraint(values, pltpu.VMEM)
    state = pltpu.VMEM((rows + 1, heads, LANES), jnp.float32)
    return pl.pallas_call(
        functools.partial(attend_kernel, scale, heads // kv_local, kv_local),
        in_specs=[smem_spec(), smem_spec(), vmem_spec(), vmem_spec(), vmem_spec()],
        out_specs=vmem_spec(),
        out_shape=jax.ShapeDtypeStruct((copies, own + 1, heads, LANES), jnp.bfloat16),
        scratch_shapes=[state, state, state],
        compiler_params=params(28),
        name="attend",
    )(items, count, queries, keys, values)


def merge_kernel(scale, parts_ref, out_ref, wide_ref):
    count, sections, heads, _ = parts_ref.shape
    own = sections - 1
    factor = scale * LOG2E
    stats = [parts_ref[s, own].astype(jnp.float32) for s in range(count)]
    tops = jnp.concatenate([s[0:1] + s[1:2] + s[2:3] for s in stats], axis=0)
    totals = jnp.concatenate([s[3:4] + s[4:5] + s[5:6] for s in stats], axis=0)
    weights = jnp.exp2((tops - jnp.max(tops, axis=0, keepdims=True)) * factor)
    weights = weights / jnp.sum(weights * totals, axis=0, keepdims=True)
    columns = weights.T
    acc = jnp.zeros((own * heads, LANES), jnp.float32)
    for s in range(count):
        part = parts_ref[s, :own].astype(jnp.float32).reshape(own * heads, LANES)
        acc = acc + part * columns[:, s : s + 1]
    wide_ref[...] = acc
    pieces = [wide_ref[pl.ds(h, own, stride=heads), :] for h in range(heads)]
    result = jnp.concatenate(pieces, axis=1).astype(jnp.bfloat16)
    for c in range(out_ref.shape[0]):
        out_ref[c] = result


def merge(parts, scale):
    count, sections, heads, _ = parts.shape
    own = sections - 1
    return pl.pallas_call(
        functools.partial(merge_kernel, scale),
        in_specs=[vmem_spec()],
        out_specs=vmem_spec(),
        out_shape=jax.ShapeDtypeStruct((count, own, heads * LANES), jnp.bfloat16),
        scratch_shapes=[pltpu.VMEM((own * heads, LANES), jnp.float32)],
        compiler_params=params(16),
        name="merge",
    )(parts)


def swap(x, axis):
    return lax.all_to_all(x, axis, split_axis=0, concat_axis=0, tiled=True)


def local(
    hidden,
    query_weight,
    adapter_down_weight,
    adapter_up_weight,
    query_norm_gain,
    paged_key_cache,
    paged_value_cache,
    output_weight,
    holder,
    holder_block_index,
    block_used_length,
    tenant,
    tenant_adapter,
):
    own, slots = holder.shape
    rows, depth = hidden.shape
    kv_count = lax.axis_size("kv")
    row_count = lax.axis_size("row")
    adapters, _, rank = adapter_down_weight.shape
    width = query_weight.shape[1]
    head_size = query_norm_gain.shape[0]
    heads = width // head_size
    blocks, block_size, kv_local, _ = paged_key_cache.shape
    scale = 1.0 / math.sqrt(head_size)

    fields = jnp.concatenate(
        [holder, holder_block_index, block_used_length, jnp.zeros((own, LANES - 3 * slots), jnp.int32)], axis=1
    ).astype(jnp.float32)
    down = jnp.swapaxes(adapter_down_weight, 1, 2).reshape(adapters * rank, depth)
    up = adapter_up_weight.reshape(adapters * rank, width)
    partial = project(
        hidden, query_weight, down, up, tenant.reshape(1, rows), tenant_adapter.reshape(1, -1), fields, rank
    )
    parts = swap(partial.reshape(kv_count, own, width + LANES), "kv")

    position = (jnp.sum(block_used_length, axis=1) - 1).astype(jnp.float32)
    half = head_size // 2
    frequency = ROPE_BASE ** (-(jnp.arange(half, dtype=jnp.float32) * 2.0) / head_size)
    angles = position[:, None] * frequency[None, :]
    cosine = jnp.concatenate([jnp.cos(angles), jnp.cos(angles)], axis=-1)
    sine = jnp.concatenate([-jnp.sin(angles), jnp.sin(angles)], axis=-1)
    queries = make_queries(parts, cosine, sine, query_norm_gain.reshape(1, head_size), heads)
    queries = swap(queries, "kv").reshape(rows, heads, head_size)

    numbers = parts[:, :, width:].astype(jnp.int32).reshape(rows, LANES)
    holders, numbers, lengths = (numbers[:, i * slots : (i + 1) * slots] for i in range(3))
    packed = jnp.where(
        holders == lax.axis_index("kv"), numbers * block_size + lengths - 1, -rows * block_size * LANES
    ).reshape(rows * slots)
    entries = own * slots
    capacity = 2 * entries // kv_count * kv_count + 2 * UNROLL
    items, count = make_list(packed, capacity, block_size, slots)

    keys = paged_key_cache.reshape(blocks, block_size * kv_local, head_size)
    values = paged_value_cache.reshape(blocks, block_size * kv_local, head_size)
    partial_out = attend(items, count, queries, keys, values, kv_count, kv_local, scale)
    attention = merge(swap(partial_out, "kv"), scale)
    attention = swap(attention, "kv").reshape(rows, width)
    terms = jnp.dot(attention, output_weight, preferred_element_type=jnp.float32).astype(jnp.bfloat16)
    terms = swap(terms.reshape(row_count, rows // row_count, -1), "row")
    return jnp.sum(terms.astype(jnp.float32), axis=0).astype(jnp.bfloat16)


def solution(mesh):
    return jax.shard_map(
        local,
        mesh=mesh,
        in_specs=(
            P(None, "kv"),
            P("kv", "row"),
            P(None, "kv", None),
            P(None, None, "row"),
            P(),
            P("kv", None, "row", None),
            P("kv", None, "row", None),
            P("row", "kv"),
            P("kv", None),
            P("kv", None),
            P("kv", None),
            P(),
            P(),
        ),
        out_specs=P("row", "kv"),
        check_vma=False,
    )
```

```python
import functools
import math

import jax
import jax.numpy as jnp
from jax import lax
from jax.experimental import pallas as pl
from jax.experimental.pallas import tpu as pltpu
from jax.sharding import PartitionSpec as P

ADAPTER_SCALE = 0.5
ROPE_BASE = 1000000.0
EPSILON = 1e-06
NEG_FILL = -1e30
LANES = 128
COLUMN_TILE = 256
UNROLL = 16
PHASES = 4
LOG2E = math.log2(math.e)
MIB = 1024 * 1024


def params(mib):
    return pltpu.CompilerParams(vmem_limit_bytes=mib * MIB)


def vmem_spec():
    return pl.BlockSpec(memory_space=pltpu.VMEM)


def in_hbm(*arrays):
    return [pltpu.with_memory_space_constraint(x, pltpu.HBM) for x in arrays]


def smem_spec():
    return pl.BlockSpec(memory_space=pltpu.SMEM)


def split2(x):
    high = x.astype(jnp.bfloat16)
    return high, (x - high.astype(jnp.float32)).astype(jnp.bfloat16)


def split3(x):
    high = x.astype(jnp.bfloat16).astype(jnp.float32)
    rest = x - high
    middle = rest.astype(jnp.bfloat16).astype(jnp.float32)
    return high, middle, (rest - middle).astype(jnp.bfloat16).astype(jnp.float32)


def to_column(row, count):
    shape = (count, count)
    eye = lax.broadcasted_iota(jnp.int32, shape, 0) == lax.broadcasted_iota(jnp.int32, shape, 1)
    return jnp.sum(jnp.where(eye, row.astype(jnp.float32), 0.0), axis=1, keepdims=True)


def project_kernel(
    rank,
    tenant_ref,
    adapter_ref,
    holder_ref,
    block_ref,
    length_ref,
    hidden_ref,
    weight_ref,
    down_ref,
    up_ref,
    out_ref,
    high_ref,
    low_ref,
):
    step = pl.program_id(0)
    rows = hidden_ref.shape[0]
    width = pl.num_programs(0) * weight_ref.shape[1]
    nt = (((1,), (1,)), ((), ()))

    @pl.when(step == 0)
    def _():
        tenants = adapter_ref.shape[1]
        tenant = to_column(tenant_ref[...], rows)
        pick = lax.broadcasted_iota(jnp.int32, (rows, tenants), 1).astype(jnp.float32) == tenant
        adapter = jnp.sum(
            jnp.where(pick, adapter_ref[...].astype(jnp.float32), 0.0), axis=1, keepdims=True
        ).astype(jnp.int32)
        low = lax.dot_general(hidden_ref[...], down_ref[...], nt, preferred_element_type=jnp.float32)
        column = lax.broadcasted_iota(jnp.int32, low.shape, 1)
        match = (column >= adapter * rank) & (column < adapter * rank + rank)
        high_part, low_part = split2(jnp.where(match, ADAPTER_SCALE * low, 0.0))
        high_ref[...] = high_part
        low_ref[...] = low_part
        own, slots = holder_ref.shape
        numbers = [holder_ref[...], block_ref[...], length_ref[...], jnp.zeros((own, LANES - 3 * slots), jnp.int32)]
        numbers = jnp.concatenate(numbers, axis=1).astype(jnp.float32)
        for start in range(0, rows, own):
            out_ref[start : start + own, width:] = numbers

    up_high, up_low = split2(up_ref[...])
    total = jnp.dot(hidden_ref[...], weight_ref[...], preferred_element_type=jnp.float32)
    total += jnp.dot(low_ref[...], up_high, preferred_element_type=jnp.float32)
    total += jnp.dot(high_ref[...], up_low, preferred_element_type=jnp.float32)
    total += jnp.dot(high_ref[...], up_high, preferred_element_type=jnp.float32)
    tile = weight_ref.shape[1]
    out_ref[:, pl.ds(pl.multiple_of(step * tile, tile), tile)] = total


def project(tenant, tenant_adapter, holder, block, length, hidden, query_weight, down, up, rank):
    rows, depth = hidden.shape
    width = query_weight.shape[1]
    low_width = down.shape[0]
    whole = lambda shape: pl.BlockSpec(shape, lambda i: (0,) * len(shape))
    operands = in_hbm(tenant, tenant_adapter, holder, block, length, hidden, query_weight, down, up)
    specs = [whole(x.shape) for x in operands]
    specs[6] = pl.BlockSpec((depth, COLUMN_TILE), lambda i: (0, i))
    specs[8] = pl.BlockSpec((low_width, COLUMN_TILE), lambda i: (0, i))
    return pl.pallas_call(
        functools.partial(project_kernel, rank),
        grid=(width // COLUMN_TILE,),
        in_specs=specs,
        out_specs=whole((rows, width + LANES)),
        out_shape=pltpu.HBM((rows, width + LANES), jnp.float32),
        scratch_shapes=[
            pltpu.VMEM((rows, low_width), jnp.bfloat16),
            pltpu.VMEM((rows, low_width), jnp.bfloat16),
        ],
        compiler_params=params(16),
        cost_estimate=pl.CostEstimate(
            flops=2 * rows * width * (depth + 3 * low_width),
            bytes_accessed=2 * depth * width + 4 * low_width * width,
            transcendentals=0,
        ),
        name="project",
    )(*operands)


def queries_kernel(parts_ref, cosine_ref, sine_ref, gain_ref, out_ref, turned_ref):
    heads = turned_ref.shape[1]
    copies = out_ref.shape[0]
    cosine, sine, gain = cosine_ref[...], sine_ref[...], gain_ref[...]
    for h in range(heads):
        columns = slice(h * LANES, (h + 1) * LANES)
        query = parts_ref[0, :, columns]
        for s in range(1, parts_ref.shape[0]):
            query = query + parts_ref[s, :, columns]
        square = jnp.mean(query * query, axis=-1, keepdims=True)
        query = query * lax.rsqrt(square + EPSILON) * gain
        turned_ref[:, h, :] = query * cosine + pltpu.roll(query, LANES // 2, 1) * sine
    result = turned_ref[...].astype(jnp.bfloat16)
    for c in range(copies):
        out_ref[c] = result


def make_queries(parts, cosine, sine, gain, heads):
    count, own, _ = parts.shape
    shape = (count, own, heads, LANES)
    return pl.pallas_call(
        queries_kernel,
        grid=(1,),
        in_specs=[vmem_spec()] * 4,
        out_specs=pl.BlockSpec(shape, lambda i: (0, 0, 0, 0)),
        out_shape=pltpu.HBM(shape, jnp.bfloat16),
        scratch_shapes=[pltpu.VMEM((own, heads, LANES), jnp.float32)],
        compiler_params=params(16),
        name="queries",
    )(parts, cosine, sine, gain)


def list_kernel(blocks, block_size, slots, numbers_ref, list_ref, bound_ref, place_ref, value_ref):
    rows = place_ref.shape[0]
    capacity = list_ref.shape[1]
    me = lax.axis_index("kv").astype(jnp.float32)
    numbers = numbers_ref[...].reshape(rows, LANES)
    holder, block, length = (numbers[:, i * slots : (i + 1) * slots] for i in range(3))
    row = lax.broadcasted_iota(jnp.int32, (rows, slots), 0).astype(jnp.float32)
    spare = float(rows * blocks * block_size)
    value_ref[...] = (row * blocks + block) * block_size + (length - 1.0) - spare

    def before(count, axis):
        first = lax.broadcasted_iota(jnp.int32, (count, count), axis)
        return jnp.where(first < lax.broadcasted_iota(jnp.int32, (count, count), 1 - axis), 1.0, 0.0).astype(
            jnp.bfloat16
        )

    slot_before, row_before = before(slots, 0), before(rows, 1)
    place = jnp.full((rows, slots), -1.0, jnp.float32)
    base = jnp.zeros((1, 1), jnp.float32)
    lane = lax.broadcasted_iota(jnp.int32, (1, LANES), 1)
    bounds = jnp.zeros((1, LANES), jnp.float32)
    size = blocks // PHASES
    for part in range(PHASES):
        inside = (holder == me) & (block >= part * size) & (block < (part + 1) * size)
        ones = jnp.where(inside, 1.0, 0.0)
        flags = ones.astype(jnp.bfloat16)
        within = jnp.dot(flags, slot_before, preferred_element_type=jnp.float32)
        above = jnp.sum(jnp.dot(row_before, flags, preferred_element_type=jnp.float32), axis=1, keepdims=True)
        place = jnp.where(inside, base + above + within, place)
        count = jnp.sum(jnp.sum(ones, axis=1, keepdims=True), axis=0, keepdims=True)
        base = base + jnp.ceil(count * (1.0 / UNROLL)) * UNROLL
        bounds = jnp.where(lane == part + 1, base * (1.0 / UNROLL), bounds)
    bound_ref[...] = bounds.astype(jnp.int32)
    place_ref[...] = place
    target = lax.broadcasted_iota(jnp.int32, (8, capacity), 1).astype(jnp.float32)

    def tile(t, total):
        here = pl.ds(pl.multiple_of(t * 8, 8), 8)
        places, values = place_ref[here, :], value_ref[here, :]
        for j in range(slots):
            total = total + jnp.where(places[:, j : j + 1] == target, values[:, j : j + 1], 0.0)
        return total

    total = lax.fori_loop(0, rows // 8, tile, jnp.zeros((8, capacity), jnp.float32))
    list_ref[...] = (jnp.sum(total, axis=0, keepdims=True) + spare).astype(jnp.int32)


def make_list(parts, slots, blocks, block_size):
    count, own, width = parts.shape
    rows = count * own
    most = 2 * own * slots // count * count + (PHASES + 2) * UNROLL
    capacity = -(-most // LANES) * LANES
    last = width // LANES - 1
    return pl.pallas_call(
        functools.partial(list_kernel, blocks, block_size, slots),
        grid=(1,),
        in_specs=[pl.BlockSpec((count, own, LANES), lambda i: (0, 0, last))],
        out_specs=[
            pl.BlockSpec((1, capacity), lambda i: (0, 0)),
            pl.BlockSpec((1, LANES), lambda i: (0, 0)),
        ],
        out_shape=[
            jax.ShapeDtypeStruct((1, capacity), jnp.int32),
            jax.ShapeDtypeStruct((1, LANES), jnp.int32),
        ],
        scratch_shapes=[pltpu.VMEM((rows, slots), jnp.float32), pltpu.VMEM((rows, slots), jnp.float32)],
        compiler_params=params(16),
        cost_estimate=pl.CostEstimate(flops=10**8, bytes_accessed=10**7, transcendentals=0),
        name="slot_list",
    )(parts)


def attend_kernel(
    scale,
    group,
    kv_local,
    list_ref,
    bound_ref,
    query_ref,
    key_hbm,
    value_hbm,
    out_ref,
    key_ref,
    value_ref,
    top_ref,
    total_ref,
    sum_ref,
    score_ref,
    part_top_ref,
    part_total_ref,
    part_sum_ref,
    sems,
):
    rows, heads, _ = query_ref.shape
    blocks, tokens, _ = key_ref.shape
    block_size = tokens // kv_local
    size = blocks // PHASES
    length_bits = (block_size - 1).bit_length()
    block_bits = (blocks - 1).bit_length()
    copies = []
    for part in range(PHASES):
        here = pl.ds(part * size, size)
        pair = (
            pltpu.make_async_copy(key_hbm.at[here], key_ref.at[here], sems.at[0, part]),
            pltpu.make_async_copy(value_hbm.at[here], value_ref.at[here], sems.at[1, part]),
        )
        for copy in pair:
            copy.start()
        copies.append(pair)

    factor = scale * LOG2E
    top_ref[...] = jnp.full(top_ref.shape, NEG_FILL, jnp.float32)
    for ref in (total_ref, sum_ref, score_ref, part_top_ref, part_total_ref, part_sum_ref):
        ref[...] = jnp.zeros(ref.shape, jnp.float32)
    head = lax.broadcasted_iota(jnp.int32, (heads, tokens), 0) // group
    place = lax.broadcasted_iota(jnp.int32, (heads, tokens), 1)
    token = jnp.where(place % kv_local == head, place // kv_local, block_size)
    nt = (((1,), (1,)), ((), ()))
    wide = (heads, LANES)

    def entries(chunk):
        return [list_ref[0, chunk * UNROLL + j] for j in range(UNROLL)]

    def row_of(entry):
        return entry >> (length_bits + block_bits)

    def block_of(entry):
        return (entry >> length_bits) & (blocks - 1)

    def turn(i, carry):
        before, top, total, acc = carry
        row = [jnp.where(i >= 2, row_of(e), rows) for e in entries(jnp.maximum(i - 2, 0))]
        states = [(top_ref[r], total_ref[r], sum_ref[r]) for r in row]
        for j in range(UNROLL):
            fresh = row[j] != before
            top, total, acc = (jnp.where(fresh, x, y) for x, y in zip(states[j], (top, total, acc)))
            part_top = part_top_ref[j]
            high = jnp.maximum(top, part_top)
            old = jnp.exp2((top - high) * factor)
            new = jnp.exp2((part_top - high) * factor)
            total = total * old + part_total_ref[j] * new
            acc = acc * old + part_sum_ref[j] * new
            top, before = high, row[j]
            top_ref[row[j]] = top
            total_ref[row[j]] = total
            sum_ref[row[j]] = acc

        for j, entry in enumerate(entries(jnp.maximum(i - 1, 0))):
            scores = jnp.where(token <= (entry & (block_size - 1)), score_ref[j], NEG_FILL)
            high = jnp.max(scores, axis=1, keepdims=True)
            weights = jnp.exp2((scores - high) * factor)
            part_top_ref[j] = jnp.broadcast_to(high, wide)
            part_total_ref[j] = jnp.broadcast_to(jnp.sum(weights, axis=1, keepdims=True), wide)
            part_sum_ref[j] = jnp.dot(
                weights.astype(jnp.bfloat16), value_ref[block_of(entry)], preferred_element_type=jnp.float32
            )

        for j, entry in enumerate(entries(i)):
            score_ref[j] = lax.dot_general(
                query_ref[jnp.minimum(row_of(entry), rows - 1)],
                key_ref[block_of(entry)],
                nt,
                preferred_element_type=jnp.float32,
            )
        return before, top, total, acc

    zero = jnp.zeros(wide, jnp.float32)
    carry = (jnp.int32(-1), zero, zero, zero)
    for part in range(PHASES):
        for copy in copies[part]:
            copy.wait()
        carry = lax.fori_loop(bound_ref[0, part], bound_ref[0, part + 1], turn, carry)
    last = bound_ref[0, PHASES]
    lax.fori_loop(last, last + 2, turn, carry)

    count, sections, _, _ = out_ref.shape
    own = sections - 1
    square = (own * heads, LANES)
    eye = lax.broadcasted_iota(jnp.int32, square, 0) == lax.broadcasted_iota(jnp.int32, square, 1)
    line = lax.broadcasted_iota(jnp.int32, wide, 0)
    for c in range(count):
        stats = jnp.zeros(wide, jnp.float32)
        position = 0
        for ref in (top_ref, total_ref):
            flat = jnp.sum(
                jnp.where(eye, ref[c * own : (c + 1) * own].reshape(square), 0.0), axis=0, keepdims=True
            )
            for piece in split3(flat):
                stats = jnp.where(line == position, piece, stats)
                position += 1
        for r in range(own):
            out_ref[c, r] = sum_ref[c * own + r].astype(jnp.bfloat16)
        out_ref[c, own] = stats.astype(jnp.bfloat16)


def attend(items, bounds, queries, keys, values, count, kv_local, scale):
    rows, heads, _ = queries.shape
    own = rows // count
    tokens = keys.shape[1]
    keys, values = in_hbm(keys, values)
    state = pltpu.VMEM((rows + 1, heads, LANES), jnp.float32)
    part = pltpu.VMEM((UNROLL, heads, LANES), jnp.float32)
    hbm = pl.BlockSpec(memory_space=pltpu.HBM)
    return pl.pallas_call(
        functools.partial(attend_kernel, scale, heads // kv_local, kv_local),
        in_specs=[smem_spec(), smem_spec(), vmem_spec(), hbm, hbm],
        out_specs=vmem_spec(),
        out_shape=jax.ShapeDtypeStruct((count, own + 1, heads, LANES), jnp.bfloat16),
        scratch_shapes=[
            pltpu.VMEM(keys.shape, keys.dtype),
            pltpu.VMEM(values.shape, values.dtype),
            state,
            state,
            state,
            pltpu.VMEM((UNROLL, heads, tokens), jnp.float32),
            part,
            part,
            part,
            pltpu.SemaphoreType.DMA((2, PHASES)),
        ],
        compiler_params=params(40),
        name="attend",
    )(items, bounds, queries, keys, values)


def merge_kernel(scale, parts_ref, out_ref, wide_ref):
    count, sections, heads, _ = parts_ref.shape
    own = sections - 1
    factor = scale * LOG2E
    stats = [parts_ref[s, own].astype(jnp.float32) for s in range(count)]
    tops = jnp.concatenate([s[0:1] + s[1:2] + s[2:3] for s in stats], axis=0)
    totals = jnp.concatenate([s[3:4] + s[4:5] + s[5:6] for s in stats], axis=0)
    weights = jnp.exp2((tops - jnp.max(tops, axis=0, keepdims=True)) * factor)
    weights = weights / jnp.sum(weights * totals, axis=0, keepdims=True)
    columns = weights.T
    acc = jnp.zeros((own * heads, LANES), jnp.float32)
    for s in range(count):
        part = parts_ref[s, :own].astype(jnp.float32).reshape(own * heads, LANES)
        acc = acc + part * columns[:, s : s + 1]
    wide_ref[...] = acc
    pieces = [wide_ref[pl.ds(h, own, stride=heads), :] for h in range(heads)]
    out_ref[...] = jnp.concatenate(pieces, axis=1).astype(jnp.bfloat16)


def merge(parts, scale):
    count, sections, heads, _ = parts.shape
    own = sections - 1
    return pl.pallas_call(
        functools.partial(merge_kernel, scale),
        in_specs=[vmem_spec()],
        out_specs=vmem_spec(),
        out_shape=jax.ShapeDtypeStruct((own, heads * LANES), jnp.bfloat16),
        scratch_shapes=[pltpu.VMEM((own * heads, LANES), jnp.float32)],
        compiler_params=params(16),
        name="merge",
    )(parts)


def output_kernel(count, row_count, *refs):
    pieces, weight_ref = refs[:count], refs[count]
    own_ref, sends = refs[count + 1], refs[count + 2 : count + 1 + row_count]
    rows_ref, terms_ref = refs[count + 1 + row_count :]
    own = pieces[0].shape[0]
    me = lax.axis_index("kv")
    for s in range(count):
        start = pl.multiple_of(jnp.bitwise_xor(me, s) * own, own)
        rows_ref[pl.ds(start, own), :] = pieces[s][...].astype(jnp.float32)
    terms_ref[...] = jnp.dot(
        rows_ref[...].astype(jnp.bfloat16), weight_ref[...], preferred_element_type=jnp.float32
    )
    me = lax.axis_index("row")
    part = own_ref.shape[0]
    for s, ref in enumerate((own_ref, *sends)):
        start = pl.multiple_of(jnp.bitwise_xor(me, s) * part, part)
        ref[...] = terms_ref[pl.ds(start, part), :].astype(ref.dtype)


def project_out(pieces, weight, row_count):
    count = len(pieces)
    own, width = pieces[0].shape
    rows, columns = count * own, weight.shape[1]
    part = rows // row_count
    send = jax.ShapeDtypeStruct((part, columns), jnp.bfloat16)
    return pl.pallas_call(
        functools.partial(output_kernel, count, row_count),
        in_specs=[vmem_spec()] * (count + 1),
        out_specs=[vmem_spec()] * row_count,
        out_shape=[jax.ShapeDtypeStruct((part, columns), jnp.float32)] + [send] * (row_count - 1),
        scratch_shapes=[pltpu.VMEM((rows, width), jnp.float32), pltpu.VMEM((rows, columns), jnp.float32)],
        compiler_params=params(24),
        name="project_out",
    )(*pieces, weight)


def swap(x, axis):
    return lax.all_to_all(x, axis, split_axis=0, concat_axis=0, tiled=True)


def exchange(x, axis, s):
    count = lax.axis_size(axis)
    return lax.ppermute(x, axis, [(i, i ^ s) for i in range(count)])


def local(
    hidden,
    query_weight,
    adapter_down_weight,
    adapter_up_weight,
    query_norm_gain,
    paged_key_cache,
    paged_value_cache,
    output_weight,
    holder,
    holder_block_index,
    block_used_length,
    tenant,
    tenant_adapter,
):
    own, slots = holder.shape
    rows, depth = hidden.shape
    kv_count = lax.axis_size("kv")
    row_count = lax.axis_size("row")
    adapters, _, rank = adapter_down_weight.shape
    width = query_weight.shape[1]
    head_size = query_norm_gain.shape[0]
    heads = width // head_size
    blocks, block_size, kv_local, _ = paged_key_cache.shape
    scale = 1.0 / math.sqrt(head_size)

    partial = project(
        tenant.reshape(1, rows),
        tenant_adapter.reshape(1, -1),
        holder,
        holder_block_index,
        block_used_length,
        hidden,
        query_weight,
        jnp.swapaxes(adapter_down_weight, 1, 2).reshape(adapters * rank, depth),
        adapter_up_weight.reshape(adapters * rank, width),
        rank,
    )
    parts = swap(partial.reshape(kv_count, own, width + LANES), "kv")

    position = (jnp.sum(block_used_length, axis=1) - 1).astype(jnp.float32)
    half = head_size // 2
    frequency = ROPE_BASE ** (-(jnp.arange(half, dtype=jnp.float32) * 2.0) / head_size)
    angles = position[:, None] * frequency[None, :]
    cosine = jnp.concatenate([jnp.cos(angles), jnp.cos(angles)], axis=-1)
    sine = jnp.concatenate([-jnp.sin(angles), jnp.sin(angles)], axis=-1)
    queries = make_queries(parts, cosine, sine, query_norm_gain.reshape(1, head_size), heads)
    queries = swap(queries, "kv").reshape(rows, heads, head_size)
    items, bounds = make_list(parts, slots, blocks, block_size)

    keys = paged_key_cache.reshape(blocks, block_size * kv_local, head_size)
    values = paged_value_cache.reshape(blocks, block_size * kv_local, head_size)
    partial_out = attend(items, bounds, queries, keys, values, kv_count, kv_local, scale)
    attention = merge(swap(partial_out, "kv"), scale)
    pieces = [attention] + [exchange(attention, "kv", s) for s in range(1, kv_count)]
    terms = project_out(pieces, output_weight, row_count)
    total = terms[0]
    for s in range(1, row_count):
        total = total + exchange(terms[s], "row", s).astype(jnp.float32)
    return total.astype(jnp.bfloat16)


def solution(mesh):
    return jax.shard_map(
        local,
        mesh=mesh,
        in_specs=(
            P(None, "kv"),
            P("kv", "row"),
            P(None, "kv", None),
            P(None, None, "row"),
            P(),
            P("kv", None, "row", None),
            P("kv", None, "row", None),
            P("row", "kv"),
            P("kv", None),
            P("kv", None),
            P("kv", None),
            P(),
            P(),
        ),
        out_specs=P("row", "kv"),
        check_vma=False,
    )
```

```python
import functools
import math

import jax
import jax.numpy as jnp
from jax import lax
from jax.experimental import pallas as pl
from jax.experimental.pallas import tpu as pltpu
from jax.sharding import PartitionSpec as P

ADAPTER_SCALE = 0.5
ROPE_BASE = 1000000.0
EPSILON = 1e-06
NEG_FILL = -1e30
LANES = 128
COLUMN_TILE = 256
PAIR = 2
TASKS = 8
CHUNK = PAIR * TASKS
PHASES = 8
LOG2E = math.log2(math.e)
MIB = 1024 * 1024


def params(mib):
    return pltpu.CompilerParams(vmem_limit_bytes=mib * MIB)


def vmem_spec():
    return pl.BlockSpec(memory_space=pltpu.VMEM)


def in_hbm(*arrays):
    return [pltpu.with_memory_space_constraint(x, pltpu.HBM) for x in arrays]


def hbm_spec():
    return pl.BlockSpec(memory_space=pltpu.HBM)


def smem_spec():
    return pl.BlockSpec(memory_space=pltpu.SMEM)


def split2(x):
    high = x.astype(jnp.bfloat16)
    return high, (x - high.astype(jnp.float32)).astype(jnp.bfloat16)


def split3(x):
    high = x.astype(jnp.bfloat16).astype(jnp.float32)
    rest = x - high
    middle = rest.astype(jnp.bfloat16).astype(jnp.float32)
    return high, middle, (rest - middle).astype(jnp.bfloat16).astype(jnp.float32)


def to_column(row, count):
    shape = (count, count)
    eye = lax.broadcasted_iota(jnp.int32, shape, 0) == lax.broadcasted_iota(jnp.int32, shape, 1)
    return jnp.sum(jnp.where(eye, row.astype(jnp.float32), 0.0), axis=1, keepdims=True)


def project_kernel(
    rank,
    tenant_ref,
    adapter_ref,
    holder_ref,
    block_ref,
    length_ref,
    hidden_hbm,
    weight_hbm,
    down_hbm,
    up_hbm,
    keep_ref,
    send_ref,
    hidden_ref,
    weight_ref,
    down_ref,
    up_ref,
    sems,
    tile_sems,
):
    chips, own, _ = keep_ref.shape
    rows = hidden_ref.shape[0]
    width = weight_ref.shape[1]
    tiles = width // COLUMN_TILE
    first = [
        pltpu.make_async_copy(hidden_hbm, hidden_ref, sems.at[0]),
        pltpu.make_async_copy(down_hbm, down_ref, sems.at[1]),
    ]
    for copy in first:
        copy.start()
    copies = []
    for i in range(tiles):
        columns = pl.ds(i * COLUMN_TILE, COLUMN_TILE)
        pair = (
            pltpu.make_async_copy(weight_hbm.at[:, columns], weight_ref.at[:, columns], tile_sems.at[0, i]),
            pltpu.make_async_copy(up_hbm.at[:, columns], up_ref.at[:, columns], tile_sems.at[1, i]),
        )
        for copy in pair:
            copy.start()
        copies.append(pair)

    slots = holder_ref.shape[1]
    numbers = [holder_ref[...], block_ref[...], length_ref[...], jnp.zeros((own, LANES - 3 * slots), jnp.int32)]
    numbers = jnp.concatenate(numbers, axis=1).astype(jnp.float32)
    for c in range(chips):
        keep_ref[c, :, width:] = numbers
        send_ref[c, :, width:] = numbers
    tenants = adapter_ref.shape[1]
    tenant = to_column(tenant_ref[...], rows)
    pick = lax.broadcasted_iota(jnp.int32, (rows, tenants), 1).astype(jnp.float32) == tenant
    adapter = jnp.sum(jnp.where(pick, adapter_ref[...].astype(jnp.float32), 0.0), axis=1, keepdims=True).astype(
        jnp.int32
    )
    for copy in first:
        copy.wait()
    hidden = hidden_ref[...]
    low = lax.dot_general(hidden, down_ref[...], (((1,), (1,)), ((), ())), preferred_element_type=jnp.float32)
    column = lax.broadcasted_iota(jnp.int32, low.shape, 1)
    match = (column >= adapter * rank) & (column < adapter * rank + rank)
    high, low = split2(jnp.where(match, ADAPTER_SCALE * low, 0.0))
    even = lax.axis_index("kv") % PAIR == 0
    for i in range(tiles):
        columns = slice(i * COLUMN_TILE, (i + 1) * COLUMN_TILE)
        for copy in copies[i]:
            copy.wait()
        up_high, up_low = split2(up_ref[:, columns])
        total = jnp.dot(hidden, weight_ref[:, columns], preferred_element_type=jnp.float32)
        total += jnp.dot(low, up_high, preferred_element_type=jnp.float32)
        total += jnp.dot(high, up_low, preferred_element_type=jnp.float32)
        total += jnp.dot(high, up_high, preferred_element_type=jnp.float32)
        total = total.reshape(chips, PAIR, own, COLUMN_TILE)
        keep_ref[:, :, columns] = jnp.where(even, total[:, 0], total[:, 1])
        send_ref[:, :, columns] = jnp.where(even, total[:, 1], total[:, 0])


def project(tenant, tenant_adapter, holder, block, length, hidden, query_weight, down, up, rank, chips):
    rows, _ = hidden.shape
    width = query_weight.shape[1]
    out = jax.ShapeDtypeStruct((chips, rows // chips // PAIR, width + LANES), jnp.float32)
    operands = in_hbm(tenant, tenant_adapter, holder, block, length, hidden, query_weight, down, up)
    large = operands[5:]
    return pl.pallas_call(
        functools.partial(project_kernel, rank),
        in_specs=[vmem_spec()] * 5 + [hbm_spec()] * 4,
        out_specs=[vmem_spec()] * 2,
        out_shape=[out] * 2,
        scratch_shapes=[pltpu.VMEM(x.shape, x.dtype) for x in large]
        + [pltpu.SemaphoreType.DMA((2,)), pltpu.SemaphoreType.DMA((2, width // COLUMN_TILE))],
        compiler_params=params(24),
        name="project",
    )(*operands)


def pair_kernel(keep_ref, got_ref, *out_refs):
    width = keep_ref.shape[2] - LANES
    chip = lax.axis_index("kv") // PAIR
    for s, ref in enumerate(out_refs):
        c = jnp.bitwise_xor(chip, s)
        ref[:, :width] = keep_ref[c, :, :width] + got_ref[c, :, :width]
        ref[:, width : width + LANES] = keep_ref[0, :, width:]
        ref[:, width + LANES :] = got_ref[0, :, width:]


def add_pair(keep, got):
    chips, own, width = keep.shape
    return pl.pallas_call(
        pair_kernel,
        in_specs=[vmem_spec()] * 2,
        out_specs=[vmem_spec()] * chips,
        out_shape=[jax.ShapeDtypeStruct((own, width + LANES), jnp.float32)] * chips,
        compiler_params=params(16),
        name="add_pair",
    )(keep, got)


def queries_kernel(*refs):
    parts, (cosine_ref, sine_ref, gain_ref, out_ref, turned_ref) = refs[:-5], refs[-5:]
    heads = turned_ref.shape[1]
    cosine, sine, gain = cosine_ref[...], sine_ref[...], gain_ref[...]
    for h in range(heads):
        columns = slice(h * LANES, (h + 1) * LANES)
        query = parts[0][:, columns]
        for part in parts[1:]:
            query = query + part[:, columns]
        square = jnp.mean(query * query, axis=-1, keepdims=True)
        query = query * lax.rsqrt(square + EPSILON) * gain
        turned_ref[:, h, :] = query * cosine + pltpu.roll(query, LANES // 2, 1) * sine
    out_ref[...] = turned_ref[...].astype(jnp.bfloat16)


def make_queries(parts, cosine, sine, gain, heads):
    own = parts[0].shape[0]
    shape = (own, heads, LANES)
    return pl.pallas_call(
        queries_kernel,
        in_specs=[vmem_spec()] * (len(parts) + 3),
        out_specs=vmem_spec(),
        out_shape=jax.ShapeDtypeStruct(shape, jnp.bfloat16),
        scratch_shapes=[pltpu.VMEM(shape, jnp.float32)],
        compiler_params=params(16),
        name="queries",
    )(*parts, cosine, sine, gain)


def list_kernel(blocks, block_size, slots, *refs):
    pieces, (list_ref, bound_ref, place_ref, value_ref) = refs[:-4], refs[-4:]
    rows = place_ref.shape[0]
    capacity = list_ref.shape[1]
    me = lax.axis_index("kv").astype(jnp.float32)
    numbers = jnp.concatenate([p[:, i * LANES : (i + 1) * LANES] for p in pieces for i in range(PAIR)], axis=0)
    holder, block, length = (numbers[:, i * slots : (i + 1) * slots] for i in range(3))
    row = lax.broadcasted_iota(jnp.int32, (rows, slots), 0).astype(jnp.float32)
    spare = float(rows * blocks * block_size)
    value_ref[...] = (row * blocks + block) * block_size + (length - 1.0) - spare
    mine = holder == me
    key = jnp.where(mine, block, -1.0)

    def before(count, axis):
        first = lax.broadcasted_iota(jnp.int32, (count, count), axis)
        return jnp.where(first < lax.broadcasted_iota(jnp.int32, (count, count), 1 - axis), 1.0, 0.0).astype(
            jnp.bfloat16
        )

    lane = lax.broadcasted_iota(jnp.int32, (rows, blocks), 1).astype(jnp.float32)
    picks = [jnp.where(key[:, j : j + 1] == lane, 1.0, 0.0) for j in range(slots)]
    count = jnp.sum(functools.reduce(jnp.add, picks), axis=0, keepdims=True)
    tasks = jnp.floor((count + (PAIR - 1)) * (1.0 / PAIR))
    earlier = jnp.dot(
        jnp.broadcast_to(tasks, (8, blocks)).astype(jnp.bfloat16),
        before(blocks, 0),
        preferred_element_type=jnp.float32,
    )[:1]
    base = earlier * PAIR
    row_before = before(rows, 1)
    slot = lax.broadcasted_iota(jnp.int32, (rows, slots), 1)
    place = jnp.full((rows, slots), -1.0, jnp.float32)
    for j in range(slots):
        above = jnp.dot(row_before, picks[j].astype(jnp.bfloat16), preferred_element_type=jnp.float32)
        here = jnp.sum(picks[j] * (above + base), axis=1, keepdims=True)
        place = jnp.where((slot == j) & mine, here, place)
        base = base + jnp.sum(picks[j], axis=0, keepdims=True)
    place_ref[...] = place
    size = blocks // PHASES
    end = earlier + tasks
    block_lane = lax.broadcasted_iota(jnp.int32, (1, blocks), 1)
    bound_lane = lax.broadcasted_iota(jnp.int32, (1, LANES), 1)
    bounds = jnp.zeros((1, LANES), jnp.float32)
    for part in range(PHASES):
        done = jnp.sum(jnp.where(block_lane == (part + 1) * size - 1, end, 0.0), axis=1, keepdims=True)
        done = done * (1.0 / TASKS)
        done = jnp.ceil(done) if part == PHASES - 1 else jnp.floor(done)
        bounds = jnp.where(bound_lane == part + 1, done, bounds)
    bound_ref[...] = bounds.astype(jnp.int32)
    target = lax.broadcasted_iota(jnp.int32, (8, capacity), 1).astype(jnp.float32)

    def tile(t, total):
        here = pl.ds(pl.multiple_of(t * 8, 8), 8)
        places, values = place_ref[here, :], value_ref[here, :]
        for j in range(slots):
            total = total + jnp.where(places[:, j : j + 1] == target, values[:, j : j + 1], 0.0)
        return total

    total = lax.fori_loop(0, rows // 8, tile, jnp.zeros((8, capacity), jnp.float32))
    list_ref[...] = (jnp.sum(total, axis=0, keepdims=True) + spare).astype(jnp.int32)


def make_list(parts, slots, blocks, block_size, count):
    own, width = parts[0].shape
    rows = count * own
    most = 2 * own * slots // count * count + (PAIR - 1) * blocks + 3 * CHUNK
    capacity = -(-most // LANES) * LANES
    last = width // (PAIR * LANES) - 1
    return pl.pallas_call(
        functools.partial(list_kernel, blocks, block_size, slots),
        grid=(1,),
        in_specs=[pl.BlockSpec((own, PAIR * LANES), lambda i: (0, last))] * len(parts),
        out_specs=[
            pl.BlockSpec((1, capacity), lambda i: (0, 0)),
            pl.BlockSpec((1, LANES), lambda i: (0, 0)),
        ],
        out_shape=[
            jax.ShapeDtypeStruct((1, capacity), jnp.int32),
            jax.ShapeDtypeStruct((1, LANES), jnp.int32),
        ],
        scratch_shapes=[pltpu.VMEM((rows, slots), jnp.float32), pltpu.VMEM((rows, slots), jnp.float32)],
        compiler_params=params(16),
        cost_estimate=pl.CostEstimate(flops=10**8, bytes_accessed=10**7, transcendentals=0),
        name="slot_list",
    )(*parts)


def attend_kernel(scale, group, kv_local, count, list_ref, bound_ref, *refs):
    queries, refs = refs[: count // PAIR], refs[count // PAIR :]
    (key_hbm, value_hbm, out_ref, query_ref, key_ref, value_ref, top_ref, total_ref, sum_ref) = refs[:9]
    (score_ref, part_top_ref, part_total_ref, part_sum_ref, sems) = refs[9:]
    heads = query_ref.shape[1]
    rows = query_ref.shape[0] - 1
    own = rows // count
    blocks, tokens, _ = key_ref.shape
    block_size = tokens // kv_local
    size = blocks // PHASES
    length_bits = (block_size - 1).bit_length()
    block_bits = (blocks - 1).bit_length()
    copies = []
    for part in range(PHASES):
        here = pl.ds(part * size, size)
        pair = (
            pltpu.make_async_copy(key_hbm.at[here], key_ref.at[here], sems.at[0, part]),
            pltpu.make_async_copy(value_hbm.at[here], value_ref.at[here], sems.at[1, part]),
        )
        for copy in pair:
            copy.start()
        copies.append(pair)

    factor = scale * LOG2E
    for s, piece in enumerate(queries):
        for t in range(PAIR):
            start = (PAIR * s + t) * own
            query_ref[start : start + own] = piece[t]
    query_ref[rows] = jnp.zeros((heads, LANES), jnp.bfloat16)
    top_ref[...] = jnp.full(top_ref.shape, NEG_FILL, jnp.float32)
    for ref in (total_ref, sum_ref, score_ref, part_top_ref, part_total_ref, part_sum_ref):
        ref[...] = jnp.zeros(ref.shape, jnp.float32)
    head = lax.broadcasted_iota(jnp.int32, (heads, tokens), 0) // group
    place = lax.broadcasted_iota(jnp.int32, (heads, tokens), 1)
    token = jnp.where(place % kv_local == head, place // kv_local, block_size)
    wide = (heads, LANES)

    def entries(chunk):
        return [list_ref[0, chunk * CHUNK + j] for j in range(CHUNK)]

    def row_of(entry):
        return entry >> (length_bits + block_bits)

    def block_of(entry):
        return (entry >> length_bits) & (blocks - 1)

    def turn(i, carry):
        row = [jnp.where(i >= 2, row_of(e), rows) for e in entries(jnp.maximum(i - 2, 0))]
        shares = []
        for j in range(CHUNK):
            top, part_top = top_ref[row[j]], part_top_ref[j]
            high = jnp.maximum(top, part_top)
            top_ref[row[j]] = high
            shares.append((jnp.exp2((top - high) * factor), jnp.exp2((part_top - high) * factor)))
        for j, (old, new) in enumerate(shares):
            t, k = divmod(j, PAIR)
            total_ref[row[j]] = total_ref[row[j]] * old + part_total_ref[j] * new
            sum_ref[row[j]] = sum_ref[row[j]] * old + part_sum_ref[t, k * heads : (k + 1) * heads] * new

        items = entries(jnp.maximum(i - 1, 0))
        for t in range(TASKS):
            pieces = []
            for k in range(PAIR):
                j = t * PAIR + k
                length = items[j] & (block_size - 1)
                scores = jnp.where(token <= length, score_ref[t, k * heads : (k + 1) * heads], NEG_FILL)
                high = jnp.max(scores, axis=1, keepdims=True)
                weights = jnp.exp2((scores - high) * factor)
                part_top_ref[j] = jnp.broadcast_to(high, wide)
                part_total_ref[j] = jnp.broadcast_to(jnp.sum(weights, axis=1, keepdims=True), wide)
                pieces.append(weights.astype(jnp.bfloat16))
            part_sum_ref[t] = jnp.dot(
                jnp.concatenate(pieces, axis=0),
                value_ref[block_of(items[t * PAIR])],
                preferred_element_type=jnp.float32,
            )

        items = entries(i)
        for t in range(TASKS):
            task = items[t * PAIR : (t + 1) * PAIR]
            score_ref[t] = lax.dot_general(
                jnp.concatenate([query_ref[row_of(e)] for e in task], axis=0),
                key_ref[block_of(task[0])],
                (((1,), (1,)), ((), ())),
                preferred_element_type=jnp.float32,
            )
        return carry

    for part in range(PHASES):
        for copy in copies[part]:
            copy.wait()
        lax.fori_loop(bound_ref[0, part], bound_ref[0, part + 1], turn, 0)
    last = bound_ref[0, PHASES]
    lax.fori_loop(last, last + 2, turn, 0)

    me = lax.axis_index("kv")
    square = (own * heads, LANES)
    eye = lax.broadcasted_iota(jnp.int32, square, 0) == lax.broadcasted_iota(jnp.int32, square, 1)
    line = lax.broadcasted_iota(jnp.int32, wide, 0)
    for c in range(count):
        stats = jnp.zeros(wide, jnp.float32)
        position = 0
        for ref in (top_ref, total_ref):
            flat = jnp.sum(
                jnp.where(eye, ref[c * own : (c + 1) * own].reshape(square), 0.0), axis=0, keepdims=True
            )
            for piece in split3(flat):
                stats = jnp.where(line == position, piece, stats)
                position += 1
        owner = jnp.bitwise_xor(me, c)
        for r in range(own):
            out_ref[owner, r] = sum_ref[c * own + r].astype(jnp.bfloat16)
        out_ref[owner, own] = stats.astype(jnp.bfloat16)


def attend(items, bounds, queries, keys, values, kv_local, scale):
    _, own, heads, _ = queries[0].shape
    count = len(queries) * PAIR
    rows = count * own
    tokens = keys.shape[1]
    keys, values = in_hbm(keys, values)
    state = pltpu.VMEM((rows + 1, heads, LANES), jnp.float32)
    part = pltpu.VMEM((CHUNK, heads, LANES), jnp.float32)
    return pl.pallas_call(
        functools.partial(attend_kernel, scale, heads // kv_local, kv_local, count),
        in_specs=[smem_spec(), smem_spec()] + [vmem_spec()] * len(queries) + [hbm_spec()] * 2,
        out_specs=vmem_spec(),
        out_shape=jax.ShapeDtypeStruct((count, own + 1, heads, LANES), jnp.bfloat16),
        scratch_shapes=[
            pltpu.VMEM((rows + 1, heads, LANES), jnp.bfloat16),
            pltpu.VMEM(keys.shape, keys.dtype),
            pltpu.VMEM(values.shape, values.dtype),
            state,
            state,
            state,
            pltpu.VMEM((TASKS, PAIR * heads, tokens), jnp.float32),
            part,
            part,
            pltpu.VMEM((TASKS, PAIR * heads, LANES), jnp.float32),
            pltpu.SemaphoreType.DMA((2, PHASES)),
        ],
        compiler_params=params(40),
        name="attend",
    )(items, bounds, *queries, keys, values)


def merge_kernel(scale, parts_ref, out_ref, wide_ref):
    count, sections, heads, _ = parts_ref.shape
    own = sections - 1
    factor = scale * LOG2E
    stats = [parts_ref[s, own].astype(jnp.float32) for s in range(count)]
    tops = jnp.concatenate([s[0:1] + s[1:2] + s[2:3] for s in stats], axis=0)
    totals = jnp.concatenate([s[3:4] + s[4:5] + s[5:6] for s in stats], axis=0)
    weights = jnp.exp2((tops - jnp.max(tops, axis=0, keepdims=True)) * factor)
    weights = weights / jnp.sum(weights * totals, axis=0, keepdims=True)
    columns = weights.T
    acc = jnp.zeros((own * heads, LANES), jnp.float32)
    for s in range(count):
        part = parts_ref[s, :own].astype(jnp.float32).reshape(own * heads, LANES)
        acc = acc + part * columns[:, s : s + 1]
    wide_ref[...] = acc
    pieces = [wide_ref[pl.ds(h, own, stride=heads), :] for h in range(heads)]
    out_ref[...] = jnp.concatenate(pieces, axis=1).astype(jnp.bfloat16)


def merge(parts, scale):
    count, sections, heads, _ = parts.shape
    own = sections - 1
    return pl.pallas_call(
        functools.partial(merge_kernel, scale),
        in_specs=[vmem_spec()],
        out_specs=vmem_spec(),
        out_shape=jax.ShapeDtypeStruct((own, heads * LANES), jnp.bfloat16),
        scratch_shapes=[pltpu.VMEM((own * heads, LANES), jnp.float32)],
        compiler_params=params(16),
        name="merge",
    )(parts)


def output_kernel(chips, row_count, *refs):
    pieces, weight_ref = refs[:chips], refs[chips]
    own_ref, sends = refs[chips + 1], refs[chips + 2 : chips + 1 + row_count]
    rows_ref, terms_ref = refs[chips + 1 + row_count :]
    own = pieces[0].shape[0] // PAIR
    me = lax.axis_index("kv")
    for s in range(chips):
        piece = pieces[s][...].astype(jnp.float32)
        for t in range(PAIR):
            start = pl.multiple_of(jnp.bitwise_xor(me, PAIR * s + t) * own, own)
            rows_ref[pl.ds(start, own), :] = piece[t * own : (t + 1) * own]
    terms_ref[...] = jnp.dot(
        rows_ref[...].astype(jnp.bfloat16), weight_ref[...], preferred_element_type=jnp.float32
    )
    me = lax.axis_index("row")
    part = own_ref.shape[0]
    for s, ref in enumerate((own_ref, *sends)):
        start = pl.multiple_of(jnp.bitwise_xor(me, s) * part, part)
        ref[...] = terms_ref[pl.ds(start, part), :].astype(ref.dtype)


def project_out(pieces, weight, row_count):
    chips = len(pieces)
    pair_rows, width = pieces[0].shape
    rows, columns = chips * pair_rows, weight.shape[1]
    part = rows // row_count
    send = jax.ShapeDtypeStruct((part, columns), jnp.bfloat16)
    return pl.pallas_call(
        functools.partial(output_kernel, chips, row_count),
        in_specs=[vmem_spec()] * (chips + 1),
        out_specs=[vmem_spec()] * row_count,
        out_shape=[jax.ShapeDtypeStruct((part, columns), jnp.float32)] + [send] * (row_count - 1),
        scratch_shapes=[pltpu.VMEM((rows, width), jnp.float32), pltpu.VMEM((rows, columns), jnp.float32)],
        compiler_params=params(24),
        name="project_out",
    )(*pieces, weight)


def swap(x, axis):
    return lax.all_to_all(x, axis, split_axis=0, concat_axis=0, tiled=True)


def exchange(x, axis, s):
    count = lax.axis_size(axis)
    return lax.ppermute(x, axis, [(i, i ^ s) for i in range(count)])


def gather_pairs(x):
    pair = jnp.concatenate([x, exchange(x, "kv", 1)], axis=0)
    return [pair] + [exchange(pair, "kv", s) for s in range(PAIR, lax.axis_size("kv"), PAIR)]


def local(
    hidden,
    query_weight,
    adapter_down_weight,
    adapter_up_weight,
    query_norm_gain,
    paged_key_cache,
    paged_value_cache,
    output_weight,
    holder,
    holder_block_index,
    block_used_length,
    tenant,
    tenant_adapter,
):
    own, slots = holder.shape
    rows, depth = hidden.shape
    kv_count = lax.axis_size("kv")
    row_count = lax.axis_size("row")
    adapters, _, rank = adapter_down_weight.shape
    width = query_weight.shape[1]
    head_size = query_norm_gain.shape[0]
    heads = width // head_size
    blocks, block_size, kv_local, _ = paged_key_cache.shape
    scale = 1.0 / math.sqrt(head_size)

    chips = kv_count // PAIR
    keep, send = project(
        tenant.reshape(1, rows),
        tenant_adapter.reshape(1, -1),
        holder,
        holder_block_index,
        block_used_length,
        hidden,
        query_weight,
        jnp.swapaxes(adapter_down_weight, 1, 2).reshape(adapters * rank, depth),
        adapter_up_weight.reshape(adapters * rank, width),
        rank,
        chips,
    )
    parts = add_pair(keep, exchange(send, "kv", 1))
    parts = [parts[0]] + [exchange(parts[s], "kv", PAIR * s) for s in range(1, chips)]

    position = (jnp.sum(block_used_length, axis=1) - 1).astype(jnp.float32)
    half = head_size // 2
    frequency = ROPE_BASE ** (-(jnp.arange(half, dtype=jnp.float32) * 2.0) / head_size)
    angles = position[:, None] * frequency[None, :]
    cosine = jnp.concatenate([jnp.cos(angles), jnp.cos(angles)], axis=-1)
    sine = jnp.concatenate([-jnp.sin(angles), jnp.sin(angles)], axis=-1)
    queries = make_queries(parts, cosine, sine, query_norm_gain.reshape(1, head_size), heads)
    queries = [q.reshape(PAIR, own, heads, head_size) for q in gather_pairs(queries)]
    items, bounds = make_list(parts, slots, blocks, block_size, kv_count)

    keys = paged_key_cache.reshape(blocks, block_size * kv_local, head_size)
    values = paged_value_cache.reshape(blocks, block_size * kv_local, head_size)
    partial_out = attend(items, bounds, queries, keys, values, kv_local, scale)
    attention = merge(swap(partial_out, "kv"), scale)
    terms = project_out(gather_pairs(attention), output_weight, row_count)
    total = terms[0]
    for s in range(1, row_count):
        total = total + exchange(terms[s], "row", s).astype(jnp.float32)
    return total.astype(jnp.bfloat16)


def solution(mesh):
    return jax.shard_map(
        local,
        mesh=mesh,
        in_specs=(
            P(None, "kv"),
            P("kv", "row"),
            P(None, "kv", None),
            P(None, None, "row"),
            P(),
            P("kv", None, "row", None),
            P("kv", None, "row", None),
            P("row", "kv"),
            P("kv", None),
            P("kv", None),
            P("kv", None),
            P(),
            P(),
        ),
        out_specs=P("row", "kv"),
        check_vma=False,
    )
```

```python
import functools
import math

import jax
import jax.numpy as jnp
from jax import lax
from jax.experimental import pallas as pl
from jax.experimental.pallas import tpu as pltpu
from jax.sharding import PartitionSpec as P

ADAPTER_SCALE = 0.5
ROPE_BASE = 1000000.0
EPSILON = 1e-06
NEG_FILL = -1e30
LANES = 128
COLUMN_TILE = 256
PAIR = 2
TASKS = 16
CHUNK = PAIR * TASKS
PHASES = 8
AHEAD = 3
DEPTH = 256
LOG2E = math.log2(math.e)
MIB = 1024 * 1024


def params(mib):
    return pltpu.CompilerParams(vmem_limit_bytes=mib * MIB)


def vmem_spec():
    return pl.BlockSpec(memory_space=pltpu.VMEM)


def in_hbm(*arrays):
    return [pltpu.with_memory_space_constraint(x, pltpu.HBM) for x in arrays]


def hbm_spec():
    return pl.BlockSpec(memory_space=pltpu.HBM)


def smem_spec():
    return pl.BlockSpec(memory_space=pltpu.SMEM)


def split2(x):
    high = x.astype(jnp.bfloat16)
    return high, (x - high.astype(jnp.float32)).astype(jnp.bfloat16)


def split3(x):
    high = x.astype(jnp.bfloat16).astype(jnp.float32)
    rest = x - high
    middle = rest.astype(jnp.bfloat16).astype(jnp.float32)
    return high, middle, (rest - middle).astype(jnp.bfloat16).astype(jnp.float32)


def to_column(row, count):
    shape = (count, count)
    eye = lax.broadcasted_iota(jnp.int32, shape, 0) == lax.broadcasted_iota(jnp.int32, shape, 1)
    return jnp.sum(jnp.where(eye, row.astype(jnp.float32), 0.0), axis=1, keepdims=True)


def project_kernel(
    rank,
    tenant_ref,
    adapter_ref,
    holder_ref,
    block_ref,
    length_ref,
    hidden_hbm,
    weight_hbm,
    down_hbm,
    up_hbm,
    keep_ref,
    send_ref,
    hidden_ref,
    weight_ref,
    down_ref,
    up_ref,
    total_ref,
    sems,
):
    chips, own, _ = keep_ref.shape
    rows, depth = hidden_ref.shape
    low_width = down_ref.shape[0]
    width = weight_ref.shape[1]
    tiles = width // COLUMN_TILE

    def start(copies):
        for copy in copies:
            copy.start()
        return copies

    def chunks(hbm, ref, offset):
        spans = [slice(i, min(i + DEPTH, ref.shape[0])) for i in range(0, ref.shape[0], DEPTH)]
        return [
            (span, pltpu.make_async_copy(hbm.at[span], ref.at[span], sems.at[offset + i]))
            for i, span in enumerate(spans)
        ]

    first = start(
        [
            pltpu.make_async_copy(hidden_hbm, hidden_ref, sems.at[0]),
            pltpu.make_async_copy(down_hbm, down_ref, sems.at[1]),
        ]
    )
    up_chunks = chunks(up_hbm, up_ref, 2)
    weight_chunks = chunks(weight_hbm, weight_ref, 2 + len(up_chunks))
    waiting = [copy for _, copy in up_chunks + weight_chunks]
    start(waiting[:1])

    slots = holder_ref.shape[1]
    numbers = [holder_ref[...], block_ref[...], length_ref[...], jnp.zeros((own, LANES - 3 * slots), jnp.int32)]
    numbers = jnp.concatenate(numbers, axis=1).astype(jnp.float32)
    for c in range(chips):
        keep_ref[c, :, width:] = numbers
        send_ref[c, :, width:] = numbers
    tenants = adapter_ref.shape[1]
    tenant = to_column(tenant_ref[...], rows)
    pick = lax.broadcasted_iota(jnp.int32, (rows, tenants), 1).astype(jnp.float32) == tenant
    adapter = jnp.sum(jnp.where(pick, adapter_ref[...].astype(jnp.float32), 0.0), axis=1, keepdims=True).astype(
        jnp.int32
    )
    for copy in first:
        copy.wait()
    start(waiting[1:3])
    hidden = hidden_ref[...]
    low = lax.dot_general(hidden, down_ref[...], (((1,), (1,)), ((), ())), preferred_element_type=jnp.float32)
    column = lax.broadcasted_iota(jnp.int32, (rows, low_width), 1)
    match = (column >= adapter * rank) & (column < adapter * rank + rank)
    high, low = split2(jnp.where(match, ADAPTER_SCALE * low, 0.0))
    both = jnp.concatenate([high, low], axis=0)
    columns = [slice(i * COLUMN_TILE, (i + 1) * COLUMN_TILE) for i in range(tiles)]
    for i, (span, copy) in enumerate(up_chunks):
        copy.wait()
        start(waiting[i + 3 : i + 4])
        for tile in columns:
            up_high, up_low = split2(up_ref[span, tile])
            twice = jnp.dot(both[:, span], up_high, preferred_element_type=jnp.float32)
            total = jnp.dot(high[:, span], up_low, preferred_element_type=jnp.float32)
            total = (total + twice[rows:]) + twice[:rows]
            total_ref[:, tile] = total if i == 0 else total_ref[:, tile] + total
    even = lax.axis_index("kv") % PAIR == 0
    for i, (span, copy) in enumerate(weight_chunks):
        copy.wait()
        start(waiting[i + len(up_chunks) + 3 : i + len(up_chunks) + 4])
        for tile in columns:
            total = total_ref[:, tile] + jnp.dot(
                hidden[:, span], weight_ref[span, tile], preferred_element_type=jnp.float32
            )
            if i < len(weight_chunks) - 1:
                total_ref[:, tile] = total
            else:
                total = total.reshape(chips, PAIR, own, COLUMN_TILE)
                keep_ref[:, :, tile] = jnp.where(even, total[:, 0], total[:, 1])
                send_ref[:, :, tile] = jnp.where(even, total[:, 1], total[:, 0])


def project(tenant, tenant_adapter, holder, block, length, hidden, query_weight, down, up, rank, chips):
    rows, depth = hidden.shape
    width = query_weight.shape[1]
    out = jax.ShapeDtypeStruct((chips, rows // chips // PAIR, width + LANES), jnp.float32)
    operands = in_hbm(tenant, tenant_adapter, holder, block, length, hidden, query_weight, down, up)
    large = operands[5:]
    return pl.pallas_call(
        functools.partial(project_kernel, rank),
        in_specs=[vmem_spec()] * 5 + [hbm_spec()] * 4,
        out_specs=[vmem_spec()] * 2,
        out_shape=[out] * 2,
        scratch_shapes=[pltpu.VMEM(x.shape, x.dtype) for x in large]
        + [
            pltpu.VMEM((rows, width), jnp.float32),
            pltpu.SemaphoreType.DMA((2 + pl.cdiv(depth, DEPTH) + pl.cdiv(down.shape[0], DEPTH),)),
        ],
        compiler_params=params(24),
        name="project",
    )(*operands)


def pair_kernel(keep_ref, got_ref, *out_refs):
    width = keep_ref.shape[2] - LANES
    chip = lax.axis_index("kv") // PAIR
    for s, ref in enumerate(out_refs):
        c = jnp.bitwise_xor(chip, s)
        ref[:, :width] = keep_ref[c, :, :width] + got_ref[c, :, :width]
        ref[:, width : width + LANES] = keep_ref[0, :, width:]
        ref[:, width + LANES :] = got_ref[0, :, width:]


def add_pair(keep, got):
    chips, own, width = keep.shape
    return pl.pallas_call(
        pair_kernel,
        in_specs=[vmem_spec()] * 2,
        out_specs=[vmem_spec()] * chips,
        out_shape=[jax.ShapeDtypeStruct((own, width + LANES), jnp.float32)] * chips,
        compiler_params=params(16),
        name="add_pair",
    )(keep, got)


def queries_kernel(*refs):
    parts, (cosine_ref, sine_ref, gain_ref, out_ref, turned_ref) = refs[:-5], refs[-5:]
    heads = turned_ref.shape[1]
    cosine, sine, gain = cosine_ref[...], sine_ref[...], gain_ref[...]
    for h in range(heads):
        columns = slice(h * LANES, (h + 1) * LANES)
        query = parts[0][:, columns]
        for part in parts[1:]:
            query = query + part[:, columns]
        square = jnp.mean(query * query, axis=-1, keepdims=True)
        query = query * lax.rsqrt(square + EPSILON) * gain
        turned_ref[:, h, :] = query * cosine + pltpu.roll(query, LANES // 2, 1) * sine
    out_ref[...] = turned_ref[...].astype(jnp.bfloat16)


def make_queries(parts, cosine, sine, gain, heads):
    own = parts[0].shape[0]
    shape = (own, heads, LANES)
    return pl.pallas_call(
        queries_kernel,
        in_specs=[vmem_spec()] * (len(parts) + 3),
        out_specs=vmem_spec(),
        out_shape=jax.ShapeDtypeStruct(shape, jnp.bfloat16),
        scratch_shapes=[pltpu.VMEM(shape, jnp.float32)],
        compiler_params=params(16),
        name="queries",
    )(*parts, cosine, sine, gain)


def list_kernel(blocks, block_size, slots, *refs):
    pieces, (list_ref, bound_ref, place_ref, value_ref) = refs[:-4], refs[-4:]
    rows = place_ref.shape[0]
    capacity = list_ref.shape[1]
    me = lax.axis_index("kv").astype(jnp.float32)
    numbers = jnp.concatenate([p[:, i * LANES : (i + 1) * LANES] for p in pieces for i in range(PAIR)], axis=0)
    holder, block, length = (numbers[:, i * slots : (i + 1) * slots] for i in range(3))
    row = lax.broadcasted_iota(jnp.int32, (rows, slots), 0).astype(jnp.float32)
    spare = float(rows * blocks * block_size)
    value_ref[...] = (row * blocks + block) * block_size + (length - 1.0) - spare
    mine = holder == me
    key = jnp.where(mine, block, -1.0)

    def before(count, axis):
        first = lax.broadcasted_iota(jnp.int32, (count, count), axis)
        return jnp.where(first < lax.broadcasted_iota(jnp.int32, (count, count), 1 - axis), 1.0, 0.0).astype(
            jnp.bfloat16
        )

    lane = lax.broadcasted_iota(jnp.int32, (rows, blocks), 1).astype(jnp.float32)
    picks = [jnp.where(key[:, j : j + 1] == lane, 1.0, 0.0) for j in range(slots)]
    count = jnp.sum(functools.reduce(jnp.add, picks), axis=0, keepdims=True)
    tasks = jnp.floor((count + (PAIR - 1)) * (1.0 / PAIR))
    earlier = jnp.dot(
        jnp.broadcast_to(tasks, (8, blocks)).astype(jnp.bfloat16),
        before(blocks, 0),
        preferred_element_type=jnp.float32,
    )[:1]
    base = earlier * PAIR
    row_before = before(rows, 1)
    slot = lax.broadcasted_iota(jnp.int32, (rows, slots), 1)
    place = jnp.full((rows, slots), -1.0, jnp.float32)
    for j in range(slots):
        above = jnp.dot(row_before, picks[j].astype(jnp.bfloat16), preferred_element_type=jnp.float32)
        here = jnp.sum(picks[j] * (above + base), axis=1, keepdims=True)
        place = jnp.where((slot == j) & mine, here, place)
        base = base + jnp.sum(picks[j], axis=0, keepdims=True)
    place_ref[...] = place
    size = blocks // PHASES
    end = earlier + tasks
    block_lane = lax.broadcasted_iota(jnp.int32, (1, blocks), 1)
    bound_lane = lax.broadcasted_iota(jnp.int32, (1, LANES), 1)
    bounds = jnp.zeros((1, LANES), jnp.float32)
    for part in range(PHASES):
        done = jnp.sum(jnp.where(block_lane == (part + 1) * size - 1, end, 0.0), axis=1, keepdims=True)
        done = done * (1.0 / TASKS)
        done = jnp.ceil(done) if part == PHASES - 1 else jnp.floor(done)
        bounds = jnp.where(bound_lane == part + 1, done, bounds)
    bound_ref[...] = bounds.astype(jnp.int32)
    target = lax.broadcasted_iota(jnp.int32, (8, capacity), 1).astype(jnp.float32)

    def tile(t, total):
        here = pl.ds(pl.multiple_of(t * 8, 8), 8)
        places, values = place_ref[here, :], value_ref[here, :]
        for j in range(slots):
            total = total + jnp.where(places[:, j : j + 1] == target, values[:, j : j + 1], 0.0)
        return total

    total = lax.fori_loop(0, rows // 8, tile, jnp.zeros((8, capacity), jnp.float32))
    list_ref[...] = (jnp.sum(total, axis=0, keepdims=True) + spare).astype(jnp.int32)


def make_list(parts, slots, blocks, block_size, count):
    own, width = parts[0].shape
    rows = count * own
    most = 2 * own * slots // count * count + (PAIR - 1) * blocks + 3 * CHUNK
    capacity = -(-most // LANES) * LANES
    last = width // (PAIR * LANES) - 1
    return pl.pallas_call(
        functools.partial(list_kernel, blocks, block_size, slots),
        grid=(1,),
        in_specs=[pl.BlockSpec((own, PAIR * LANES), lambda i: (0, last))] * len(parts),
        out_specs=[
            pl.BlockSpec((1, capacity), lambda i: (0, 0)),
            pl.BlockSpec((1, LANES), lambda i: (0, 0)),
        ],
        out_shape=[
            jax.ShapeDtypeStruct((1, capacity), jnp.int32),
            jax.ShapeDtypeStruct((1, LANES), jnp.int32),
        ],
        scratch_shapes=[pltpu.VMEM((rows, slots), jnp.float32), pltpu.VMEM((rows, slots), jnp.float32)],
        compiler_params=params(16),
        cost_estimate=pl.CostEstimate(flops=10**8, bytes_accessed=10**7, transcendentals=0),
        name="slot_list",
    )(*parts)


def attend_kernel(scale, group, kv_local, count, list_ref, bound_ref, *refs):
    queries, refs = refs[: count // PAIR], refs[count // PAIR :]
    (key_hbm, value_hbm, keep_ref, send_ref, query_ref, key_ref, value_ref, top_ref, total_ref, sum_ref) = refs[:10]
    (score_ref, part_top_ref, part_total_ref, part_sum_ref, sems) = refs[10:]
    heads = query_ref.shape[1]
    rows = query_ref.shape[0] - 1
    own = rows // count
    blocks, tokens, _ = key_ref.shape
    block_size = tokens // kv_local
    size = blocks // PHASES
    length_bits = (block_size - 1).bit_length()
    block_bits = (blocks - 1).bit_length()
    copies = []
    for part in range(PHASES):
        here = pl.ds(part * size, size)
        copies.append(
            (
                pltpu.make_async_copy(key_hbm.at[here], key_ref.at[here], sems.at[0, part]),
                pltpu.make_async_copy(value_hbm.at[here], value_ref.at[here], sems.at[1, part]),
            )
        )
    for pair in copies[:AHEAD]:
        for copy in pair:
            copy.start()

    factor = scale * LOG2E
    for s, piece in enumerate(queries):
        for t in range(PAIR):
            start = (PAIR * s + t) * own
            query_ref[start : start + own] = piece[t]
    query_ref[rows] = jnp.zeros((heads, LANES), jnp.bfloat16)
    top_ref[...] = jnp.full(top_ref.shape, NEG_FILL, jnp.float32)
    for ref in (total_ref, sum_ref, score_ref, part_top_ref, part_total_ref, part_sum_ref):
        ref[...] = jnp.zeros(ref.shape, jnp.float32)
    head = lax.broadcasted_iota(jnp.int32, (heads, tokens), 0) // group
    place = lax.broadcasted_iota(jnp.int32, (heads, tokens), 1)
    token = jnp.where(place % kv_local == head, place // kv_local, block_size)
    wide = (heads, LANES)

    def entries(chunk):
        return [list_ref[0, chunk * CHUNK + j] for j in range(CHUNK)]

    def row_of(entry):
        return entry >> (length_bits + block_bits)

    def block_of(entry):
        return (entry >> length_bits) & (blocks - 1)

    def merge_item(row, t, k):
        j = t * PAIR + k
        top, part_top = top_ref[row], part_top_ref[j]
        high = jnp.maximum(top, part_top)
        top_ref[row] = high
        old, new = jnp.exp2((top - high) * factor), jnp.exp2((part_top - high) * factor)
        total_ref[row] = total_ref[row] * old + part_total_ref[j] * new
        sum_ref[row] = sum_ref[row] * old + part_sum_ref[t, k * heads : (k + 1) * heads] * new

    def weigh_item(entry, t, k):
        j = t * PAIR + k
        scores = jnp.where(token <= (entry & (block_size - 1)), score_ref[t, k * heads : (k + 1) * heads], NEG_FILL)
        high = jnp.max(scores, axis=1, keepdims=True)
        weights = jnp.exp2((scores - high) * factor)
        part_top_ref[j] = jnp.broadcast_to(high, wide)
        part_total_ref[j] = jnp.broadcast_to(jnp.sum(weights, axis=1, keepdims=True), wide)
        return weights.astype(jnp.bfloat16)

    def turn(i, carry):
        merged, weighed, scored = (entries(jnp.maximum(i - back, 0)) for back in (2, 1, 0))
        for t in range(TASKS):
            task = slice(t * PAIR, (t + 1) * PAIR)
            for k, entry in enumerate(merged[task]):
                merge_item(jnp.where(i >= 2, row_of(entry), rows), t, k)
            weights = [weigh_item(entry, t, k) for k, entry in enumerate(weighed[task])]
            part_sum_ref[t] = jnp.dot(
                jnp.concatenate(weights, axis=0),
                value_ref[block_of(weighed[task][0])],
                preferred_element_type=jnp.float32,
            )
            score_ref[t] = lax.dot_general(
                jnp.concatenate([query_ref[row_of(entry)] for entry in scored[task]], axis=0),
                key_ref[block_of(scored[task][0])],
                (((1,), (1,)), ((), ())),
                preferred_element_type=jnp.float32,
            )
        return carry

    for part in range(PHASES):
        for copy in copies[part]:
            copy.wait()
        for pair in copies[part + AHEAD : part + AHEAD + 1]:
            for copy in pair:
                copy.start()
        lax.fori_loop(bound_ref[0, part], bound_ref[0, part + 1], turn, 0)
    last = bound_ref[0, PHASES]
    lax.fori_loop(last, last + 2, turn, 0)

    square = (own * heads, LANES)
    eye = lax.broadcasted_iota(jnp.int32, square, 0) == lax.broadcasted_iota(jnp.int32, square, 1)
    line = lax.broadcasted_iota(jnp.int32, wide, 0)
    for q in range(count):
        ref = (keep_ref, send_ref)[q % PAIR]
        mine = slice(q * own, (q + 1) * own)
        top, total = (
            jnp.sum(jnp.where(eye, state[mine].reshape(square), 0.0), axis=0, keepdims=True)
            for state in (top_ref, total_ref)
        )
        ref[q // PAIR, :own] = sum_ref[mine]
        ref[q // PAIR, own] = jnp.where(line == 0, top, jnp.where(line == 1, total, 0.0))


def attend(items, bounds, queries, keys, values, kv_local, scale):
    _, own, heads, _ = queries[0].shape
    count = len(queries) * PAIR
    rows = count * own
    tokens = keys.shape[1]
    keys, values = in_hbm(keys, values)
    state = pltpu.VMEM((rows + 1, heads, LANES), jnp.float32)
    part = pltpu.VMEM((CHUNK, heads, LANES), jnp.float32)
    return pl.pallas_call(
        functools.partial(attend_kernel, scale, heads // kv_local, kv_local, count),
        in_specs=[smem_spec(), smem_spec()] + [vmem_spec()] * len(queries) + [hbm_spec()] * 2,
        out_specs=[vmem_spec()] * PAIR,
        out_shape=[jax.ShapeDtypeStruct((count // PAIR, own + 1, heads, LANES), jnp.float32)] * PAIR,
        scratch_shapes=[
            pltpu.VMEM((rows + 1, heads, LANES), jnp.bfloat16),
            pltpu.VMEM(keys.shape, keys.dtype),
            pltpu.VMEM(values.shape, values.dtype),
            state,
            state,
            state,
            pltpu.VMEM((TASKS, PAIR * heads, tokens), jnp.float32),
            part,
            part,
            pltpu.VMEM((TASKS, PAIR * heads, LANES), jnp.float32),
            pltpu.SemaphoreType.DMA((2, PHASES)),
        ],
        compiler_params=params(40),
        name="attend",
    )(items, bounds, *queries, keys, values)


def merge_pair_kernel(scale, keep_ref, got_ref, out_ref):
    chips, sections, heads, _ = keep_ref.shape
    own = sections - 1
    factor = scale * LOG2E
    line = lax.broadcasted_iota(jnp.int32, (heads, LANES), 0)
    shares, stats = [], []
    for s in range(chips):
        keep, got = keep_ref[s, own], got_ref[s, own]
        high = jnp.maximum(keep[0:1], got[0:1])
        pair = [jnp.exp2((x[0:1] - high) * factor) for x in (keep, got)]
        shares += pair
        total = pair[0] * keep[1:2] + pair[1] * got[1:2]
        stat = jnp.zeros((heads, LANES), jnp.float32)
        for position, piece in enumerate(split3(high) + split3(total)):
            stat = jnp.where(line == position, piece, stat)
        stats.append(stat)
    columns = jnp.concatenate(shares, axis=0).T
    flat = (own * heads, LANES)
    for s in range(chips):
        total = keep_ref[s, :own].reshape(flat) * columns[:, PAIR * s : PAIR * s + 1]
        total = total + got_ref[s, :own].reshape(flat) * columns[:, PAIR * s + 1 : PAIR * s + 2]
        out_ref[s, :own] = total.astype(jnp.bfloat16).reshape(own, heads, LANES)
        out_ref[s, own] = stats[s].astype(jnp.bfloat16)


def merge_pair(keep, got, scale):
    return pl.pallas_call(
        functools.partial(merge_pair_kernel, scale),
        in_specs=[vmem_spec()] * 2,
        out_specs=vmem_spec(),
        out_shape=jax.ShapeDtypeStruct(keep.shape, jnp.bfloat16),
        compiler_params=params(16),
        name="merge_pair",
    )(keep, got)


def merge_kernel(scale, *refs):
    pieces, (out_ref, wide_ref) = refs[:-2], refs[-2:]
    chips, sections, heads, _ = pieces[0].shape
    own = sections - 1
    factor = scale * LOG2E
    shares = []
    for s in range(chips):
        stats = [pieces[j][s ^ j, own].astype(jnp.float32) for j in range(chips)]
        tops = jnp.concatenate([x[0:1] + x[1:2] + x[2:3] for x in stats], axis=0)
        totals = jnp.concatenate([x[3:4] + x[4:5] + x[5:6] for x in stats], axis=0)
        weights = jnp.exp2((tops - jnp.max(tops, axis=0, keepdims=True)) * factor)
        shares.append(weights / jnp.sum(weights * totals, axis=0, keepdims=True))
    columns = jnp.concatenate(shares, axis=0).T
    flat = own * heads
    for s in range(chips):
        total = jnp.zeros((flat, LANES), jnp.float32)
        for j in range(chips):
            part = pieces[j][s ^ j, :own].astype(jnp.float32).reshape(flat, LANES)
            total = total + part * columns[:, s * chips + j : s * chips + j + 1]
        wide_ref[s * flat : (s + 1) * flat, :] = total
    rows = [wide_ref[pl.ds(h, chips * own, stride=heads), :] for h in range(heads)]
    out_ref[...] = jnp.concatenate(rows, axis=1).astype(jnp.bfloat16)


def merge(pieces, scale):
    chips, sections, heads, _ = pieces[0].shape
    own = sections - 1
    return pl.pallas_call(
        functools.partial(merge_kernel, scale),
        in_specs=[vmem_spec()] * chips,
        out_specs=vmem_spec(),
        out_shape=jax.ShapeDtypeStruct((chips * own, heads * LANES), jnp.bfloat16),
        scratch_shapes=[pltpu.VMEM((chips * own * heads, LANES), jnp.float32)],
        compiler_params=params(32),
        name="merge",
    )(*pieces)


def output_kernel(own, row_count, *refs):
    pieces, weight_ref = refs[:PAIR], refs[PAIR]
    own_ref, sends = refs[PAIR + 1], refs[PAIR + 2 : PAIR + 1 + row_count]
    rows_ref, terms_ref = refs[PAIR + 1 + row_count :]
    me = lax.axis_index("kv")
    for t in range(PAIR):
        piece = pieces[t][...].astype(jnp.float32)
        for s in range(piece.shape[0] // own):
            start = pl.multiple_of(jnp.bitwise_xor(me, PAIR * s + t) * own, own)
            rows_ref[pl.ds(start, own), :] = piece[s * own : (s + 1) * own]
    terms_ref[...] = jnp.dot(
        rows_ref[...].astype(jnp.bfloat16), weight_ref[...], preferred_element_type=jnp.float32
    )
    me = lax.axis_index("row")
    part = own_ref.shape[0]
    for s, ref in enumerate((own_ref, *sends)):
        start = pl.multiple_of(jnp.bitwise_xor(me, s) * part, part)
        ref[...] = terms_ref[pl.ds(start, part), :].astype(ref.dtype)


def project_out(pieces, weight, own, row_count):
    half, width = pieces[0].shape
    rows, columns = PAIR * half, weight.shape[1]
    part = rows // row_count
    send = jax.ShapeDtypeStruct((part, columns), jnp.bfloat16)
    return pl.pallas_call(
        functools.partial(output_kernel, own, row_count),
        in_specs=[vmem_spec()] * (PAIR + 1),
        out_specs=[vmem_spec()] * row_count,
        out_shape=[jax.ShapeDtypeStruct((part, columns), jnp.float32)] + [send] * (row_count - 1),
        scratch_shapes=[pltpu.VMEM((rows, width), jnp.float32), pltpu.VMEM((rows, columns), jnp.float32)],
        compiler_params=params(24),
        name="project_out",
    )(*pieces, weight)


def exchange(x, axis, s):
    count = lax.axis_size(axis)
    return lax.ppermute(x, axis, [(i, i ^ s) for i in range(count)])


def gather_chips(x):
    return [x] + [exchange(x, "kv", s) for s in range(PAIR, lax.axis_size("kv"), PAIR)]


def gather_pairs(x):
    return gather_chips(jnp.concatenate([x, exchange(x, "kv", 1)], axis=0))


def local(
    hidden,
    query_weight,
    adapter_down_weight,
    adapter_up_weight,
    query_norm_gain,
    paged_key_cache,
    paged_value_cache,
    output_weight,
    holder,
    holder_block_index,
    block_used_length,
    tenant,
    tenant_adapter,
):
    own, slots = holder.shape
    rows, depth = hidden.shape
    kv_count = lax.axis_size("kv")
    row_count = lax.axis_size("row")
    adapters, _, rank = adapter_down_weight.shape
    width = query_weight.shape[1]
    head_size = query_norm_gain.shape[0]
    heads = width // head_size
    blocks, block_size, kv_local, _ = paged_key_cache.shape
    scale = 1.0 / math.sqrt(head_size)

    chips = kv_count // PAIR
    keep, send = project(
        tenant.reshape(1, rows),
        tenant_adapter.reshape(1, -1),
        holder,
        holder_block_index,
        block_used_length,
        hidden,
        query_weight,
        jnp.swapaxes(adapter_down_weight, 1, 2).reshape(adapters * rank, depth),
        adapter_up_weight.reshape(adapters * rank, width),
        rank,
        chips,
    )
    parts = add_pair(keep, exchange(send, "kv", 1))
    parts = [parts[0]] + [exchange(parts[s], "kv", PAIR * s) for s in range(1, chips)]

    position = (jnp.sum(block_used_length, axis=1) - 1).astype(jnp.float32)
    half = head_size // 2
    frequency = ROPE_BASE ** (-(jnp.arange(half, dtype=jnp.float32) * 2.0) / head_size)
    angles = position[:, None] * frequency[None, :]
    cosine = jnp.concatenate([jnp.cos(angles), jnp.cos(angles)], axis=-1)
    sine = jnp.concatenate([-jnp.sin(angles), jnp.sin(angles)], axis=-1)
    queries = make_queries(parts, cosine, sine, query_norm_gain.reshape(1, head_size), heads)
    queries = [q.reshape(PAIR, own, heads, head_size) for q in gather_pairs(queries)]
    items, bounds = make_list(parts, slots, blocks, block_size, kv_count)

    keys = paged_key_cache.reshape(blocks, block_size * kv_local, head_size)
    values = paged_value_cache.reshape(blocks, block_size * kv_local, head_size)
    keep, send = attend(items, bounds, queries, keys, values, kv_local, scale)
    merged = merge_pair(keep, exchange(send, "kv", 1), scale)
    attention = merge(gather_chips(merged), scale)
    terms = project_out([attention, exchange(attention, "kv", 1)], output_weight, own, row_count)
    total = terms[0]
    for s in range(1, row_count):
        total = total + exchange(terms[s], "row", s).astype(jnp.float32)
    return total.astype(jnp.bfloat16)


def solution(mesh):
    return jax.shard_map(
        local,
        mesh=mesh,
        in_specs=(
            P(None, "kv"),
            P("kv", "row"),
            P(None, "kv", None),
            P(None, None, "row"),
            P(),
            P("kv", None, "row", None),
            P("kv", None, "row", None),
            P("row", "kv"),
            P("kv", None),
            P("kv", None),
            P("kv", None),
            P(),
            P(),
        ),
        out_specs=P("row", "kv"),
        check_vma=False,
    )
```

```python
import functools
import math

import jax
import jax.numpy as jnp
from jax import lax
from jax.experimental import pallas as pl
from jax.experimental.pallas import tpu as pltpu
from jax.sharding import PartitionSpec as P

ADAPTER_SCALE = 0.5
ROPE_BASE = 1000000.0
EPSILON = 1e-06
NEG_FILL = -1e30
LANES = 128
COLUMN_TILE = 256
PAIR = 2
GROUP = 4
TASKS = 8
CHUNK = GROUP * TASKS
PHASES = 8
AHEAD = 3
DEPTH = 256
LOG2E = math.log2(math.e)
MIB = 1024 * 1024


def params(mib):
    return pltpu.CompilerParams(vmem_limit_bytes=mib * MIB)


def vmem_spec():
    return pl.BlockSpec(memory_space=pltpu.VMEM)


def in_hbm(*arrays):
    return [pltpu.with_memory_space_constraint(x, pltpu.HBM) for x in arrays]


def hbm_spec():
    return pl.BlockSpec(memory_space=pltpu.HBM)


def smem_spec():
    return pl.BlockSpec(memory_space=pltpu.SMEM)


def split2(x):
    high = x.astype(jnp.bfloat16)
    return high, (x - high.astype(jnp.float32)).astype(jnp.bfloat16)


def split3(x):
    high = x.astype(jnp.bfloat16).astype(jnp.float32)
    rest = x - high
    middle = rest.astype(jnp.bfloat16).astype(jnp.float32)
    return high, middle, (rest - middle).astype(jnp.bfloat16).astype(jnp.float32)


def to_column(row, count):
    shape = (count, count)
    eye = lax.broadcasted_iota(jnp.int32, shape, 0) == lax.broadcasted_iota(jnp.int32, shape, 1)
    return jnp.sum(jnp.where(eye, row.astype(jnp.float32), 0.0), axis=1, keepdims=True)


def project_kernel(
    rank,
    tenant_ref,
    adapter_ref,
    holder_ref,
    block_ref,
    length_ref,
    hidden_hbm,
    weight_hbm,
    down_hbm,
    up_hbm,
    keep_ref,
    send_ref,
    hidden_ref,
    weight_ref,
    down_ref,
    up_ref,
    total_ref,
    sems,
):
    chips, own, _ = keep_ref.shape
    rows, depth = hidden_ref.shape
    low_width = down_ref.shape[0]
    width = weight_ref.shape[1]
    tiles = width // COLUMN_TILE

    def start(copies):
        for copy in copies:
            copy.start()
        return copies

    def chunks(hbm, ref, offset):
        spans = [slice(i, min(i + DEPTH, ref.shape[0])) for i in range(0, ref.shape[0], DEPTH)]
        return [
            (span, pltpu.make_async_copy(hbm.at[span], ref.at[span], sems.at[offset + i]))
            for i, span in enumerate(spans)
        ]

    first = start(
        [
            pltpu.make_async_copy(hidden_hbm, hidden_ref, sems.at[0]),
            pltpu.make_async_copy(down_hbm, down_ref, sems.at[1]),
        ]
    )
    up_chunks = chunks(up_hbm, up_ref, 2)
    weight_chunks = chunks(weight_hbm, weight_ref, 2 + len(up_chunks))
    waiting = [copy for _, copy in up_chunks + weight_chunks]
    start(waiting[:1])

    slots = holder_ref.shape[1]
    numbers = [holder_ref[...], block_ref[...], length_ref[...], jnp.zeros((own, LANES - 3 * slots), jnp.int32)]
    numbers = jnp.concatenate(numbers, axis=1).astype(jnp.float32)
    for c in range(chips):
        keep_ref[c, :, width:] = numbers
        send_ref[c, :, width:] = numbers
    tenants = adapter_ref.shape[1]
    tenant = to_column(tenant_ref[...], rows)
    pick = lax.broadcasted_iota(jnp.int32, (rows, tenants), 1).astype(jnp.float32) == tenant
    adapter = jnp.sum(jnp.where(pick, adapter_ref[...].astype(jnp.float32), 0.0), axis=1, keepdims=True).astype(
        jnp.int32
    )
    for copy in first:
        copy.wait()
    start(waiting[1:3])
    hidden = hidden_ref[...]
    low = lax.dot_general(hidden, down_ref[...], (((1,), (1,)), ((), ())), preferred_element_type=jnp.float32)
    column = lax.broadcasted_iota(jnp.int32, (rows, low_width), 1)
    match = (column >= adapter * rank) & (column < adapter * rank + rank)
    high, low = split2(jnp.where(match, ADAPTER_SCALE * low, 0.0))
    both = jnp.concatenate([high, low], axis=0)
    columns = [slice(i * COLUMN_TILE, (i + 1) * COLUMN_TILE) for i in range(tiles)]
    for i, (span, copy) in enumerate(up_chunks):
        copy.wait()
        start(waiting[i + 3 : i + 4])
        for tile in columns:
            up_high, up_low = split2(up_ref[span, tile])
            twice = jnp.dot(both[:, span], up_high, preferred_element_type=jnp.float32)
            total = jnp.dot(high[:, span], up_low, preferred_element_type=jnp.float32)
            total = (total + twice[rows:]) + twice[:rows]
            total_ref[:, tile] = total if i == 0 else total_ref[:, tile] + total
    even = lax.axis_index("kv") % PAIR == 0
    for i, (span, copy) in enumerate(weight_chunks):
        copy.wait()
        start(waiting[i + len(up_chunks) + 3 : i + len(up_chunks) + 4])
        for tile in columns:
            total = total_ref[:, tile] + jnp.dot(
                hidden[:, span], weight_ref[span, tile], preferred_element_type=jnp.float32
            )
            if i < len(weight_chunks) - 1:
                total_ref[:, tile] = total
            else:
                total = total.reshape(chips, PAIR, own, COLUMN_TILE)
                keep_ref[:, :, tile] = jnp.where(even, total[:, 0], total[:, 1])
                send_ref[:, :, tile] = jnp.where(even, total[:, 1], total[:, 0])


def project(tenant, tenant_adapter, holder, block, length, hidden, query_weight, down, up, rank, chips):
    rows, depth = hidden.shape
    width = query_weight.shape[1]
    out = jax.ShapeDtypeStruct((chips, rows // chips // PAIR, width + LANES), jnp.float32)
    operands = in_hbm(tenant, tenant_adapter, holder, block, length, hidden, query_weight, down, up)
    large = operands[5:]
    return pl.pallas_call(
        functools.partial(project_kernel, rank),
        in_specs=[vmem_spec()] * 5 + [hbm_spec()] * 4,
        out_specs=[vmem_spec()] * 2,
        out_shape=[out] * 2,
        scratch_shapes=[pltpu.VMEM(x.shape, x.dtype) for x in large]
        + [
            pltpu.VMEM((rows, width), jnp.float32),
            pltpu.SemaphoreType.DMA((2 + pl.cdiv(depth, DEPTH) + pl.cdiv(down.shape[0], DEPTH),)),
        ],
        compiler_params=params(24),
        name="project",
    )(*operands)


def pair_kernel(keep_ref, got_ref, *out_refs):
    width = keep_ref.shape[2] - LANES
    chip = lax.axis_index("kv") // PAIR
    for s, ref in enumerate(out_refs):
        c = jnp.bitwise_xor(chip, s)
        ref[:, :width] = keep_ref[c, :, :width] + got_ref[c, :, :width]
        ref[:, width : width + LANES] = keep_ref[0, :, width:]
        ref[:, width + LANES :] = got_ref[0, :, width:]


def add_pair(keep, got):
    chips, own, width = keep.shape
    return pl.pallas_call(
        pair_kernel,
        in_specs=[vmem_spec()] * 2,
        out_specs=[vmem_spec()] * chips,
        out_shape=[jax.ShapeDtypeStruct((own, width + LANES), jnp.float32)] * chips,
        compiler_params=params(16),
        name="add_pair",
    )(keep, got)


def queries_kernel(*refs):
    parts, (cosine_ref, sine_ref, gain_ref, out_ref, turned_ref) = refs[:-5], refs[-5:]
    heads = turned_ref.shape[1]
    cosine, sine, gain = cosine_ref[...], sine_ref[...], gain_ref[...]
    for h in range(heads):
        columns = slice(h * LANES, (h + 1) * LANES)
        query = parts[0][:, columns]
        for part in parts[1:]:
            query = query + part[:, columns]
        square = jnp.mean(query * query, axis=-1, keepdims=True)
        query = query * lax.rsqrt(square + EPSILON) * gain
        turned_ref[:, h, :] = query * cosine + pltpu.roll(query, LANES // 2, 1) * sine
    out_ref[...] = turned_ref[...].astype(jnp.bfloat16)


def make_queries(parts, cosine, sine, gain, heads):
    own = parts[0].shape[0]
    shape = (own, heads, LANES)
    return pl.pallas_call(
        queries_kernel,
        in_specs=[vmem_spec()] * (len(parts) + 3),
        out_specs=vmem_spec(),
        out_shape=jax.ShapeDtypeStruct(shape, jnp.bfloat16),
        scratch_shapes=[pltpu.VMEM(shape, jnp.float32)],
        compiler_params=params(16),
        name="queries",
    )(*parts, cosine, sine, gain)


def list_kernel(blocks, block_size, slots, *refs):
    pieces, (list_ref, bound_ref, place_ref, value_ref) = refs[:-4], refs[-4:]
    rows = place_ref.shape[0]
    capacity = list_ref.shape[1]
    me = lax.axis_index("kv").astype(jnp.float32)
    numbers = jnp.concatenate([p[:, i * LANES : (i + 1) * LANES] for p in pieces for i in range(PAIR)], axis=0)
    holder, block, length = (numbers[:, i * slots : (i + 1) * slots] for i in range(3))
    row = lax.broadcasted_iota(jnp.int32, (rows, slots), 0).astype(jnp.float32)
    spare = float(rows * blocks * block_size)
    value_ref[...] = (row * blocks + block) * block_size + (length - 1.0) - spare
    mine = holder == me
    key = jnp.where(mine, block, -1.0)

    def before(count, axis):
        first = lax.broadcasted_iota(jnp.int32, (count, count), axis)
        return jnp.where(first < lax.broadcasted_iota(jnp.int32, (count, count), 1 - axis), 1.0, 0.0).astype(
            jnp.bfloat16
        )

    lane = lax.broadcasted_iota(jnp.int32, (rows, blocks), 1).astype(jnp.float32)
    picks = [jnp.where(key[:, j : j + 1] == lane, 1.0, 0.0) for j in range(slots)]
    count = jnp.sum(functools.reduce(jnp.add, picks), axis=0, keepdims=True)
    tasks = jnp.floor((count + (GROUP - 1)) * (1.0 / GROUP))
    earlier = jnp.dot(
        jnp.broadcast_to(tasks, (8, blocks)).astype(jnp.bfloat16),
        before(blocks, 0),
        preferred_element_type=jnp.float32,
    )[:1]
    base = earlier * GROUP
    row_before = before(rows, 1)
    slot = lax.broadcasted_iota(jnp.int32, (rows, slots), 1)
    place = jnp.full((rows, slots), -1.0, jnp.float32)
    for j in range(slots):
        above = jnp.dot(row_before, picks[j].astype(jnp.bfloat16), preferred_element_type=jnp.float32)
        here = jnp.sum(picks[j] * (above + base), axis=1, keepdims=True)
        place = jnp.where((slot == j) & mine, here, place)
        base = base + jnp.sum(picks[j], axis=0, keepdims=True)
    place_ref[...] = place
    size = blocks // PHASES
    end = earlier + tasks
    block_lane = lax.broadcasted_iota(jnp.int32, (1, blocks), 1)
    bound_lane = lax.broadcasted_iota(jnp.int32, (1, LANES), 1)
    bounds = jnp.zeros((1, LANES), jnp.float32)
    for part in range(PHASES):
        done = jnp.sum(jnp.where(block_lane == (part + 1) * size - 1, end, 0.0), axis=1, keepdims=True)
        done = done * (1.0 / TASKS)
        done = jnp.ceil(done) if part == PHASES - 1 else jnp.floor(done)
        bounds = jnp.where(bound_lane == part + 1, done, bounds)
    bound_ref[...] = bounds.astype(jnp.int32)
    target = lax.broadcasted_iota(jnp.int32, (8, capacity), 1).astype(jnp.float32)

    def tile(t, total):
        here = pl.ds(pl.multiple_of(t * 8, 8), 8)
        places, values = place_ref[here, :], value_ref[here, :]
        for j in range(slots):
            total = total + jnp.where(places[:, j : j + 1] == target, values[:, j : j + 1], 0.0)
        return total

    total = lax.fori_loop(0, rows // 8, tile, jnp.zeros((8, capacity), jnp.float32))
    list_ref[...] = (jnp.sum(total, axis=0, keepdims=True) + spare).astype(jnp.int32)


def make_list(parts, slots, blocks, block_size, count):
    own, width = parts[0].shape
    rows = count * own
    most = 2 * own * slots // count * count + (GROUP - 1) * blocks + 3 * CHUNK
    capacity = -(-most // LANES) * LANES
    last = width // (PAIR * LANES) - 1
    return pl.pallas_call(
        functools.partial(list_kernel, blocks, block_size, slots),
        grid=(1,),
        in_specs=[pl.BlockSpec((own, PAIR * LANES), lambda i: (0, last))] * len(parts),
        out_specs=[
            pl.BlockSpec((1, capacity), lambda i: (0, 0)),
            pl.BlockSpec((1, LANES), lambda i: (0, 0)),
        ],
        out_shape=[
            jax.ShapeDtypeStruct((1, capacity), jnp.int32),
            jax.ShapeDtypeStruct((1, LANES), jnp.int32),
        ],
        scratch_shapes=[pltpu.VMEM((rows, slots), jnp.float32), pltpu.VMEM((rows, slots), jnp.float32)],
        compiler_params=params(16),
        cost_estimate=pl.CostEstimate(flops=10**8, bytes_accessed=10**7, transcendentals=0),
        name="slot_list",
    )(*parts)


def attend_kernel(scale, group, kv_local, count, list_ref, bound_ref, *refs):
    queries, refs = refs[: count // PAIR], refs[count // PAIR :]
    (key_hbm, value_hbm, keep_ref, send_ref, query_ref, key_ref, value_ref, top_ref, total_ref, sum_ref) = refs[:10]
    (score_ref, part_top_ref, part_total_ref, part_sum_ref, sems) = refs[10:]
    heads = query_ref.shape[1]
    rows = query_ref.shape[0] - 1
    own = rows // count
    blocks, tokens, _ = key_ref.shape
    block_size = tokens // kv_local
    size = blocks // PHASES
    length_bits = (block_size - 1).bit_length()
    block_bits = (blocks - 1).bit_length()
    copies = []
    for part in range(PHASES):
        here = pl.ds(part * size, size)
        copies.append(
            (
                pltpu.make_async_copy(key_hbm.at[here], key_ref.at[here], sems.at[0, part]),
                pltpu.make_async_copy(value_hbm.at[here], value_ref.at[here], sems.at[1, part]),
            )
        )
    for pair in copies[:AHEAD]:
        for copy in pair:
            copy.start()

    factor = scale * LOG2E
    for s, piece in enumerate(queries):
        for t in range(PAIR):
            start = (PAIR * s + t) * own
            query_ref[start : start + own] = piece[t]
    query_ref[rows] = jnp.zeros((heads, LANES), jnp.bfloat16)
    top_ref[...] = jnp.full(top_ref.shape, NEG_FILL, jnp.float32)
    for ref in (total_ref, sum_ref, score_ref, part_top_ref, part_total_ref, part_sum_ref):
        ref[...] = jnp.zeros(ref.shape, jnp.float32)
    head = lax.broadcasted_iota(jnp.int32, (heads, tokens), 0) // group
    place = lax.broadcasted_iota(jnp.int32, (heads, tokens), 1)
    token = jnp.where(place % kv_local == head, place // kv_local, block_size)
    wide = (heads, LANES)

    def entries(chunk):
        return [list_ref[0, chunk * CHUNK + j] for j in range(CHUNK)]

    def row_of(entry):
        return entry >> (length_bits + block_bits)

    def block_of(entry):
        return (entry >> length_bits) & (blocks - 1)

    def merge_item(row, t, k):
        j = t * GROUP + k
        top, part_top = top_ref[row], part_top_ref[j]
        high = jnp.maximum(top, part_top)
        top_ref[row] = high
        old, new = jnp.exp2((top - high) * factor), jnp.exp2((part_top - high) * factor)
        total_ref[row] = total_ref[row] * old + part_total_ref[j] * new
        sum_ref[row] = sum_ref[row] * old + part_sum_ref[t, k * heads : (k + 1) * heads] * new

    def weigh_item(entry, t, k):
        j = t * GROUP + k
        scores = jnp.where(token <= (entry & (block_size - 1)), score_ref[t, k * heads : (k + 1) * heads], NEG_FILL)
        high = jnp.max(scores, axis=1, keepdims=True)
        weights = jnp.exp2((scores - high) * factor)
        part_top_ref[j] = jnp.broadcast_to(high, wide)
        part_total_ref[j] = jnp.broadcast_to(jnp.sum(weights, axis=1, keepdims=True), wide)
        return weights.astype(jnp.bfloat16)

    def turn(i, carry):
        merged, weighed, scored = (entries(jnp.maximum(i - back, 0)) for back in (2, 1, 0))
        for t in range(TASKS):
            task = slice(t * GROUP, (t + 1) * GROUP)
            for k, entry in enumerate(merged[task]):
                merge_item(jnp.where(i >= 2, row_of(entry), rows), t, k)
            weights = [weigh_item(entry, t, k) for k, entry in enumerate(weighed[task])]
            part_sum_ref[t] = jnp.dot(
                jnp.concatenate(weights, axis=0),
                value_ref[block_of(weighed[task][0])],
                preferred_element_type=jnp.float32,
            )
            score_ref[t] = lax.dot_general(
                jnp.concatenate([query_ref[row_of(entry)] for entry in scored[task]], axis=0),
                key_ref[block_of(scored[task][0])],
                (((1,), (1,)), ((), ())),
                preferred_element_type=jnp.float32,
            )
        return carry

    for part in range(PHASES):
        for copy in copies[part]:
            copy.wait()
        for pair in copies[part + AHEAD : part + AHEAD + 1]:
            for copy in pair:
                copy.start()
        lax.fori_loop(bound_ref[0, part], bound_ref[0, part + 1], turn, 0)
    last = bound_ref[0, PHASES]
    lax.fori_loop(last, last + 2, turn, 0)

    square = (own * heads, LANES)
    eye = lax.broadcasted_iota(jnp.int32, square, 0) == lax.broadcasted_iota(jnp.int32, square, 1)
    line = lax.broadcasted_iota(jnp.int32, wide, 0)
    for q in range(count):
        ref = (keep_ref, send_ref)[q % PAIR]
        mine = slice(q * own, (q + 1) * own)
        top, total = (
            jnp.sum(jnp.where(eye, state[mine].reshape(square), 0.0), axis=0, keepdims=True)
            for state in (top_ref, total_ref)
        )
        ref[q // PAIR, :own] = sum_ref[mine]
        ref[q // PAIR, own] = jnp.where(line == 0, top, jnp.where(line == 1, total, 0.0))


def attend(items, bounds, queries, keys, values, kv_local, scale):
    _, own, heads, _ = queries[0].shape
    count = len(queries) * PAIR
    rows = count * own
    tokens = keys.shape[1]
    keys, values = in_hbm(keys, values)
    state = pltpu.VMEM((rows + 1, heads, LANES), jnp.float32)
    part = pltpu.VMEM((CHUNK, heads, LANES), jnp.float32)
    return pl.pallas_call(
        functools.partial(attend_kernel, scale, heads // kv_local, kv_local, count),
        in_specs=[smem_spec(), smem_spec()] + [vmem_spec()] * len(queries) + [hbm_spec()] * 2,
        out_specs=[vmem_spec()] * PAIR,
        out_shape=[jax.ShapeDtypeStruct((count // PAIR, own + 1, heads, LANES), jnp.float32)] * PAIR,
        scratch_shapes=[
            pltpu.VMEM((rows + 1, heads, LANES), jnp.bfloat16),
            pltpu.VMEM(keys.shape, keys.dtype),
            pltpu.VMEM(values.shape, values.dtype),
            state,
            state,
            state,
            pltpu.VMEM((TASKS, GROUP * heads, tokens), jnp.float32),
            part,
            part,
            pltpu.VMEM((TASKS, GROUP * heads, LANES), jnp.float32),
            pltpu.SemaphoreType.DMA((2, PHASES)),
        ],
        compiler_params=params(40),
        name="attend",
    )(items, bounds, *queries, keys, values)


def merge_pair_kernel(scale, keep_ref, got_ref, out_ref):
    chips, sections, heads, _ = keep_ref.shape
    own = sections - 1
    factor = scale * LOG2E
    line = lax.broadcasted_iota(jnp.int32, (heads, LANES), 0)
    shares, stats = [], []
    for s in range(chips):
        keep, got = keep_ref[s, own], got_ref[s, own]
        high = jnp.maximum(keep[0:1], got[0:1])
        pair = [jnp.exp2((x[0:1] - high) * factor) for x in (keep, got)]
        shares += pair
        total = pair[0] * keep[1:2] + pair[1] * got[1:2]
        stat = jnp.zeros((heads, LANES), jnp.float32)
        for position, piece in enumerate(split3(high) + split3(total)):
            stat = jnp.where(line == position, piece, stat)
        stats.append(stat)
    columns = jnp.concatenate(shares, axis=0).T
    flat = (own * heads, LANES)
    for s in range(chips):
        total = keep_ref[s, :own].reshape(flat) * columns[:, PAIR * s : PAIR * s + 1]
        total = total + got_ref[s, :own].reshape(flat) * columns[:, PAIR * s + 1 : PAIR * s + 2]
        out_ref[s, :own] = total.astype(jnp.bfloat16).reshape(own, heads, LANES)
        out_ref[s, own] = stats[s].astype(jnp.bfloat16)


def merge_pair(keep, got, scale):
    return pl.pallas_call(
        functools.partial(merge_pair_kernel, scale),
        in_specs=[vmem_spec()] * 2,
        out_specs=vmem_spec(),
        out_shape=jax.ShapeDtypeStruct(keep.shape, jnp.bfloat16),
        compiler_params=params(16),
        name="merge_pair",
    )(keep, got)


def merge_kernel(scale, *refs):
    pieces, (out_ref, wide_ref) = refs[:-2], refs[-2:]
    chips, sections, heads, _ = pieces[0].shape
    own = sections - 1
    factor = scale * LOG2E
    shares = []
    for s in range(chips):
        stats = [pieces[j][s ^ j, own].astype(jnp.float32) for j in range(chips)]
        tops = jnp.concatenate([x[0:1] + x[1:2] + x[2:3] for x in stats], axis=0)
        totals = jnp.concatenate([x[3:4] + x[4:5] + x[5:6] for x in stats], axis=0)
        weights = jnp.exp2((tops - jnp.max(tops, axis=0, keepdims=True)) * factor)
        shares.append(weights / jnp.sum(weights * totals, axis=0, keepdims=True))
    columns = jnp.concatenate(shares, axis=0).T
    flat = own * heads
    for s in range(chips):
        total = jnp.zeros((flat, LANES), jnp.float32)
        for j in range(chips):
            part = pieces[j][s ^ j, :own].astype(jnp.float32).reshape(flat, LANES)
            total = total + part * columns[:, s * chips + j : s * chips + j + 1]
        wide_ref[s * flat : (s + 1) * flat, :] = total
    rows = [wide_ref[pl.ds(h, chips * own, stride=heads), :] for h in range(heads)]
    out_ref[...] = jnp.concatenate(rows, axis=1).astype(jnp.bfloat16)


def merge(pieces, scale):
    chips, sections, heads, _ = pieces[0].shape
    own = sections - 1
    return pl.pallas_call(
        functools.partial(merge_kernel, scale),
        in_specs=[vmem_spec()] * chips,
        out_specs=vmem_spec(),
        out_shape=jax.ShapeDtypeStruct((chips * own, heads * LANES), jnp.bfloat16),
        scratch_shapes=[pltpu.VMEM((chips * own * heads, LANES), jnp.float32)],
        compiler_params=params(32),
        name="merge",
    )(*pieces)


def output_kernel(own, row_count, *refs):
    pieces, weight_ref = refs[:PAIR], refs[PAIR]
    keep_ref, send_ref, rows_ref, terms_ref = refs[PAIR + 1 :]
    me = lax.axis_index("kv")
    for t in range(PAIR):
        piece = pieces[t][...].astype(jnp.float32)
        for s in range(piece.shape[0] // own):
            start = pl.multiple_of(jnp.bitwise_xor(me, PAIR * s + t) * own, own)
            rows_ref[pl.ds(start, own), :] = piece[s * own : (s + 1) * own]
    terms_ref[...] = jnp.dot(
        rows_ref[...].astype(jnp.bfloat16), weight_ref[...], preferred_element_type=jnp.float32
    )
    me = lax.axis_index("row")
    part = keep_ref.shape[1]
    for s in range(row_count):
        start = pl.multiple_of(jnp.bitwise_xor(me, s) * part, part)
        ref = (keep_ref, send_ref)[s % PAIR]
        ref[s // PAIR] = terms_ref[pl.ds(start, part), :].astype(ref.dtype)


def project_out(pieces, weight, own, row_count):
    half, width = pieces[0].shape
    rows, columns = PAIR * half, weight.shape[1]
    shape = (row_count // PAIR, rows // row_count, columns)
    return pl.pallas_call(
        functools.partial(output_kernel, own, row_count),
        in_specs=[vmem_spec()] * (PAIR + 1),
        out_specs=[vmem_spec()] * PAIR,
        out_shape=[jax.ShapeDtypeStruct(shape, jnp.float32), jax.ShapeDtypeStruct(shape, jnp.bfloat16)],
        scratch_shapes=[pltpu.VMEM((rows, width), jnp.float32), pltpu.VMEM((rows, columns), jnp.float32)],
        compiler_params=params(24),
        name="project_out",
    )(*pieces, weight)


def exchange(x, axis, s):
    count = lax.axis_size(axis)
    return lax.ppermute(x, axis, [(i, i ^ s) for i in range(count)])


def gather_chips(x):
    return [x] + [exchange(x, "kv", s) for s in range(PAIR, lax.axis_size("kv"), PAIR)]


def gather_pairs(x):
    return gather_chips(jnp.concatenate([x, exchange(x, "kv", 1)], axis=0))


def local(
    hidden,
    query_weight,
    adapter_down_weight,
    adapter_up_weight,
    query_norm_gain,
    paged_key_cache,
    paged_value_cache,
    output_weight,
    holder,
    holder_block_index,
    block_used_length,
    tenant,
    tenant_adapter,
):
    own, slots = holder.shape
    rows, depth = hidden.shape
    kv_count = lax.axis_size("kv")
    row_count = lax.axis_size("row")
    adapters, _, rank = adapter_down_weight.shape
    width = query_weight.shape[1]
    head_size = query_norm_gain.shape[0]
    heads = width // head_size
    blocks, block_size, kv_local, _ = paged_key_cache.shape
    scale = 1.0 / math.sqrt(head_size)

    chips = kv_count // PAIR
    keep, send = project(
        tenant.reshape(1, rows),
        tenant_adapter.reshape(1, -1),
        holder,
        holder_block_index,
        block_used_length,
        hidden,
        query_weight,
        jnp.swapaxes(adapter_down_weight, 1, 2).reshape(adapters * rank, depth),
        adapter_up_weight.reshape(adapters * rank, width),
        rank,
        chips,
    )
    parts = add_pair(keep, exchange(send, "kv", 1))
    parts = [parts[0]] + [exchange(parts[s], "kv", PAIR * s) for s in range(1, chips)]

    position = (jnp.sum(block_used_length, axis=1) - 1).astype(jnp.float32)
    half = head_size // 2
    frequency = ROPE_BASE ** (-(jnp.arange(half, dtype=jnp.float32) * 2.0) / head_size)
    angles = position[:, None] * frequency[None, :]
    cosine = jnp.concatenate([jnp.cos(angles), jnp.cos(angles)], axis=-1)
    sine = jnp.concatenate([-jnp.sin(angles), jnp.sin(angles)], axis=-1)
    queries = make_queries(parts, cosine, sine, query_norm_gain.reshape(1, head_size), heads)
    queries = [q.reshape(PAIR, own, heads, head_size) for q in gather_pairs(queries)]
    items, bounds = make_list(parts, slots, blocks, block_size, kv_count)

    keys = paged_key_cache.reshape(blocks, block_size * kv_local, head_size)
    values = paged_value_cache.reshape(blocks, block_size * kv_local, head_size)
    keep, send = attend(items, bounds, queries, keys, values, kv_local, scale)
    merged = merge_pair(keep, exchange(send, "kv", 1), scale)
    attention = merge(gather_chips(merged), scale)
    keep, send = project_out([attention, exchange(attention, "kv", 1)], output_weight, own, row_count)
    step = 1
    while True:
        total = keep + exchange(send, "row", step).astype(jnp.float32)
        step *= 2
        if step == row_count:
            return total[0].astype(jnp.bfloat16)
        keep, send = total[0::2], total[1::2]


def solution(mesh):
    return jax.shard_map(
        local,
        mesh=mesh,
        in_specs=(
            P(None, "kv"),
            P("kv", "row"),
            P(None, "kv", None),
            P(None, None, "row"),
            P(),
            P("kv", None, "row", None),
            P("kv", None, "row", None),
            P("row", "kv"),
            P("kv", None),
            P("kv", None),
            P("kv", None),
            P(),
            P(),
        ),
        out_specs=P("row", "kv"),
        check_vma=False,
    )
```

```python
import functools
import math

import jax
import jax.numpy as jnp
from jax import lax
from jax.experimental import pallas as pl
from jax.experimental.pallas import tpu as pltpu
from jax.sharding import PartitionSpec as P

ADAPTER_SCALE = 0.5
ROPE_BASE = 1000000.0
EPSILON = 1e-06
NEG_FILL = -1e30
LANES = 128
COLUMN_TILE = 256
PAIR = 2
GROUP = 4
TASKS = 8
CHUNK = GROUP * TASKS
PHASES = 16
AHEAD = 6
DEPTH = 256
LOG2E = math.log2(math.e)
MIB = 1024 * 1024


def params(mib):
    return pltpu.CompilerParams(vmem_limit_bytes=mib * MIB)


def vmem_spec():
    return pl.BlockSpec(memory_space=pltpu.VMEM)


def in_hbm(*arrays):
    return [pltpu.with_memory_space_constraint(x, pltpu.HBM) for x in arrays]


def hbm_spec():
    return pl.BlockSpec(memory_space=pltpu.HBM)


def split2(x):
    high = x.astype(jnp.bfloat16)
    return high, (x - high.astype(jnp.float32)).astype(jnp.bfloat16)


def split3(x):
    high = x.astype(jnp.bfloat16).astype(jnp.float32)
    rest = x - high
    middle = rest.astype(jnp.bfloat16).astype(jnp.float32)
    return high, middle, (rest - middle).astype(jnp.bfloat16).astype(jnp.float32)


def to_column(row, count):
    shape = (count, count)
    eye = lax.broadcasted_iota(jnp.int32, shape, 0) == lax.broadcasted_iota(jnp.int32, shape, 1)
    return jnp.sum(jnp.where(eye, row.astype(jnp.float32), 0.0), axis=1, keepdims=True)


def project_kernel(
    rank,
    tenant_ref,
    adapter_ref,
    holder_ref,
    block_ref,
    length_ref,
    hidden_hbm,
    weight_hbm,
    down_hbm,
    up_hbm,
    keep_ref,
    send_ref,
    hidden_ref,
    weight_ref,
    down_ref,
    up_ref,
    total_ref,
    sems,
):
    chips, own, _ = keep_ref.shape
    rows, depth = hidden_ref.shape
    low_width = down_ref.shape[0]
    width = weight_ref.shape[1]
    tiles = width // COLUMN_TILE

    def start(copies):
        for copy in copies:
            copy.start()
        return copies

    def chunks(hbm, ref, offset):
        spans = [slice(i, min(i + DEPTH, ref.shape[0])) for i in range(0, ref.shape[0], DEPTH)]
        return [
            (span, pltpu.make_async_copy(hbm.at[span], ref.at[span], sems.at[offset + i]))
            for i, span in enumerate(spans)
        ]

    first = start(
        [
            pltpu.make_async_copy(hidden_hbm, hidden_ref, sems.at[0]),
            pltpu.make_async_copy(down_hbm, down_ref, sems.at[1]),
        ]
    )
    up_chunks = chunks(up_hbm, up_ref, 2)
    weight_chunks = chunks(weight_hbm, weight_ref, 2 + len(up_chunks))
    waiting = [copy for _, copy in up_chunks + weight_chunks]
    start(waiting[:1])

    slots = holder_ref.shape[1]
    numbers = [holder_ref[...], block_ref[...], length_ref[...], jnp.zeros((own, LANES - 3 * slots), jnp.int32)]
    numbers = jnp.concatenate(numbers, axis=1).astype(jnp.float32)
    for c in range(chips):
        keep_ref[c, :, width:] = numbers
        send_ref[c, :, width:] = numbers
    tenants = adapter_ref.shape[1]
    tenant = to_column(tenant_ref[...], rows)
    pick = lax.broadcasted_iota(jnp.int32, (rows, tenants), 1).astype(jnp.float32) == tenant
    adapter = jnp.sum(jnp.where(pick, adapter_ref[...].astype(jnp.float32), 0.0), axis=1, keepdims=True).astype(
        jnp.int32
    )
    for copy in first:
        copy.wait()
    start(waiting[1:3])
    hidden = hidden_ref[...]
    low = lax.dot_general(hidden, down_ref[...], (((1,), (1,)), ((), ())), preferred_element_type=jnp.float32)
    column = lax.broadcasted_iota(jnp.int32, (rows, low_width), 1)
    match = (column >= adapter * rank) & (column < adapter * rank + rank)
    high, low = split2(jnp.where(match, ADAPTER_SCALE * low, 0.0))
    both = jnp.concatenate([high, low], axis=0)
    columns = [slice(i * COLUMN_TILE, (i + 1) * COLUMN_TILE) for i in range(tiles)]
    for i, (span, copy) in enumerate(up_chunks):
        copy.wait()
        start(waiting[i + 3 : i + 4])
        for tile in columns:
            up_high, up_low = split2(up_ref[span, tile])
            twice = jnp.dot(both[:, span], up_high, preferred_element_type=jnp.float32)
            total = jnp.dot(high[:, span], up_low, preferred_element_type=jnp.float32)
            total = (total + twice[rows:]) + twice[:rows]
            total_ref[:, tile] = total if i == 0 else total_ref[:, tile] + total
    even = lax.axis_index("kv") % PAIR == 0
    for i, (span, copy) in enumerate(weight_chunks):
        copy.wait()
        start(waiting[i + len(up_chunks) + 3 : i + len(up_chunks) + 4])
        for tile in columns:
            total = total_ref[:, tile] + jnp.dot(
                hidden[:, span], weight_ref[span, tile], preferred_element_type=jnp.float32
            )
            if i < len(weight_chunks) - 1:
                total_ref[:, tile] = total
            else:
                total = total.reshape(chips, PAIR, own, COLUMN_TILE)
                keep_ref[:, :, tile] = jnp.where(even, total[:, 0], total[:, 1])
                send_ref[:, :, tile] = jnp.where(even, total[:, 1], total[:, 0])


def project(tenant, tenant_adapter, holder, block, length, hidden, query_weight, down, up, rank, chips):
    rows, depth = hidden.shape
    width = query_weight.shape[1]
    out = jax.ShapeDtypeStruct((chips, rows // chips // PAIR, width + LANES), jnp.float32)
    operands = in_hbm(tenant, tenant_adapter, holder, block, length, hidden, query_weight, down, up)
    large = operands[5:]
    return pl.pallas_call(
        functools.partial(project_kernel, rank),
        in_specs=[vmem_spec()] * 5 + [hbm_spec()] * 4,
        out_specs=[vmem_spec()] * 2,
        out_shape=[out] * 2,
        scratch_shapes=[pltpu.VMEM(x.shape, x.dtype) for x in large]
        + [
            pltpu.VMEM((rows, width), jnp.float32),
            pltpu.SemaphoreType.DMA((2 + pl.cdiv(depth, DEPTH) + pl.cdiv(down.shape[0], DEPTH),)),
        ],
        compiler_params=params(24),
        name="project",
    )(*operands)


def pair_kernel(keep_ref, got_ref, *out_refs):
    width = keep_ref.shape[2] - LANES
    chip = lax.axis_index("kv") // PAIR
    for s, ref in enumerate(out_refs):
        c = jnp.bitwise_xor(chip, s)
        ref[:, :width] = keep_ref[c, :, :width] + got_ref[c, :, :width]
        ref[:, width : width + LANES] = keep_ref[0, :, width:]
        ref[:, width + LANES :] = got_ref[0, :, width:]


def add_pair(keep, got):
    chips, own, width = keep.shape
    return pl.pallas_call(
        pair_kernel,
        in_specs=[vmem_spec()] * 2,
        out_specs=[vmem_spec()] * chips,
        out_shape=[jax.ShapeDtypeStruct((own, width + LANES), jnp.float32)] * chips,
        compiler_params=params(16),
        name="add_pair",
    )(keep, got)


def queries_kernel(*refs):
    parts, (cosine_ref, sine_ref, gain_ref, out_ref, turned_ref) = refs[:-5], refs[-5:]
    heads = turned_ref.shape[1]
    cosine, sine, gain = cosine_ref[...], sine_ref[...], gain_ref[...]
    for h in range(heads):
        columns = slice(h * LANES, (h + 1) * LANES)
        query = parts[0][:, columns]
        for part in parts[1:]:
            query = query + part[:, columns]
        square = jnp.mean(query * query, axis=-1, keepdims=True)
        query = query * lax.rsqrt(square + EPSILON) * gain
        turned_ref[:, h, :] = query * cosine + pltpu.roll(query, LANES // 2, 1) * sine
    out_ref[...] = turned_ref[...].astype(jnp.bfloat16)


def make_queries(parts, cosine, sine, gain, heads):
    own = parts[0].shape[0]
    shape = (own, heads, LANES)
    return pl.pallas_call(
        queries_kernel,
        in_specs=[vmem_spec()] * (len(parts) + 3),
        out_specs=vmem_spec(),
        out_shape=jax.ShapeDtypeStruct(shape, jnp.bfloat16),
        scratch_shapes=[pltpu.VMEM(shape, jnp.float32)],
        compiler_params=params(16),
        name="queries",
    )(*parts, cosine, sine, gain)


def list_kernel(blocks, block_size, slots, *refs):
    pieces, (list_ref, bound_ref, place_ref, value_ref) = refs[:-4], refs[-4:]
    rows = place_ref.shape[0]
    capacity = list_ref.shape[1]
    me = lax.axis_index("kv").astype(jnp.float32)
    numbers = jnp.concatenate([p[:, i * LANES : (i + 1) * LANES] for p in pieces for i in range(PAIR)], axis=0)
    holder, block, length = (numbers[:, i * slots : (i + 1) * slots] for i in range(3))
    row = lax.broadcasted_iota(jnp.int32, (rows, slots), 0).astype(jnp.float32)
    spare = float(rows * blocks * block_size)
    value_ref[...] = (row * blocks + block) * block_size + (length - 1.0) - spare
    mine = holder == me
    key = jnp.where(mine, block, -1.0)

    def before(count, axis):
        first = lax.broadcasted_iota(jnp.int32, (count, count), axis)
        return jnp.where(first < lax.broadcasted_iota(jnp.int32, (count, count), 1 - axis), 1.0, 0.0).astype(
            jnp.bfloat16
        )

    lane = lax.broadcasted_iota(jnp.int32, (rows, blocks), 1).astype(jnp.float32)
    picks = [jnp.where(key[:, j : j + 1] == lane, 1.0, 0.0) for j in range(slots)]
    count = jnp.sum(functools.reduce(jnp.add, picks), axis=0, keepdims=True)
    tasks = jnp.floor((count + (GROUP - 1)) * (1.0 / GROUP))
    earlier = jnp.dot(
        jnp.broadcast_to(tasks, (8, blocks)).astype(jnp.bfloat16),
        before(blocks, 0),
        preferred_element_type=jnp.float32,
    )[:1]
    base = earlier * GROUP
    row_before = before(rows, 1)
    slot = lax.broadcasted_iota(jnp.int32, (rows, slots), 1)
    place = jnp.full((rows, slots), -1.0, jnp.float32)
    for j in range(slots):
        above = jnp.dot(row_before, picks[j].astype(jnp.bfloat16), preferred_element_type=jnp.float32)
        here = jnp.sum(picks[j] * (above + base), axis=1, keepdims=True)
        place = jnp.where((slot == j) & mine, here, place)
        base = base + jnp.sum(picks[j], axis=0, keepdims=True)
    place_ref[...] = place
    size = blocks // PHASES
    end = earlier + tasks
    block_lane = lax.broadcasted_iota(jnp.int32, (1, blocks), 1)
    bound_lane = lax.broadcasted_iota(jnp.int32, (1, LANES), 1)
    bounds = jnp.zeros((1, LANES), jnp.float32)
    for part in range(PHASES):
        done = jnp.sum(jnp.where(block_lane == (part + 1) * size - 1, end, 0.0), axis=1, keepdims=True)
        done = done * (1.0 / TASKS)
        done = jnp.ceil(done) if part == PHASES - 1 else jnp.floor(done)
        bounds = jnp.where(bound_lane == part + 1, done, bounds)
    bound_ref[...] = bounds.astype(jnp.int32)
    target = lax.broadcasted_iota(jnp.int32, (8, capacity), 1).astype(jnp.float32)

    def tile(t, total):
        here = pl.ds(pl.multiple_of(t * 8, 8), 8)
        places, values = place_ref[here, :], value_ref[here, :]
        for j in range(slots):
            total = total + jnp.where(places[:, j : j + 1] == target, values[:, j : j + 1], 0.0)
        return total

    total = lax.fori_loop(0, rows // 8, tile, jnp.zeros((8, capacity), jnp.float32))
    list_ref[...] = (jnp.sum(total, axis=0, keepdims=True) + spare).astype(jnp.int32)


def make_list(parts, slots, blocks, block_size, count):
    own, width = parts[0].shape
    rows = count * own
    most = 2 * own * slots // count * count + (GROUP - 1) * blocks + 3 * CHUNK
    capacity = -(-most // LANES) * LANES
    last = width // (PAIR * LANES) - 1
    return pl.pallas_call(
        functools.partial(list_kernel, blocks, block_size, slots),
        grid=(1,),
        in_specs=[pl.BlockSpec((own, PAIR * LANES), lambda i: (0, last))] * len(parts),
        out_specs=[
            pl.BlockSpec((1, capacity), lambda i: (0, 0)),
            pl.BlockSpec((1, LANES), lambda i: (0, 0)),
        ],
        out_shape=[
            jax.ShapeDtypeStruct((1, capacity), jnp.int32),
            jax.ShapeDtypeStruct((1, LANES), jnp.int32),
        ],
        scratch_shapes=[pltpu.VMEM((rows, slots), jnp.float32), pltpu.VMEM((rows, slots), jnp.float32)],
        compiler_params=params(16),
        cost_estimate=pl.CostEstimate(flops=10**8, bytes_accessed=10**7, transcendentals=0),
        name="slot_list",
    )(*parts)


def attend_kernel(scale, kv_local, count, list_vmem, bound_vmem, *refs):
    queries, refs = refs[: count // PAIR], refs[count // PAIR :]
    (key_hbm, value_hbm, keep_ref, send_ref, list_ref, bound_ref, query_ref, key_ref, value_ref) = refs[:9]
    (top_ref, total_ref, sum_ref, score_ref, part_top_ref, part_total_ref, part_sum_ref, number_sems, sems) = refs[9:]
    heads = query_ref.shape[1]
    rows = query_ref.shape[0] - 1
    own = rows // count
    blocks, tokens, _ = key_ref.shape
    block_size = tokens // kv_local
    size = blocks // PHASES
    length_bits = (block_size - 1).bit_length()
    block_bits = (blocks - 1).bit_length()
    copies = []
    for part in range(PHASES):
        here = pl.ds(part * size, size)
        copies.append(
            (
                pltpu.make_async_copy(key_hbm.at[here], key_ref.at[here], sems.at[0, part]),
                pltpu.make_async_copy(value_hbm.at[here], value_ref.at[here], sems.at[1, part]),
            )
        )
    numbers = (
        pltpu.make_async_copy(list_vmem, list_ref, number_sems.at[0]),
        pltpu.make_async_copy(bound_vmem, bound_ref, number_sems.at[1]),
    )
    for pair in (copies[0], numbers, *copies[1:AHEAD]):
        for copy in pair:
            copy.start()

    factor = scale * LOG2E
    for s, piece in enumerate(queries):
        for t in range(PAIR):
            start = (PAIR * s + t) * own
            query_ref[start : start + own] = piece[t]
    query_ref[rows] = jnp.zeros((heads, LANES), jnp.bfloat16)
    top_ref[...] = jnp.full(top_ref.shape, NEG_FILL, jnp.float32)
    for ref in (total_ref, sum_ref, score_ref, part_top_ref, part_total_ref, part_sum_ref):
        ref[...] = jnp.zeros(ref.shape, jnp.float32)
    group = heads // kv_local
    column = lax.broadcasted_iota(jnp.int32, (group, tokens), 1)
    first = column % kv_local == 0
    wide = (heads, LANES)
    narrow = (group, LANES)

    def entries(chunk):
        return [list_ref[0, chunk * CHUNK + j] for j in range(CHUNK)]

    def row_of(entry):
        return entry >> (length_bits + block_bits)

    def block_of(entry):
        return (entry >> length_bits) & (blocks - 1)

    def merge_item(row, t, k):
        j = t * GROUP + k
        top, part_top = top_ref[row], part_top_ref[j]
        top_ref[row] = jnp.maximum(top, part_top)
        share = jnp.exp2(-jnp.abs(top - part_top) * factor)
        lower = top < part_top
        old, new = jnp.where(lower, share, 1.0), jnp.where(lower, 1.0, share)
        total_ref[row] = total_ref[row] * old + part_total_ref[j] * new
        sum_ref[row] = sum_ref[row] * old + part_sum_ref[t, k * heads : (k + 1) * heads] * new

    def weigh_item(entry, t, k):
        j = t * GROUP + k
        start = k * heads
        scores = jnp.where(
            first, score_ref[t, start : start + group], score_ref[t, start + group : start + heads]
        )
        length = (entry & (block_size - 1)) + 1
        scores = jnp.where(column < length * kv_local, scores, NEG_FILL)
        tops = [
            jnp.max(x, axis=1, keepdims=True)
            for x in (jnp.where(first, scores, NEG_FILL), jnp.where(first, NEG_FILL, scores))
        ]
        weights = jnp.exp2((scores - jnp.where(first, tops[0], tops[1])) * factor)
        weights = (jnp.where(first, weights, 0.0), jnp.where(first, 0.0, weights))
        for a in range(kv_local):
            here = slice(a * group, (a + 1) * group)
            part_top_ref[j, here] = jnp.broadcast_to(tops[a], narrow)
            part_total_ref[j, here] = jnp.broadcast_to(jnp.sum(weights[a], axis=1, keepdims=True), narrow)
        return jnp.concatenate(weights, axis=0).astype(jnp.bfloat16)

    def turn(stages, i, carry):
        merged, weighed, scored = (entries(jnp.maximum(i - back, 0)) for back in (2, 1, 0))
        for t in range(TASKS):
            task = slice(t * GROUP, (t + 1) * GROUP)
            for k, entry in enumerate(merged[task]):
                merge_item(jnp.where(i >= 2, row_of(entry), rows), t, k)
            if stages > 1:
                weights = [weigh_item(entry, t, k) for k, entry in enumerate(weighed[task])]
                part_sum_ref[t] = jnp.dot(
                    jnp.concatenate(weights, axis=0),
                    value_ref[block_of(weighed[task][0])],
                    preferred_element_type=jnp.float32,
                )
            if stages > 2:
                score_ref[t] = lax.dot_general(
                    jnp.concatenate([query_ref[row_of(entry)] for entry in scored[task]], axis=0),
                    key_ref[block_of(scored[task][0])],
                    (((1,), (1,)), ((), ())),
                    preferred_element_type=jnp.float32,
                )
        return carry

    for copy in numbers:
        copy.wait()
    for part in range(PHASES):
        for copy in copies[part]:
            copy.wait()
        for pair in copies[part + AHEAD : part + AHEAD + 1]:
            for copy in pair:
                copy.start()
        lax.fori_loop(bound_ref[0, part], bound_ref[0, part + 1], functools.partial(turn, 3), 0)
    last = bound_ref[0, PHASES]
    turn(2, last, 0)
    turn(1, last + 1, 0)

    square = (own * heads, LANES)
    eye = lax.broadcasted_iota(jnp.int32, square, 0) == lax.broadcasted_iota(jnp.int32, square, 1)
    line = lax.broadcasted_iota(jnp.int32, wide, 0)
    for q in range(count):
        ref = (keep_ref, send_ref)[q % PAIR]
        mine = slice(q * own, (q + 1) * own)
        top, total = (
            jnp.sum(jnp.where(eye, state[mine].reshape(square), 0.0), axis=0, keepdims=True)
            for state in (top_ref, total_ref)
        )
        ref[q // PAIR, :own] = sum_ref[mine]
        ref[q // PAIR, own] = jnp.where(line == 0, top, jnp.where(line == 1, total, 0.0))


def attend(items, bounds, queries, keys, values, kv_local, scale):
    _, own, heads, _ = queries[0].shape
    count = len(queries) * PAIR
    rows = count * own
    tokens = keys.shape[1]
    keys, values = in_hbm(keys, values)
    state = pltpu.VMEM((rows + 1, heads, LANES), jnp.float32)
    part = pltpu.VMEM((CHUNK, heads, LANES), jnp.float32)
    return pl.pallas_call(
        functools.partial(attend_kernel, scale, kv_local, count),
        in_specs=[vmem_spec()] * (2 + len(queries)) + [hbm_spec()] * 2,
        out_specs=[vmem_spec()] * PAIR,
        out_shape=[jax.ShapeDtypeStruct((count // PAIR, own + 1, heads, LANES), jnp.float32)] * PAIR,
        scratch_shapes=[
            pltpu.SMEM(items.shape, items.dtype),
            pltpu.SMEM(bounds.shape, bounds.dtype),
            pltpu.VMEM((rows + 1, heads, LANES), jnp.bfloat16),
            pltpu.VMEM(keys.shape, keys.dtype),
            pltpu.VMEM(values.shape, values.dtype),
            state,
            state,
            state,
            pltpu.VMEM((TASKS, GROUP * heads, tokens), jnp.float32),
            part,
            part,
            pltpu.VMEM((TASKS, GROUP * heads, LANES), jnp.float32),
            pltpu.SemaphoreType.DMA((2,)),
            pltpu.SemaphoreType.DMA((2, PHASES)),
        ],
        compiler_params=params(40),
        name="attend",
    )(items, bounds, *queries, keys, values)


def merge_pair_kernel(scale, keep_ref, got_ref, out_ref):
    chips, sections, heads, _ = keep_ref.shape
    own = sections - 1
    factor = scale * LOG2E
    line = lax.broadcasted_iota(jnp.int32, (heads, LANES), 0)
    shares, stats = [], []
    for s in range(chips):
        keep, got = keep_ref[s, own], got_ref[s, own]
        high = jnp.maximum(keep[0:1], got[0:1])
        pair = [jnp.exp2((x[0:1] - high) * factor) for x in (keep, got)]
        shares += pair
        total = pair[0] * keep[1:2] + pair[1] * got[1:2]
        stat = jnp.zeros((heads, LANES), jnp.float32)
        for position, piece in enumerate(split3(high) + split3(total)):
            stat = jnp.where(line == position, piece, stat)
        stats.append(stat)
    columns = jnp.concatenate(shares, axis=0).T
    flat = (own * heads, LANES)
    for s in range(chips):
        total = keep_ref[s, :own].reshape(flat) * columns[:, PAIR * s : PAIR * s + 1]
        total = total + got_ref[s, :own].reshape(flat) * columns[:, PAIR * s + 1 : PAIR * s + 2]
        out_ref[s, :own] = total.astype(jnp.bfloat16).reshape(own, heads, LANES)
        out_ref[s, own] = stats[s].astype(jnp.bfloat16)


def merge_pair(keep, got, scale):
    return pl.pallas_call(
        functools.partial(merge_pair_kernel, scale),
        in_specs=[vmem_spec()] * 2,
        out_specs=vmem_spec(),
        out_shape=jax.ShapeDtypeStruct(keep.shape, jnp.bfloat16),
        compiler_params=params(16),
        name="merge_pair",
    )(keep, got)


def merge_kernel(scale, *refs):
    pieces, (out_ref, wide_ref) = refs[:-2], refs[-2:]
    chips, sections, heads, _ = pieces[0].shape
    own = sections - 1
    factor = scale * LOG2E
    shares = []
    for s in range(chips):
        stats = [pieces[j][s ^ j, own].astype(jnp.float32) for j in range(chips)]
        tops = jnp.concatenate([x[0:1] + x[1:2] + x[2:3] for x in stats], axis=0)
        totals = jnp.concatenate([x[3:4] + x[4:5] + x[5:6] for x in stats], axis=0)
        weights = jnp.exp2((tops - jnp.max(tops, axis=0, keepdims=True)) * factor)
        shares.append(weights / jnp.sum(weights * totals, axis=0, keepdims=True))
    columns = jnp.concatenate(shares, axis=0).T
    flat = own * heads
    for s in range(chips):
        total = jnp.zeros((flat, LANES), jnp.float32)
        for j in range(chips):
            part = pieces[j][s ^ j, :own].astype(jnp.float32).reshape(flat, LANES)
            total = total + part * columns[:, s * chips + j : s * chips + j + 1]
        wide_ref[s * flat : (s + 1) * flat, :] = total
    rows = [wide_ref[pl.ds(h, chips * own, stride=heads), :] for h in range(heads)]
    out_ref[...] = jnp.concatenate(rows, axis=1).astype(jnp.bfloat16)


def merge(pieces, scale):
    chips, sections, heads, _ = pieces[0].shape
    own = sections - 1
    return pl.pallas_call(
        functools.partial(merge_kernel, scale),
        in_specs=[vmem_spec()] * chips,
        out_specs=vmem_spec(),
        out_shape=jax.ShapeDtypeStruct((chips * own, heads * LANES), jnp.bfloat16),
        scratch_shapes=[pltpu.VMEM((chips * own * heads, LANES), jnp.float32)],
        compiler_params=params(32),
        name="merge",
    )(*pieces)


def output_kernel(own, *refs):
    pieces, weight_ref = refs[:PAIR], refs[PAIR]
    outs, (rows_ref, terms_ref) = refs[PAIR + 1 : -2], refs[-2:]
    me = lax.axis_index("kv")
    for t in range(PAIR):
        piece = pieces[t][...].astype(jnp.float32)
        for s in range(piece.shape[0] // own):
            start = pl.multiple_of(jnp.bitwise_xor(me, PAIR * s + t) * own, own)
            rows_ref[pl.ds(start, own), :] = piece[s * own : (s + 1) * own]
    terms_ref[...] = jnp.dot(
        rows_ref[...].astype(jnp.bfloat16), weight_ref[...], preferred_element_type=jnp.float32
    )
    me = lax.axis_index("row")
    part = outs[0].shape[0]
    for s, ref in enumerate(outs):
        start = pl.multiple_of(jnp.bitwise_xor(me, s) * part, part)
        ref[...] = terms_ref[pl.ds(start, part), :].astype(ref.dtype)


def project_out(pieces, weight, own, row_count):
    half, width = pieces[0].shape
    rows, columns = PAIR * half, weight.shape[1]
    shape = (rows // row_count, columns)
    send = jax.ShapeDtypeStruct(shape, jnp.bfloat16)
    return pl.pallas_call(
        functools.partial(output_kernel, own),
        in_specs=[vmem_spec()] * (PAIR + 1),
        out_specs=[vmem_spec()] * row_count,
        out_shape=[jax.ShapeDtypeStruct(shape, jnp.float32)] + [send] * (row_count - 1),
        scratch_shapes=[pltpu.VMEM((rows, width), jnp.float32), pltpu.VMEM((rows, columns), jnp.float32)],
        compiler_params=params(24),
        name="project_out",
    )(*pieces, weight)


def exchange(x, axis, s):
    count = lax.axis_size(axis)
    return lax.ppermute(x, axis, [(i, i ^ s) for i in range(count)])


def gather_chips(x):
    return [x] + [exchange(x, "kv", s) for s in range(PAIR, lax.axis_size("kv"), PAIR)]


def gather_pairs(x):
    return gather_chips(jnp.concatenate([x, exchange(x, "kv", 1)], axis=0))


def local(
    hidden,
    query_weight,
    adapter_down_weight,
    adapter_up_weight,
    query_norm_gain,
    paged_key_cache,
    paged_value_cache,
    output_weight,
    holder,
    holder_block_index,
    block_used_length,
    tenant,
    tenant_adapter,
):
    own, slots = holder.shape
    rows, depth = hidden.shape
    kv_count = lax.axis_size("kv")
    row_count = lax.axis_size("row")
    adapters, _, rank = adapter_down_weight.shape
    width = query_weight.shape[1]
    head_size = query_norm_gain.shape[0]
    heads = width // head_size
    blocks, block_size, kv_local, _ = paged_key_cache.shape
    scale = 1.0 / math.sqrt(head_size)

    chips = kv_count // PAIR
    keep, send = project(
        tenant.reshape(1, rows),
        tenant_adapter.reshape(1, -1),
        holder,
        holder_block_index,
        block_used_length,
        hidden,
        query_weight,
        jnp.swapaxes(adapter_down_weight, 1, 2).reshape(adapters * rank, depth),
        adapter_up_weight.reshape(adapters * rank, width),
        rank,
        chips,
    )
    parts = add_pair(keep, exchange(send, "kv", 1))
    parts = [parts[0]] + [exchange(parts[s], "kv", PAIR * s) for s in range(1, chips)]

    position = (jnp.sum(block_used_length, axis=1) - 1).astype(jnp.float32)
    half = head_size // 2
    frequency = ROPE_BASE ** (-(jnp.arange(half, dtype=jnp.float32) * 2.0) / head_size)
    angles = position[:, None] * frequency[None, :]
    cosine = jnp.concatenate([jnp.cos(angles), jnp.cos(angles)], axis=-1)
    sine = jnp.concatenate([-jnp.sin(angles), jnp.sin(angles)], axis=-1)
    queries = make_queries(parts, cosine, sine, query_norm_gain.reshape(1, head_size), heads)
    queries = [q.reshape(PAIR, own, heads, head_size) for q in gather_pairs(queries)]
    items, bounds = make_list(parts, slots, blocks, block_size, kv_count)

    keys = paged_key_cache.reshape(blocks, block_size * kv_local, head_size)
    values = paged_value_cache.reshape(blocks, block_size * kv_local, head_size)
    keep, send = attend(items, bounds, queries, keys, values, kv_local, scale)
    merged = merge_pair(keep, exchange(send, "kv", 1), scale)
    attention = merge(gather_chips(merged), scale)
    terms = project_out([attention, exchange(attention, "kv", 1)], output_weight, own, row_count)
    total = terms[0]
    for s in range(1, row_count):
        total = total + exchange(terms[s], "row", s).astype(jnp.float32)
    return total.astype(jnp.bfloat16)


def solution(mesh):
    return jax.shard_map(
        local,
        mesh=mesh,
        in_specs=(
            P(None, "kv"),
            P("kv", "row"),
            P(None, "kv", None),
            P(None, None, "row"),
            P(),
            P("kv", None, "row", None),
            P("kv", None, "row", None),
            P("row", "kv"),
            P("kv", None),
            P("kv", None),
            P("kv", None),
            P(),
            P(),
        ),
        out_specs=P("row", "kv"),
        check_vma=False,
    )
```

```python
import functools
import math

import jax
import jax.numpy as jnp
from jax import lax
from jax.experimental import pallas as pl
from jax.experimental.pallas import tpu as pltpu
from jax.sharding import PartitionSpec as P

ADAPTER_SCALE = 0.5
ROPE_BASE = 1000000.0
EPSILON = 1e-06
NEG_FILL = -1e30
LANES = 128
COLUMN_TILE = 256
PAIR = 2
GROUP = 4
TASKS = 8
CHUNK = GROUP * TASKS
PHASES = 8
AHEAD = 4
DEPTH = 256
LOG2E = math.log2(math.e)
MIB = 1024 * 1024


def params(mib):
    return pltpu.CompilerParams(vmem_limit_bytes=mib * MIB)


def vmem_spec():
    return pl.BlockSpec(memory_space=pltpu.VMEM)


def in_hbm(*arrays):
    return [pltpu.with_memory_space_constraint(x, pltpu.HBM) for x in arrays]


def hbm_spec():
    return pl.BlockSpec(memory_space=pltpu.HBM)


def split3(x):
    high = x.astype(jnp.bfloat16).astype(jnp.float32)
    rest = x - high
    middle = rest.astype(jnp.bfloat16).astype(jnp.float32)
    return high, middle, (rest - middle).astype(jnp.bfloat16).astype(jnp.float32)


def to_column(row, count):
    shape = (count, count)
    eye = lax.broadcasted_iota(jnp.int32, shape, 0) == lax.broadcasted_iota(jnp.int32, shape, 1)
    return jnp.sum(jnp.where(eye, row.astype(jnp.float32), 0.0), axis=1, keepdims=True)


def project_kernel(
    rank,
    tenant_ref,
    adapter_ref,
    holder_ref,
    block_ref,
    length_ref,
    hidden_hbm,
    weight_hbm,
    down_hbm,
    keep_ref,
    send_ref,
    hidden_ref,
    weight_ref,
    down_ref,
    total_ref,
    sems,
):
    chips, own, _ = keep_ref.shape
    rows, depth = hidden_ref.shape
    width = weight_ref.shape[1]
    spans = [slice(i, min(i + DEPTH, depth)) for i in range(0, depth, DEPTH)]
    first = [
        pltpu.make_async_copy(hidden_hbm, hidden_ref, sems.at[0]),
        pltpu.make_async_copy(down_hbm, down_ref, sems.at[1]),
    ]
    chunks = [
        pltpu.make_async_copy(weight_hbm.at[span], weight_ref.at[span], sems.at[2 + i])
        for i, span in enumerate(spans)
    ]
    for copy in first + chunks:
        copy.start()

    slots = holder_ref.shape[1]
    numbers = [holder_ref[...], block_ref[...], length_ref[...], jnp.zeros((own, LANES - 3 * slots), jnp.int32)]
    numbers = jnp.concatenate(numbers, axis=1).astype(jnp.float32)
    tenants = adapter_ref.shape[1]
    tenant = to_column(tenant_ref[...], rows)
    pick = lax.broadcasted_iota(jnp.int32, (rows, tenants), 1).astype(jnp.float32) == tenant
    adapter = jnp.sum(jnp.where(pick, adapter_ref[...].astype(jnp.float32), 0.0), axis=1, keepdims=True).astype(
        jnp.int32
    )
    even = lax.axis_index("kv") % PAIR == 0

    def store(columns, total):
        total = total.reshape(chips, PAIR, own, total.shape[1])
        keep_ref[:, :, columns] = jnp.where(even, total[:, 0], total[:, 1])
        send_ref[:, :, columns] = jnp.where(even, total[:, 1], total[:, 0])

    for copy in first:
        copy.wait()
    hidden = hidden_ref[...]
    low = lax.dot_general(hidden, down_ref[...], (((1,), (1,)), ((), ())), preferred_element_type=jnp.float32)
    column = lax.broadcasted_iota(jnp.int32, low.shape, 1)
    low = jnp.where((column >= adapter * rank) & (column < adapter * rank + rank), low, 0.0)
    low = sum(low[:, i : i + LANES] for i in range(LANES, low.shape[1], LANES)) + low[:, :LANES]
    shift = LANES // 2
    while shift >= rank:
        low = low + pltpu.roll(low, shift, 1)
        shift //= 2
    lane = lax.broadcasted_iota(jnp.int32, (rows, LANES), 1)
    numbers = jnp.concatenate([numbers] * (rows // own), axis=0)
    store(slice(width, width + LANES), jnp.where(lane < 3 * slots, numbers, low))
    for i, (span, copy) in enumerate(zip(spans, chunks)):
        copy.wait()
        for start in range(0, width, COLUMN_TILE):
            tile = slice(start, start + COLUMN_TILE)
            total = jnp.dot(hidden[:, span], weight_ref[span, tile], preferred_element_type=jnp.float32)
            if i > 0:
                total = total_ref[:, tile] + total
            if i < len(chunks) - 1:
                total_ref[:, tile] = total
            else:
                store(tile, total)


def project(tenant, tenant_adapter, holder, block, length, hidden, query_weight, down, rank, chips):
    rows, depth = hidden.shape
    width = query_weight.shape[1]
    out = jax.ShapeDtypeStruct((chips, rows // chips // PAIR, width + LANES), jnp.float32)
    operands = in_hbm(tenant, tenant_adapter, holder, block, length, hidden, query_weight, down)
    large = operands[5:]
    return pl.pallas_call(
        functools.partial(project_kernel, rank),
        in_specs=[vmem_spec()] * 5 + [hbm_spec()] * 3,
        out_specs=[vmem_spec()] * 2,
        out_shape=[out] * 2,
        scratch_shapes=[pltpu.VMEM(x.shape, x.dtype) for x in large]
        + [pltpu.VMEM((rows, width), jnp.float32), pltpu.SemaphoreType.DMA((2 + pl.cdiv(depth, DEPTH),))],
        compiler_params=params(16),
        name="project",
    )(*operands)


def gather_up_kernel(tenant_ref, adapter_ref, up_hbm, out_ref, sems):
    own = out_ref.shape[0]
    me = lax.axis_index("kv")
    copies = [
        pltpu.make_async_copy(up_hbm.at[adapter_ref[tenant_ref[me * own + r]]], out_ref.at[r], sems.at[r])
        for r in range(own)
    ]
    for copy in copies:
        copy.start()
    for copy in copies:
        copy.wait()


def gather_up(tenant, tenant_adapter, up, own):
    (up,) = in_hbm(up)
    smem = pl.BlockSpec(memory_space=pltpu.SMEM)
    return pl.pallas_call(
        gather_up_kernel,
        in_specs=[smem, smem, hbm_spec()],
        out_specs=vmem_spec(),
        out_shape=jax.ShapeDtypeStruct((own, *up.shape[1:]), up.dtype),
        scratch_shapes=[pltpu.SemaphoreType.DMA((own,))],
        compiler_params=params(16),
        cost_estimate=pl.CostEstimate(flops=0, bytes_accessed=own * up.shape[1] * up.shape[2] * 4, transcendentals=0),
        name="gather_up",
    )(tenant, tenant_adapter, up)


def pair_kernel(number_lanes, keep_ref, got_ref, *out_refs):
    chips, own, width = keep_ref.shape
    width = width - LANES
    chip = lax.axis_index("kv") // PAIR
    lane = lax.broadcasted_iota(jnp.int32, (own, LANES), 1)
    for s, ref in enumerate(out_refs):
        c = jnp.bitwise_xor(chip, s)
        ref[:, :width] = keep_ref[c, :, :width] + got_ref[c, :, :width]
        keep = keep_ref[c, :, width:]
        ref[:, width : width + LANES] = jnp.where(lane < number_lanes, keep, keep + got_ref[c, :, width:])
        ref[:, width + LANES :] = got_ref[c, :, width:]


def add_pair(keep, got, number_lanes):
    chips, own, width = keep.shape
    return pl.pallas_call(
        functools.partial(pair_kernel, number_lanes),
        in_specs=[vmem_spec()] * 2,
        out_specs=[vmem_spec()] * chips,
        out_shape=[jax.ShapeDtypeStruct((own, width + LANES), jnp.float32)] * chips,
        compiler_params=params(16),
        name="add_pair",
    )(keep, got)


def queries_kernel(number_lanes, *refs):
    parts, (up_ref, cosine_ref, sine_ref, gain_ref, out_ref, turned_ref) = refs[:-6], refs[-6:]
    own, rank, width = up_ref.shape
    heads = turned_ref.shape[1]

    def whole(columns):
        total = parts[0][:, columns]
        for part in parts[1:]:
            total = total + part[:, columns]
        return total

    low = whole(slice(width, width + LANES)) * ADAPTER_SCALE
    line = lax.broadcasted_iota(jnp.int32, (rank, LANES), 0)
    lane = lax.broadcasted_iota(jnp.int32, (rank, LANES), 1)
    low = [
        jnp.sum(jnp.where(lane == line + number_lanes, low[r : r + 1], 0.0), axis=1, keepdims=True)
        for r in range(own)
    ]
    row = lax.broadcasted_iota(jnp.int32, (own, LANES), 0)
    cosine, sine, gain = cosine_ref[...], sine_ref[...], gain_ref[...]
    for h in range(heads):
        columns = slice(h * LANES, (h + 1) * LANES)
        query = whole(columns)
        adapted = jnp.zeros((own, LANES), jnp.float32)
        for r in range(own):
            adapted = jnp.where(row == r, jnp.sum(up_ref[r, :, columns] * low[r], axis=0, keepdims=True), adapted)
        query = query + adapted
        square = jnp.mean(query * query, axis=-1, keepdims=True)
        query = query * lax.rsqrt(square + EPSILON) * gain
        turned_ref[:, h, :] = query * cosine + pltpu.roll(query, LANES // 2, 1) * sine
    out_ref[...] = turned_ref[...].astype(jnp.bfloat16)


def make_queries(parts, up, cosine, sine, gain, heads, number_lanes):
    own = parts[0].shape[0]
    shape = (own, heads, LANES)
    return pl.pallas_call(
        functools.partial(queries_kernel, number_lanes),
        in_specs=[vmem_spec()] * (len(parts) + 4),
        out_specs=vmem_spec(),
        out_shape=jax.ShapeDtypeStruct(shape, jnp.bfloat16),
        scratch_shapes=[pltpu.VMEM(shape, jnp.float32)],
        compiler_params=params(16),
        name="queries",
    )(*parts, up, cosine, sine, gain)


def list_kernel(blocks, block_size, slots, *refs):
    pieces, (list_ref, bound_ref, place_ref, value_ref) = refs[:-4], refs[-4:]
    rows = place_ref.shape[0]
    capacity = list_ref.shape[1]
    me = lax.axis_index("kv").astype(jnp.float32)
    numbers = jnp.concatenate([p[:, i * LANES : (i + 1) * LANES] for p in pieces for i in range(PAIR)], axis=0)
    holder, block, length = (numbers[:, i * slots : (i + 1) * slots] for i in range(3))
    row = lax.broadcasted_iota(jnp.int32, (rows, slots), 0).astype(jnp.float32)
    spare = float(rows * blocks * block_size)
    value_ref[...] = (row * blocks + block) * block_size + (length - 1.0) - spare
    mine = holder == me
    key = jnp.where(mine, block, -1.0)

    def before(count, axis):
        first = lax.broadcasted_iota(jnp.int32, (count, count), axis)
        return jnp.where(first < lax.broadcasted_iota(jnp.int32, (count, count), 1 - axis), 1.0, 0.0).astype(
            jnp.bfloat16
        )

    lane = lax.broadcasted_iota(jnp.int32, (rows, blocks), 1).astype(jnp.float32)
    picks = [jnp.where(key[:, j : j + 1] == lane, 1.0, 0.0) for j in range(slots)]
    count = jnp.sum(functools.reduce(jnp.add, picks), axis=0, keepdims=True)
    tasks = jnp.floor((count + (GROUP - 1)) * (1.0 / GROUP))
    earlier = jnp.dot(
        jnp.broadcast_to(tasks, (8, blocks)).astype(jnp.bfloat16),
        before(blocks, 0),
        preferred_element_type=jnp.float32,
    )[:1]
    base = earlier * GROUP
    row_before = before(rows, 1)
    slot = lax.broadcasted_iota(jnp.int32, (rows, slots), 1)
    place = jnp.full((rows, slots), -1.0, jnp.float32)
    for j in range(slots):
        above = jnp.dot(row_before, picks[j].astype(jnp.bfloat16), preferred_element_type=jnp.float32)
        here = jnp.sum(picks[j] * (above + base), axis=1, keepdims=True)
        place = jnp.where((slot == j) & mine, here, place)
        base = base + jnp.sum(picks[j], axis=0, keepdims=True)
    place_ref[...] = place
    size = blocks // PHASES
    end = earlier + tasks
    block_lane = lax.broadcasted_iota(jnp.int32, (1, blocks), 1)
    bound_lane = lax.broadcasted_iota(jnp.int32, (1, LANES), 1)
    bounds = jnp.zeros((1, LANES), jnp.float32)
    for part in range(PHASES):
        done = jnp.sum(jnp.where(block_lane == (part + 1) * size - 1, end, 0.0), axis=1, keepdims=True)
        done = done * (1.0 / TASKS)
        done = jnp.ceil(done) if part == PHASES - 1 else jnp.floor(done)
        bounds = jnp.where(bound_lane == part + 1, done, bounds)
    bound_ref[...] = bounds.astype(jnp.int32)
    target = lax.broadcasted_iota(jnp.int32, (8, capacity), 1).astype(jnp.float32)

    def tile(t, total):
        here = pl.ds(pl.multiple_of(t * 8, 8), 8)
        places, values = place_ref[here, :], value_ref[here, :]
        for j in range(slots):
            total = total + jnp.where(places[:, j : j + 1] == target, values[:, j : j + 1], 0.0)
        return total

    total = lax.fori_loop(0, rows // 8, tile, jnp.zeros((8, capacity), jnp.float32))
    list_ref[...] = (jnp.sum(total, axis=0, keepdims=True) + spare).astype(jnp.int32)


def make_list(parts, slots, blocks, block_size, count):
    own, width = parts[0].shape
    rows = count * own
    most = 2 * own * slots // count * count + (GROUP - 1) * blocks + 3 * CHUNK
    capacity = -(-most // LANES) * LANES
    last = width // (PAIR * LANES) - 1
    return pl.pallas_call(
        functools.partial(list_kernel, blocks, block_size, slots),
        grid=(1,),
        in_specs=[pl.BlockSpec((own, PAIR * LANES), lambda i: (0, last))] * len(parts),
        out_specs=[
            pl.BlockSpec((1, capacity), lambda i: (0, 0)),
            pl.BlockSpec((1, LANES), lambda i: (0, 0)),
        ],
        out_shape=[
            jax.ShapeDtypeStruct((1, capacity), jnp.int32),
            jax.ShapeDtypeStruct((1, LANES), jnp.int32),
        ],
        scratch_shapes=[pltpu.VMEM((rows, slots), jnp.float32), pltpu.VMEM((rows, slots), jnp.float32)],
        compiler_params=params(16),
        cost_estimate=pl.CostEstimate(flops=10**8, bytes_accessed=10**7, transcendentals=0),
        name="slot_list",
    )(*parts)


def attend_kernel(scale, kv_local, count, list_vmem, bound_vmem, *refs):
    queries, refs = refs[: count // PAIR], refs[count // PAIR :]
    (key_ref, value_hbm, keep_ref, send_ref, list_ref, bound_ref, query_ref, value_ref) = refs[:8]
    (top_ref, total_ref, sum_ref, score_ref, part_top_ref, part_total_ref, part_sum_ref, number_sems, sems) = refs[8:]
    heads = query_ref.shape[1]
    rows = query_ref.shape[0] - 1
    own = rows // count
    blocks, tokens, _ = key_ref.shape
    block_size = tokens // kv_local
    length_bits = (block_size - 1).bit_length()
    block_bits = (blocks - 1).bit_length()
    numbers = (
        pltpu.make_async_copy(list_vmem, list_ref, number_sems.at[0]),
        pltpu.make_async_copy(bound_vmem, bound_ref, number_sems.at[1]),
    )
    size = blocks // PHASES
    spans = [pl.ds(part * size, size) for part in range(PHASES)]
    copies = [
        pltpu.make_async_copy(value_hbm.at[span], value_ref.at[span], sems.at[part]) for part, span in enumerate(spans)
    ]
    for copy in (copies[0], *numbers, *copies[1:AHEAD]):
        copy.start()

    factor = scale * LOG2E
    for s, piece in enumerate(queries):
        for t in range(PAIR):
            start = (PAIR * s + t) * own
            query_ref[start : start + own] = piece[t]
    query_ref[rows] = jnp.zeros((heads, LANES), jnp.bfloat16)
    top_ref[...] = jnp.full(top_ref.shape, NEG_FILL, jnp.float32)
    for ref in (total_ref, sum_ref, score_ref, part_top_ref, part_total_ref, part_sum_ref):
        ref[...] = jnp.zeros(ref.shape, jnp.float32)
    group = heads // kv_local
    column = lax.broadcasted_iota(jnp.int32, (group, tokens), 1)
    first = column % kv_local == 0
    wide = (heads, LANES)
    narrow = (group, LANES)

    def entries(chunk):
        return [list_ref[0, chunk * CHUNK + j] for j in range(CHUNK)]

    def row_of(entry):
        return entry >> (length_bits + block_bits)

    def block_of(entry):
        return (entry >> length_bits) & (blocks - 1)

    def merge_item(row, t, k):
        j = t * GROUP + k
        top, part_top = top_ref[row], part_top_ref[j]
        top_ref[row] = jnp.maximum(top, part_top)
        share = jnp.exp2(-jnp.abs(top - part_top) * factor)
        lower = top < part_top
        old, new = jnp.where(lower, share, 1.0), jnp.where(lower, 1.0, share)
        total_ref[row] = total_ref[row] * old + part_total_ref[j] * new
        sum_ref[row] = sum_ref[row] * old + part_sum_ref[t, k * heads : (k + 1) * heads] * new

    def weigh_item(entry, t, k):
        j = t * GROUP + k
        start = k * heads
        scores = jnp.where(
            first, score_ref[t, start : start + group], score_ref[t, start + group : start + heads]
        )
        length = (entry & (block_size - 1)) + 1
        scores = jnp.where(column < length * kv_local, scores, NEG_FILL)
        tops = [
            jnp.max(x, axis=1, keepdims=True)
            for x in (jnp.where(first, scores, NEG_FILL), jnp.where(first, NEG_FILL, scores))
        ]
        weights = jnp.exp2((scores - jnp.where(first, tops[0], tops[1])) * factor)
        weights = (jnp.where(first, weights, 0.0), jnp.where(first, 0.0, weights))
        for a in range(kv_local):
            here = slice(a * group, (a + 1) * group)
            part_top_ref[j, here] = jnp.broadcast_to(tops[a], narrow)
            part_total_ref[j, here] = jnp.broadcast_to(jnp.sum(weights[a], axis=1, keepdims=True), narrow)
        return jnp.concatenate(weights, axis=0).astype(jnp.bfloat16)

    def turn(stages, i, carry):
        merged, weighed, scored = (entries(jnp.maximum(i - back, 0)) for back in (2, 1, 0))
        for t in range(TASKS):
            task = slice(t * GROUP, (t + 1) * GROUP)
            for k, entry in enumerate(merged[task]):
                merge_item(jnp.where(i >= 2, row_of(entry), rows), t, k)
            if stages > 1:
                weights = [weigh_item(entry, t, k) for k, entry in enumerate(weighed[task])]
                part_sum_ref[t] = jnp.dot(
                    jnp.concatenate(weights, axis=0),
                    value_ref[block_of(weighed[task][0])],
                    preferred_element_type=jnp.float32,
                )
            if stages > 2:
                score_ref[t] = lax.dot_general(
                    jnp.concatenate([query_ref[row_of(entry)] for entry in scored[task]], axis=0),
                    key_ref[block_of(scored[task][0])],
                    (((1,), (1,)), ((), ())),
                    preferred_element_type=jnp.float32,
                )
        return carry

    for copy in numbers:
        copy.wait()
    for part in range(PHASES):
        copies[part].wait()
        for copy in copies[part + AHEAD : part + AHEAD + 1]:
            copy.start()
        lax.fori_loop(bound_ref[0, part], bound_ref[0, part + 1], functools.partial(turn, 3), 0)
    last = bound_ref[0, PHASES]
    turn(2, last, 0)
    turn(1, last + 1, 0)

    square = (own * heads, LANES)
    eye = lax.broadcasted_iota(jnp.int32, square, 0) == lax.broadcasted_iota(jnp.int32, square, 1)
    line = lax.broadcasted_iota(jnp.int32, wide, 0)
    for q in range(count):
        ref = (keep_ref, send_ref)[q % PAIR]
        mine = slice(q * own, (q + 1) * own)
        top, total = (
            jnp.sum(jnp.where(eye, state[mine].reshape(square), 0.0), axis=0, keepdims=True)
            for state in (top_ref, total_ref)
        )
        ref[q // PAIR, :own] = sum_ref[mine]
        ref[q // PAIR, own] = jnp.where(line == 0, top, jnp.where(line == 1, total, 0.0))


def attend(items, bounds, queries, keys, values, kv_local, scale):
    _, own, heads, _ = queries[0].shape
    count = len(queries) * PAIR
    rows = count * own
    tokens = keys.shape[1]
    keys = pltpu.with_memory_space_constraint(keys, pltpu.VMEM)
    (values,) = in_hbm(values)
    state = pltpu.VMEM((rows + 1, heads, LANES), jnp.float32)
    part = pltpu.VMEM((CHUNK, heads, LANES), jnp.float32)
    return pl.pallas_call(
        functools.partial(attend_kernel, scale, kv_local, count),
        in_specs=[vmem_spec()] * (3 + len(queries)) + [hbm_spec()],
        out_specs=[vmem_spec()] * PAIR,
        out_shape=[jax.ShapeDtypeStruct((count // PAIR, own + 1, heads, LANES), jnp.float32)] * PAIR,
        scratch_shapes=[
            pltpu.SMEM(items.shape, items.dtype),
            pltpu.SMEM(bounds.shape, bounds.dtype),
            pltpu.VMEM((rows + 1, heads, LANES), jnp.bfloat16),
            pltpu.VMEM(values.shape, values.dtype),
            state,
            state,
            state,
            pltpu.VMEM((TASKS, GROUP * heads, tokens), jnp.float32),
            part,
            part,
            pltpu.VMEM((TASKS, GROUP * heads, LANES), jnp.float32),
            pltpu.SemaphoreType.DMA((2,)),
            pltpu.SemaphoreType.DMA((PHASES,)),
        ],
        compiler_params=params(32),
        name="attend",
    )(items, bounds, *queries, keys, values)


def merge_pair_kernel(scale, keep_ref, got_ref, out_ref):
    chips, sections, heads, _ = keep_ref.shape
    own = sections - 1
    factor = scale * LOG2E
    line = lax.broadcasted_iota(jnp.int32, (heads, LANES), 0)
    shares, stats = [], []
    for s in range(chips):
        keep, got = keep_ref[s, own], got_ref[s, own]
        high = jnp.maximum(keep[0:1], got[0:1])
        pair = [jnp.exp2((x[0:1] - high) * factor) for x in (keep, got)]
        shares += pair
        total = pair[0] * keep[1:2] + pair[1] * got[1:2]
        stat = jnp.zeros((heads, LANES), jnp.float32)
        for position, piece in enumerate(split3(high) + split3(total)):
            stat = jnp.where(line == position, piece, stat)
        stats.append(stat)
    columns = jnp.concatenate(shares, axis=0).T
    flat = (own * heads, LANES)
    for s in range(chips):
        total = keep_ref[s, :own].reshape(flat) * columns[:, PAIR * s : PAIR * s + 1]
        total = total + got_ref[s, :own].reshape(flat) * columns[:, PAIR * s + 1 : PAIR * s + 2]
        out_ref[s, :own] = total.astype(jnp.bfloat16).reshape(own, heads, LANES)
        out_ref[s, own] = stats[s].astype(jnp.bfloat16)


def merge_pair(keep, got, scale):
    return pl.pallas_call(
        functools.partial(merge_pair_kernel, scale),
        in_specs=[vmem_spec()] * 2,
        out_specs=vmem_spec(),
        out_shape=jax.ShapeDtypeStruct(keep.shape, jnp.bfloat16),
        compiler_params=params(16),
        name="merge_pair",
    )(keep, got)


def merge_kernel(scale, *refs):
    pieces, (out_ref, wide_ref) = refs[:-2], refs[-2:]
    chips, sections, heads, _ = pieces[0].shape
    own = sections - 1
    factor = scale * LOG2E
    shares = []
    for s in range(chips):
        stats = [pieces[j][s ^ j, own].astype(jnp.float32) for j in range(chips)]
        tops = jnp.concatenate([x[0:1] + x[1:2] + x[2:3] for x in stats], axis=0)
        totals = jnp.concatenate([x[3:4] + x[4:5] + x[5:6] for x in stats], axis=0)
        weights = jnp.exp2((tops - jnp.max(tops, axis=0, keepdims=True)) * factor)
        shares.append(weights / jnp.sum(weights * totals, axis=0, keepdims=True))
    columns = jnp.concatenate(shares, axis=0).T
    flat = own * heads
    for s in range(chips):
        total = jnp.zeros((flat, LANES), jnp.float32)
        for j in range(chips):
            part = pieces[j][s ^ j, :own].astype(jnp.float32).reshape(flat, LANES)
            total = total + part * columns[:, s * chips + j : s * chips + j + 1]
        wide_ref[s * flat : (s + 1) * flat, :] = total
    rows = [wide_ref[pl.ds(h, chips * own, stride=heads), :] for h in range(heads)]
    out_ref[...] = jnp.concatenate(rows, axis=1).astype(jnp.bfloat16)


def merge(pieces, scale):
    chips, sections, heads, _ = pieces[0].shape
    own = sections - 1
    return pl.pallas_call(
        functools.partial(merge_kernel, scale),
        in_specs=[vmem_spec()] * chips,
        out_specs=vmem_spec(),
        out_shape=jax.ShapeDtypeStruct((chips * own, heads * LANES), jnp.bfloat16),
        scratch_shapes=[pltpu.VMEM((chips * own * heads, LANES), jnp.float32)],
        compiler_params=params(32),
        name="merge",
    )(*pieces)


def output_kernel(own, *refs):
    pieces, weight_ref = refs[:PAIR], refs[PAIR]
    outs, (rows_ref, terms_ref) = refs[PAIR + 1 : -2], refs[-2:]
    me = lax.axis_index("kv")
    for t in range(PAIR):
        piece = pieces[t][...].astype(jnp.float32)
        for s in range(piece.shape[0] // own):
            start = pl.multiple_of(jnp.bitwise_xor(me, PAIR * s + t) * own, own)
            rows_ref[pl.ds(start, own), :] = piece[s * own : (s + 1) * own]
    terms_ref[...] = jnp.dot(
        rows_ref[...].astype(jnp.bfloat16), weight_ref[...], preferred_element_type=jnp.float32
    )
    me = lax.axis_index("row")
    part = outs[0].shape[0]
    for s, ref in enumerate(outs):
        start = pl.multiple_of(jnp.bitwise_xor(me, s) * part, part)
        ref[...] = terms_ref[pl.ds(start, part), :].astype(ref.dtype)


def project_out(pieces, weight, own, row_count):
    half, width = pieces[0].shape
    rows, columns = PAIR * half, weight.shape[1]
    shape = (rows // row_count, columns)
    send = jax.ShapeDtypeStruct(shape, jnp.bfloat16)
    return pl.pallas_call(
        functools.partial(output_kernel, own),
        in_specs=[vmem_spec()] * (PAIR + 1),
        out_specs=[vmem_spec()] * row_count,
        out_shape=[jax.ShapeDtypeStruct(shape, jnp.float32)] + [send] * (row_count - 1),
        scratch_shapes=[pltpu.VMEM((rows, width), jnp.float32), pltpu.VMEM((rows, columns), jnp.float32)],
        compiler_params=params(24),
        name="project_out",
    )(*pieces, weight)


def exchange(x, axis, s):
    count = lax.axis_size(axis)
    return lax.ppermute(x, axis, [(i, i ^ s) for i in range(count)])


def gather_chips(x):
    return [x] + [exchange(x, "kv", s) for s in range(PAIR, lax.axis_size("kv"), PAIR)]


def gather_pairs(x):
    return gather_chips(jnp.concatenate([x, exchange(x, "kv", 1)], axis=0))


def local(
    hidden,
    query_weight,
    adapter_down_weight,
    adapter_up_weight,
    query_norm_gain,
    paged_key_cache,
    paged_value_cache,
    output_weight,
    holder,
    holder_block_index,
    block_used_length,
    tenant,
    tenant_adapter,
):
    own, slots = holder.shape
    rows, depth = hidden.shape
    kv_count = lax.axis_size("kv")
    row_count = lax.axis_size("row")
    adapters, _, rank = adapter_down_weight.shape
    width = query_weight.shape[1]
    head_size = query_norm_gain.shape[0]
    heads = width // head_size
    blocks, block_size, kv_local, _ = paged_key_cache.shape
    scale = 1.0 / math.sqrt(head_size)

    chips = kv_count // PAIR
    keep, send = project(
        tenant.reshape(1, rows),
        tenant_adapter.reshape(1, -1),
        holder,
        holder_block_index,
        block_used_length,
        hidden,
        query_weight,
        jnp.swapaxes(adapter_down_weight, 1, 2).reshape(adapters * rank, depth),
        rank,
        chips,
    )
    up = gather_up(tenant, tenant_adapter, adapter_up_weight, own)
    parts = add_pair(keep, exchange(send, "kv", 1), 3 * slots)
    parts = [parts[0]] + [exchange(parts[s], "kv", PAIR * s) for s in range(1, chips)]

    position = (jnp.sum(block_used_length, axis=1) - 1).astype(jnp.float32)
    half = head_size // 2
    frequency = ROPE_BASE ** (-(jnp.arange(half, dtype=jnp.float32) * 2.0) / head_size)
    angles = position[:, None] * frequency[None, :]
    cosine = jnp.concatenate([jnp.cos(angles), jnp.cos(angles)], axis=-1)
    sine = jnp.concatenate([-jnp.sin(angles), jnp.sin(angles)], axis=-1)
    queries = make_queries(parts, up, cosine, sine, query_norm_gain.reshape(1, head_size), heads, 3 * slots)
    queries = [q.reshape(PAIR, own, heads, head_size) for q in gather_pairs(queries)]
    items, bounds = make_list(parts, slots, blocks, block_size, kv_count)

    keys = paged_key_cache.reshape(blocks, block_size * kv_local, head_size)
    values = paged_value_cache.reshape(blocks, block_size * kv_local, head_size)
    keep, send = attend(items, bounds, queries, keys, values, kv_local, scale)
    merged = merge_pair(keep, exchange(send, "kv", 1), scale)
    attention = merge(gather_chips(merged), scale)
    terms = project_out([attention, exchange(attention, "kv", 1)], output_weight, own, row_count)
    total = terms[0]
    for s in range(1, row_count):
        total = total + exchange(terms[s], "row", s).astype(jnp.float32)
    return total.astype(jnp.bfloat16)


def solution(mesh):
    return jax.shard_map(
        local,
        mesh=mesh,
        in_specs=(
            P(None, "kv"),
            P("kv", "row"),
            P(None, "kv", None),
            P(None, None, "row"),
            P(),
            P("kv", None, "row", None),
            P("kv", None, "row", None),
            P("row", "kv"),
            P("kv", None),
            P("kv", None),
            P("kv", None),
            P(),
            P(),
        ),
        out_specs=P("row", "kv"),
        check_vma=False,
    )
```

```python
import functools
import math

import jax
import jax.numpy as jnp
from jax import lax
from jax.experimental import pallas as pl
from jax.experimental.pallas import tpu as pltpu
from jax.sharding import PartitionSpec as P

ADAPTER_SCALE = 0.5
ROPE_BASE = 1000000.0
EPSILON = 1e-06
NEG_FILL = -1e30
LANES = 128
COLUMN_TILE = 256
PAIR = 2
GROUP = 4
TASKS = 8
CHUNK = GROUP * TASKS
PHASES = 16
AHEAD = 6
DEPTH = 256
LOG2E = math.log2(math.e)
MIB = 1024 * 1024


def params(mib):
    return pltpu.CompilerParams(vmem_limit_bytes=mib * MIB)


def vmem_spec():
    return pl.BlockSpec(memory_space=pltpu.VMEM)


def in_hbm(*arrays):
    return [pltpu.with_memory_space_constraint(x, pltpu.HBM) for x in arrays]


def hbm_spec():
    return pl.BlockSpec(memory_space=pltpu.HBM)


def split3(x):
    high = x.astype(jnp.bfloat16).astype(jnp.float32)
    rest = x - high
    middle = rest.astype(jnp.bfloat16).astype(jnp.float32)
    return high, middle, (rest - middle).astype(jnp.bfloat16).astype(jnp.float32)


def to_column(row, count):
    shape = (count, count)
    eye = lax.broadcasted_iota(jnp.int32, shape, 0) == lax.broadcasted_iota(jnp.int32, shape, 1)
    return jnp.sum(jnp.where(eye, row.astype(jnp.float32), 0.0), axis=1, keepdims=True)


def project_kernel(
    rank,
    tenant_hbm,
    adapter_hbm,
    tenant_ref,
    adapter_ref,
    holder_ref,
    block_ref,
    length_ref,
    hidden_hbm,
    weight_hbm,
    down_hbm,
    up_hbm,
    keep_ref,
    send_ref,
    own_up_ref,
    hidden_ref,
    weight_ref,
    down_ref,
    total_ref,
    tenant_smem,
    adapter_smem,
    sems,
    up_sems,
):
    chips, own, _ = keep_ref.shape
    rows, depth = hidden_ref.shape
    width = weight_ref.shape[1]
    spans = [slice(i, min(i + DEPTH, depth)) for i in range(0, depth, DEPTH)]
    first = [
        pltpu.make_async_copy(hidden_hbm, hidden_ref, sems.at[0]),
        pltpu.make_async_copy(down_hbm, down_ref, sems.at[1]),
    ]
    chunks = [
        pltpu.make_async_copy(weight_hbm.at[span], weight_ref.at[span], sems.at[2 + i])
        for i, span in enumerate(spans)
    ]
    scalars = [
        pltpu.make_async_copy(tenant_hbm, tenant_smem, up_sems.at[own]),
        pltpu.make_async_copy(adapter_hbm, adapter_smem, up_sems.at[own + 1]),
    ]
    for copy in scalars + first + chunks:
        copy.start()

    slots = holder_ref.shape[1]
    numbers = [holder_ref[...], block_ref[...], length_ref[...], jnp.zeros((own, LANES - 3 * slots), jnp.int32)]
    numbers = jnp.concatenate(numbers, axis=1).astype(jnp.float32)
    tenants = adapter_ref.shape[1]
    tenant = to_column(tenant_ref[...], rows)
    pick = lax.broadcasted_iota(jnp.int32, (rows, tenants), 1).astype(jnp.float32) == tenant
    adapter = jnp.sum(jnp.where(pick, adapter_ref[...].astype(jnp.float32), 0.0), axis=1, keepdims=True).astype(
        jnp.int32
    )
    me = lax.axis_index("kv")
    even = me % PAIR == 0
    for copy in scalars:
        copy.wait()
    ups = [
        pltpu.make_async_copy(
            up_hbm.at[adapter_smem[tenant_smem[me * own + r]]], own_up_ref.at[r], up_sems.at[r]
        )
        for r in range(own)
    ]
    for copy in ups:
        copy.start()

    def store(columns, total):
        total = total.reshape(chips, PAIR, own, total.shape[1])
        keep_ref[:, :, columns] = jnp.where(even, total[:, 0], total[:, 1])
        send_ref[:, :, columns] = jnp.where(even, total[:, 1], total[:, 0])

    for copy in first:
        copy.wait()
    hidden = hidden_ref[...]
    low = lax.dot_general(hidden, down_ref[...], (((1,), (1,)), ((), ())), preferred_element_type=jnp.float32)
    column = lax.broadcasted_iota(jnp.int32, low.shape, 1)
    low = jnp.where((column >= adapter * rank) & (column < adapter * rank + rank), low, 0.0)
    low = sum(low[:, i : i + LANES] for i in range(LANES, low.shape[1], LANES)) + low[:, :LANES]
    shift = LANES // 2
    while shift >= rank:
        low = low + pltpu.roll(low, shift, 1)
        shift //= 2
    lane = lax.broadcasted_iota(jnp.int32, (rows, LANES), 1)
    numbers = jnp.concatenate([numbers] * (rows // own), axis=0)
    store(slice(width, width + LANES), jnp.where(lane < 3 * slots, numbers, low))
    for i, (span, copy) in enumerate(zip(spans, chunks)):
        copy.wait()
        for start in range(0, width, COLUMN_TILE):
            tile = slice(start, start + COLUMN_TILE)
            total = jnp.dot(hidden[:, span], weight_ref[span, tile], preferred_element_type=jnp.float32)
            if i > 0:
                total = total_ref[:, tile] + total
            if i < len(chunks) - 1:
                total_ref[:, tile] = total
            else:
                store(tile, total)
    for copy in ups:
        copy.wait()


def project(tenant, tenant_adapter, holder, block, length, hidden, query_weight, down, up, rank, chips):
    rows, depth = hidden.shape
    width = query_weight.shape[1]
    own = rows // chips // PAIR
    out = jax.ShapeDtypeStruct((chips, own, width + LANES), jnp.float32)
    tables = [x.reshape(1, -1) for x in (tenant, tenant_adapter)]
    operands = in_hbm(tenant, tenant_adapter, *tables, holder, block, length, hidden, query_weight, down, up)
    large = operands[7:10]
    return pl.pallas_call(
        functools.partial(project_kernel, rank),
        in_specs=[hbm_spec()] * 2 + [vmem_spec()] * 5 + [hbm_spec()] * 4,
        out_specs=[vmem_spec()] * 3,
        out_shape=[out, out, jax.ShapeDtypeStruct((own, *up.shape[1:]), up.dtype)],
        scratch_shapes=[pltpu.VMEM(x.shape, x.dtype) for x in large]
        + [
            pltpu.VMEM((rows, width), jnp.float32),
            pltpu.SMEM(tenant.shape, tenant.dtype),
            pltpu.SMEM(tenant_adapter.shape, tenant_adapter.dtype),
            pltpu.SemaphoreType.DMA((2 + pl.cdiv(depth, DEPTH),)),
            pltpu.SemaphoreType.DMA((own + 2,)),
        ],
        compiler_params=params(16),
        name="project",
    )(*operands)


def pair_kernel(number_lanes, keep_ref, got_ref, *out_refs):
    chips, own, width = keep_ref.shape
    width = width - LANES
    chip = lax.axis_index("kv") // PAIR
    lane = lax.broadcasted_iota(jnp.int32, (own, LANES), 1)
    for s, ref in enumerate(out_refs):
        c = jnp.bitwise_xor(chip, s)
        ref[:, :width] = keep_ref[c, :, :width] + got_ref[c, :, :width]
        keep = keep_ref[c, :, width:]
        ref[:, width : width + LANES] = jnp.where(lane < number_lanes, keep, keep + got_ref[c, :, width:])
        ref[:, width + LANES :] = got_ref[c, :, width:]


def add_pair(keep, got, number_lanes):
    chips, own, width = keep.shape
    return pl.pallas_call(
        functools.partial(pair_kernel, number_lanes),
        in_specs=[vmem_spec()] * 2,
        out_specs=[vmem_spec()] * chips,
        out_shape=[jax.ShapeDtypeStruct((own, width + LANES), jnp.float32)] * chips,
        compiler_params=params(16),
        name="add_pair",
    )(keep, got)


def queries_kernel(number_lanes, *refs):
    parts, (up_ref, cosine_ref, sine_ref, gain_ref, out_ref, turned_ref) = refs[:-6], refs[-6:]
    own, rank, width = up_ref.shape
    heads = turned_ref.shape[1]

    def whole(columns):
        total = parts[0][:, columns]
        for part in parts[1:]:
            total = total + part[:, columns]
        return total

    low = whole(slice(width, width + LANES)) * ADAPTER_SCALE
    line = lax.broadcasted_iota(jnp.int32, (rank, LANES), 0)
    lane = lax.broadcasted_iota(jnp.int32, (rank, LANES), 1)
    low = [
        jnp.sum(jnp.where(lane == line + number_lanes, low[r : r + 1], 0.0), axis=1, keepdims=True)
        for r in range(own)
    ]
    row = lax.broadcasted_iota(jnp.int32, (own, LANES), 0)
    cosine, sine, gain = cosine_ref[...], sine_ref[...], gain_ref[...]
    for h in range(heads):
        columns = slice(h * LANES, (h + 1) * LANES)
        query = whole(columns)
        adapted = jnp.zeros((own, LANES), jnp.float32)
        for r in range(own):
            adapted = jnp.where(row == r, jnp.sum(up_ref[r, :, columns] * low[r], axis=0, keepdims=True), adapted)
        query = query + adapted
        square = jnp.mean(query * query, axis=-1, keepdims=True)
        query = query * lax.rsqrt(square + EPSILON) * gain
        turned_ref[:, h, :] = query * cosine + pltpu.roll(query, LANES // 2, 1) * sine
    out_ref[...] = turned_ref[...].astype(jnp.bfloat16)


def make_queries(parts, up, cosine, sine, gain, heads, number_lanes):
    own = parts[0].shape[0]
    shape = (own, heads, LANES)
    return pl.pallas_call(
        functools.partial(queries_kernel, number_lanes),
        in_specs=[vmem_spec()] * (len(parts) + 4),
        out_specs=vmem_spec(),
        out_shape=jax.ShapeDtypeStruct(shape, jnp.bfloat16),
        scratch_shapes=[pltpu.VMEM(shape, jnp.float32)],
        compiler_params=params(16),
        name="queries",
    )(*parts, up, cosine, sine, gain)


def list_kernel(blocks, block_size, slots, *refs):
    pieces, (list_ref, bound_ref, place_ref, value_ref) = refs[:-4], refs[-4:]
    rows = place_ref.shape[0]
    capacity = list_ref.shape[1]
    me = lax.axis_index("kv").astype(jnp.float32)
    numbers = jnp.concatenate([p[:, i * LANES : (i + 1) * LANES] for p in pieces for i in range(PAIR)], axis=0)
    holder, block, length = (numbers[:, i * slots : (i + 1) * slots] for i in range(3))
    row = lax.broadcasted_iota(jnp.int32, (rows, slots), 0).astype(jnp.float32)
    spare = float(rows * blocks * block_size)
    value_ref[...] = (row * blocks + block) * block_size + (length - 1.0) - spare
    mine = holder == me
    key = jnp.where(mine, block, -1.0)

    def before(count, axis):
        first = lax.broadcasted_iota(jnp.int32, (count, count), axis)
        return jnp.where(first < lax.broadcasted_iota(jnp.int32, (count, count), 1 - axis), 1.0, 0.0).astype(
            jnp.bfloat16
        )

    lane = lax.broadcasted_iota(jnp.int32, (rows, blocks), 1).astype(jnp.float32)
    picks = [jnp.where(key[:, j : j + 1] == lane, 1.0, 0.0) for j in range(slots)]
    count = jnp.sum(functools.reduce(jnp.add, picks), axis=0, keepdims=True)
    tasks = jnp.floor((count + (GROUP - 1)) * (1.0 / GROUP))
    earlier = jnp.dot(
        jnp.broadcast_to(tasks, (8, blocks)).astype(jnp.bfloat16),
        before(blocks, 0),
        preferred_element_type=jnp.float32,
    )[:1]
    base = earlier * GROUP
    row_before = before(rows, 1)
    slot = lax.broadcasted_iota(jnp.int32, (rows, slots), 1)
    place = jnp.full((rows, slots), -1.0, jnp.float32)
    for j in range(slots):
        above = jnp.dot(row_before, picks[j].astype(jnp.bfloat16), preferred_element_type=jnp.float32)
        here = jnp.sum(picks[j] * (above + base), axis=1, keepdims=True)
        place = jnp.where((slot == j) & mine, here, place)
        base = base + jnp.sum(picks[j], axis=0, keepdims=True)
    place_ref[...] = place
    size = blocks // PHASES
    end = earlier + tasks
    block_lane = lax.broadcasted_iota(jnp.int32, (1, blocks), 1)
    bound_lane = lax.broadcasted_iota(jnp.int32, (1, LANES), 1)
    bounds = jnp.zeros((1, LANES), jnp.float32)
    for part in range(PHASES):
        done = jnp.sum(jnp.where(block_lane == (part + 1) * size - 1, end, 0.0), axis=1, keepdims=True)
        done = done * (1.0 / TASKS)
        done = jnp.ceil(done) if part == PHASES - 1 else jnp.floor(done)
        bounds = jnp.where(bound_lane == part + 1, done, bounds)
    bound_ref[...] = bounds.astype(jnp.int32)
    target = lax.broadcasted_iota(jnp.int32, (8, capacity), 1).astype(jnp.float32)

    def tile(t, total):
        here = pl.ds(pl.multiple_of(t * 8, 8), 8)
        places, values = place_ref[here, :], value_ref[here, :]
        for j in range(slots):
            total = total + jnp.where(places[:, j : j + 1] == target, values[:, j : j + 1], 0.0)
        return total

    total = lax.fori_loop(0, rows // 8, tile, jnp.zeros((8, capacity), jnp.float32))
    list_ref[...] = (jnp.sum(total, axis=0, keepdims=True) + spare).astype(jnp.int32)


def make_list(parts, slots, blocks, block_size, count):
    own, width = parts[0].shape
    rows = count * own
    most = 2 * own * slots // count * count + (GROUP - 1) * blocks + 3 * CHUNK
    capacity = -(-most // LANES) * LANES
    last = width // (PAIR * LANES) - 1
    return pl.pallas_call(
        functools.partial(list_kernel, blocks, block_size, slots),
        grid=(1,),
        in_specs=[pl.BlockSpec((own, PAIR * LANES), lambda i: (0, last))] * len(parts),
        out_specs=[
            pl.BlockSpec((1, capacity), lambda i: (0, 0)),
            pl.BlockSpec((1, LANES), lambda i: (0, 0)),
        ],
        out_shape=[
            jax.ShapeDtypeStruct((1, capacity), jnp.int32),
            jax.ShapeDtypeStruct((1, LANES), jnp.int32),
        ],
        scratch_shapes=[pltpu.VMEM((rows, slots), jnp.float32), pltpu.VMEM((rows, slots), jnp.float32)],
        compiler_params=params(16),
        cost_estimate=pl.CostEstimate(flops=10**8, bytes_accessed=10**7, transcendentals=0),
        name="slot_list",
    )(*parts)


def attend_kernel(scale, kv_local, count, list_vmem, bound_vmem, *refs):
    queries, refs = refs[: count // PAIR], refs[count // PAIR :]
    (key_hbm, value_hbm, keep_ref, send_ref, list_ref, bound_ref, query_ref, key_ref, value_ref) = refs[:9]
    (score_ref, part_top_ref, part_total_ref, part_sum_ref, number_sems, sems) = refs[9:15]
    states = [refs[15 + 3 * k : 18 + 3 * k] for k in range(GROUP)]
    heads = query_ref.shape[1]
    rows = query_ref.shape[0] - 1
    own = rows // count
    blocks, tokens, _ = key_ref.shape
    block_size = tokens // kv_local
    length_bits = (block_size - 1).bit_length()
    block_bits = (blocks - 1).bit_length()
    numbers = (
        pltpu.make_async_copy(list_vmem, list_ref, number_sems.at[0]),
        pltpu.make_async_copy(bound_vmem, bound_ref, number_sems.at[1]),
    )
    size = blocks // PHASES
    spans = [pl.ds(part * size, size) for part in range(PHASES)]
    copies = [
        (
            pltpu.make_async_copy(key_hbm.at[span], key_ref.at[span], sems.at[0, part]),
            pltpu.make_async_copy(value_hbm.at[span], value_ref.at[span], sems.at[1, part]),
        )
        for part, span in enumerate(spans)
    ]
    for pair in (copies[0], numbers, *copies[1:AHEAD]):
        for copy in pair:
            copy.start()

    factor = scale * LOG2E
    for s, piece in enumerate(queries):
        for t in range(PAIR):
            start = (PAIR * s + t) * own
            query_ref[start : start + own] = piece[t]
    query_ref[rows] = jnp.zeros((heads, LANES), jnp.bfloat16)
    for state in states:
        for ref, value in zip(state, (NEG_FILL, 0.0, 0.0)):
            ref[...] = jnp.full(ref.shape, value, jnp.float32)
    for ref in (score_ref, part_top_ref, part_total_ref, part_sum_ref):
        ref[...] = jnp.zeros(ref.shape, jnp.float32)
    group = heads // kv_local
    column = lax.broadcasted_iota(jnp.int32, (group, tokens), 1)
    first = column % kv_local == 0
    wide = (heads, LANES)
    narrow = (group, LANES)

    def entries(chunk):
        return [list_ref[0, chunk * CHUNK + j] for j in range(CHUNK)]

    def row_of(entry):
        return entry >> (length_bits + block_bits)

    def block_of(entry):
        return (entry >> length_bits) & (blocks - 1)

    def merge_task(row, t):
        before = [[ref[row[k]] for ref in states[k]] for k in range(GROUP)]
        after = []
        for k, (top, total, acc) in enumerate(before):
            j = t * GROUP + k
            part_top = part_top_ref[j]
            share = jnp.exp2(-jnp.abs(top - part_top) * factor)
            lower = top < part_top
            old, new = jnp.where(lower, share, 1.0), jnp.where(lower, 1.0, share)
            after.append(
                (
                    jnp.maximum(top, part_top),
                    total * old + part_total_ref[j] * new,
                    acc * old + part_sum_ref[t, k * heads : (k + 1) * heads] * new,
                )
            )
        for k in range(GROUP):
            for ref, value in zip(states[k], after[k]):
                ref[row[k]] = value

    def weigh_item(entry, t, k):
        j = t * GROUP + k
        start = k * heads
        scores = jnp.where(
            first, score_ref[t, start : start + group], score_ref[t, start + group : start + heads]
        )
        length = (entry & (block_size - 1)) + 1
        scores = jnp.where(column < length * kv_local, scores, NEG_FILL)
        tops = [
            jnp.max(x, axis=1, keepdims=True)
            for x in (jnp.where(first, scores, NEG_FILL), jnp.where(first, NEG_FILL, scores))
        ]
        weights = jnp.exp2((scores - jnp.where(first, tops[0], tops[1])) * factor)
        weights = (jnp.where(first, weights, 0.0), jnp.where(first, 0.0, weights))
        for a in range(kv_local):
            here = slice(a * group, (a + 1) * group)
            part_top_ref[j, here] = jnp.broadcast_to(tops[a], narrow)
            part_total_ref[j, here] = jnp.broadcast_to(jnp.sum(weights[a], axis=1, keepdims=True), narrow)
        return jnp.concatenate(weights, axis=0).astype(jnp.bfloat16)

    def turn(stages, i, carry):
        merged, weighed, scored = (entries(jnp.maximum(i - back, 0)) for back in (2, 1, 0))
        for t in range(TASKS):
            task = slice(t * GROUP, (t + 1) * GROUP)
            merge_task([jnp.where(i >= 2, row_of(entry), rows) for entry in merged[task]], t)
            if stages > 1:
                weights = [weigh_item(entry, t, k) for k, entry in enumerate(weighed[task])]
                part_sum_ref[t] = jnp.dot(
                    jnp.concatenate(weights, axis=0),
                    value_ref[block_of(weighed[task][0])],
                    preferred_element_type=jnp.float32,
                )
            if stages > 2:
                score_ref[t] = lax.dot_general(
                    jnp.concatenate([query_ref[row_of(entry)] for entry in scored[task]], axis=0),
                    key_ref[block_of(scored[task][0])],
                    (((1,), (1,)), ((), ())),
                    preferred_element_type=jnp.float32,
                )
        return carry

    for copy in numbers:
        copy.wait()
    for part in range(PHASES):
        for copy in copies[part]:
            copy.wait()
        for pair in copies[part + AHEAD : part + AHEAD + 1]:
            for copy in pair:
                copy.start()
        lax.fori_loop(bound_ref[0, part], bound_ref[0, part + 1], functools.partial(turn, 3), 0)
    last = bound_ref[0, PHASES]
    turn(2, last, 0)
    turn(1, last + 1, 0)

    square = (own * heads, LANES)
    eye = lax.broadcasted_iota(jnp.int32, square, 0) == lax.broadcasted_iota(jnp.int32, square, 1)
    line = lax.broadcasted_iota(jnp.int32, wide, 0)
    for q in range(count):
        ref = (keep_ref, send_ref)[q % PAIR]
        mine = slice(q * own, (q + 1) * own)
        tops = [top_ref[mine] for top_ref, _, _ in states]
        high = functools.reduce(jnp.maximum, tops)
        shares = [jnp.exp2((top - high) * factor) for top in tops]
        total = sum(total_ref[mine] * share for (_, total_ref, _), share in zip(states, shares))
        ref[q // PAIR, :own] = sum(sum_ref[mine] * share for (_, _, sum_ref), share in zip(states, shares))
        high, total = (
            jnp.sum(jnp.where(eye, x.reshape(square), 0.0), axis=0, keepdims=True) for x in (high, total)
        )
        ref[q // PAIR, own] = jnp.where(line == 0, high, jnp.where(line == 1, total, 0.0))


def attend(items, bounds, queries, keys, values, kv_local, scale):
    _, own, heads, _ = queries[0].shape
    count = len(queries) * PAIR
    rows = count * own
    tokens = keys.shape[1]
    keys, values = in_hbm(keys, values)
    state = pltpu.VMEM((rows + 1, heads, LANES), jnp.float32)
    part = pltpu.VMEM((CHUNK, heads, LANES), jnp.float32)
    return pl.pallas_call(
        functools.partial(attend_kernel, scale, kv_local, count),
        in_specs=[vmem_spec()] * (2 + len(queries)) + [hbm_spec()] * 2,
        out_specs=[vmem_spec()] * PAIR,
        out_shape=[jax.ShapeDtypeStruct((count // PAIR, own + 1, heads, LANES), jnp.float32)] * PAIR,
        scratch_shapes=[
            pltpu.SMEM(items.shape, items.dtype),
            pltpu.SMEM(bounds.shape, bounds.dtype),
            pltpu.VMEM((rows + 1, heads, LANES), jnp.bfloat16),
            pltpu.VMEM(keys.shape, keys.dtype),
            pltpu.VMEM(values.shape, values.dtype),
            pltpu.VMEM((TASKS, GROUP * heads, tokens), jnp.float32),
            part,
            part,
            pltpu.VMEM((TASKS, GROUP * heads, LANES), jnp.float32),
            pltpu.SemaphoreType.DMA((2,)),
            pltpu.SemaphoreType.DMA((2, PHASES)),
        ]
        + [state] * (3 * GROUP),
        compiler_params=params(28 + 3 * GROUP * rows * heads * LANES * 4 // MIB),
        name="attend",
    )(items, bounds, *queries, keys, values)


def merge_pair_kernel(scale, keep_ref, got_ref, out_ref):
    chips, sections, heads, _ = keep_ref.shape
    own = sections - 1
    factor = scale * LOG2E
    line = lax.broadcasted_iota(jnp.int32, (heads, LANES), 0)
    shares, stats = [], []
    for s in range(chips):
        keep, got = keep_ref[s, own], got_ref[s, own]
        high = jnp.maximum(keep[0:1], got[0:1])
        pair = [jnp.exp2((x[0:1] - high) * factor) for x in (keep, got)]
        shares += pair
        total = pair[0] * keep[1:2] + pair[1] * got[1:2]
        stat = jnp.zeros((heads, LANES), jnp.float32)
        for position, piece in enumerate(split3(high) + split3(total)):
            stat = jnp.where(line == position, piece, stat)
        stats.append(stat)
    columns = jnp.concatenate(shares, axis=0).T
    flat = (own * heads, LANES)
    for s in range(chips):
        total = keep_ref[s, :own].reshape(flat) * columns[:, PAIR * s : PAIR * s + 1]
        total = total + got_ref[s, :own].reshape(flat) * columns[:, PAIR * s + 1 : PAIR * s + 2]
        out_ref[s, :own] = total.astype(jnp.bfloat16).reshape(own, heads, LANES)
        out_ref[s, own] = stats[s].astype(jnp.bfloat16)


def merge_pair(keep, got, scale):
    return pl.pallas_call(
        functools.partial(merge_pair_kernel, scale),
        in_specs=[vmem_spec()] * 2,
        out_specs=vmem_spec(),
        out_shape=jax.ShapeDtypeStruct(keep.shape, jnp.bfloat16),
        compiler_params=params(16),
        name="merge_pair",
    )(keep, got)


def merge_kernel(scale, *refs):
    pieces, (out_ref, wide_ref) = refs[:-2], refs[-2:]
    chips, sections, heads, _ = pieces[0].shape
    own = sections - 1
    factor = scale * LOG2E
    shares = []
    for s in range(chips):
        stats = [pieces[j][s ^ j, own].astype(jnp.float32) for j in range(chips)]
        tops = jnp.concatenate([x[0:1] + x[1:2] + x[2:3] for x in stats], axis=0)
        totals = jnp.concatenate([x[3:4] + x[4:5] + x[5:6] for x in stats], axis=0)
        weights = jnp.exp2((tops - jnp.max(tops, axis=0, keepdims=True)) * factor)
        shares.append(weights / jnp.sum(weights * totals, axis=0, keepdims=True))
    columns = jnp.concatenate(shares, axis=0).T
    flat = own * heads
    for s in range(chips):
        total = jnp.zeros((flat, LANES), jnp.float32)
        for j in range(chips):
            part = pieces[j][s ^ j, :own].astype(jnp.float32).reshape(flat, LANES)
            total = total + part * columns[:, s * chips + j : s * chips + j + 1]
        wide_ref[s * flat : (s + 1) * flat, :] = total
    rows = [wide_ref[pl.ds(h, chips * own, stride=heads), :] for h in range(heads)]
    out_ref[...] = jnp.concatenate(rows, axis=1).astype(jnp.bfloat16)


def merge(pieces, scale):
    chips, sections, heads, _ = pieces[0].shape
    own = sections - 1
    return pl.pallas_call(
        functools.partial(merge_kernel, scale),
        in_specs=[vmem_spec()] * chips,
        out_specs=vmem_spec(),
        out_shape=jax.ShapeDtypeStruct((chips * own, heads * LANES), jnp.bfloat16),
        scratch_shapes=[pltpu.VMEM((chips * own * heads, LANES), jnp.float32)],
        compiler_params=params(32),
        name="merge",
    )(*pieces)


def output_kernel(own, *refs):
    pieces, weight_ref = refs[:PAIR], refs[PAIR]
    outs, (rows_ref, terms_ref) = refs[PAIR + 1 : -2], refs[-2:]
    me = lax.axis_index("kv")
    for t in range(PAIR):
        piece = pieces[t][...].astype(jnp.float32)
        for s in range(piece.shape[0] // own):
            start = pl.multiple_of(jnp.bitwise_xor(me, PAIR * s + t) * own, own)
            rows_ref[pl.ds(start, own), :] = piece[s * own : (s + 1) * own]
    terms_ref[...] = jnp.dot(
        rows_ref[...].astype(jnp.bfloat16), weight_ref[...], preferred_element_type=jnp.float32
    )
    me = lax.axis_index("row")
    part = outs[0].shape[0]
    for s, ref in enumerate(outs):
        start = pl.multiple_of(jnp.bitwise_xor(me, s) * part, part)
        ref[...] = terms_ref[pl.ds(start, part), :].astype(ref.dtype)


def project_out(pieces, weight, own, row_count):
    half, width = pieces[0].shape
    rows, columns = PAIR * half, weight.shape[1]
    shape = (rows // row_count, columns)
    send = jax.ShapeDtypeStruct(shape, jnp.bfloat16)
    return pl.pallas_call(
        functools.partial(output_kernel, own),
        in_specs=[vmem_spec()] * (PAIR + 1),
        out_specs=[vmem_spec()] * row_count,
        out_shape=[jax.ShapeDtypeStruct(shape, jnp.float32)] + [send] * (row_count - 1),
        scratch_shapes=[pltpu.VMEM((rows, width), jnp.float32), pltpu.VMEM((rows, columns), jnp.float32)],
        compiler_params=params(24),
        name="project_out",
    )(*pieces, weight)


def exchange(x, axis, s):
    count = lax.axis_size(axis)
    return lax.ppermute(x, axis, [(i, i ^ s) for i in range(count)])


def gather_chips(x):
    return [x] + [exchange(x, "kv", s) for s in range(PAIR, lax.axis_size("kv"), PAIR)]


def gather_pairs(x):
    return gather_chips(jnp.concatenate([x, exchange(x, "kv", 1)], axis=0))


def local(
    hidden,
    query_weight,
    adapter_down_weight,
    adapter_up_weight,
    query_norm_gain,
    paged_key_cache,
    paged_value_cache,
    output_weight,
    holder,
    holder_block_index,
    block_used_length,
    tenant,
    tenant_adapter,
):
    own, slots = holder.shape
    rows, depth = hidden.shape
    kv_count = lax.axis_size("kv")
    row_count = lax.axis_size("row")
    adapters, _, rank = adapter_down_weight.shape
    width = query_weight.shape[1]
    head_size = query_norm_gain.shape[0]
    heads = width // head_size
    blocks, block_size, kv_local, _ = paged_key_cache.shape
    scale = 1.0 / math.sqrt(head_size)

    chips = kv_count // PAIR
    keep, send, up = project(
        tenant,
        tenant_adapter,
        holder,
        holder_block_index,
        block_used_length,
        hidden,
        query_weight,
        jnp.swapaxes(adapter_down_weight, 1, 2).reshape(adapters * rank, depth),
        adapter_up_weight,
        rank,
        chips,
    )
    parts = add_pair(keep, exchange(send, "kv", 1), 3 * slots)
    parts = [parts[0]] + [exchange(parts[s], "kv", PAIR * s) for s in range(1, chips)]

    position = (jnp.sum(block_used_length, axis=1) - 1).astype(jnp.float32)
    half = head_size // 2
    frequency = ROPE_BASE ** (-(jnp.arange(half, dtype=jnp.float32) * 2.0) / head_size)
    angles = position[:, None] * frequency[None, :]
    cosine = jnp.concatenate([jnp.cos(angles), jnp.cos(angles)], axis=-1)
    sine = jnp.concatenate([-jnp.sin(angles), jnp.sin(angles)], axis=-1)
    queries = make_queries(parts, up, cosine, sine, query_norm_gain.reshape(1, head_size), heads, 3 * slots)
    queries = [q.reshape(PAIR, own, heads, head_size) for q in gather_pairs(queries)]
    items, bounds = make_list(parts, slots, blocks, block_size, kv_count)

    keys = paged_key_cache.reshape(blocks, block_size * kv_local, head_size)
    values = paged_value_cache.reshape(blocks, block_size * kv_local, head_size)
    keep, send = attend(items, bounds, queries, keys, values, kv_local, scale)
    merged = merge_pair(keep, exchange(send, "kv", 1), scale)
    attention = merge(gather_chips(merged), scale)
    terms = project_out([attention, exchange(attention, "kv", 1)], output_weight, own, row_count)
    total = terms[0]
    for s in range(1, row_count):
        total = total + exchange(terms[s], "row", s).astype(jnp.float32)
    return total.astype(jnp.bfloat16)


def solution(mesh):
    return jax.shard_map(
        local,
        mesh=mesh,
        in_specs=(
            P(None, "kv"),
            P("kv", "row"),
            P(None, "kv", None),
            P(None, None, "row"),
            P(),
            P("kv", None, "row", None),
            P("kv", None, "row", None),
            P("row", "kv"),
            P("kv", None),
            P("kv", None),
            P("kv", None),
            P(),
            P(),
        ),
        out_specs=P("row", "kv"),
        check_vma=False,
    )
```

```python
import functools
import math

import jax
import jax.numpy as jnp
from jax import lax
from jax.experimental import pallas as pl
from jax.experimental.pallas import tpu as pltpu
from jax.sharding import PartitionSpec as P

ADAPTER_SCALE = 0.5
ROPE_BASE = 1000000.0
EPSILON = 1e-06
NEG_FILL = -1e30
LANES = 128
COLUMN_TILE = 256
PAIR = 2
GROUP = 4
TASKS = 8
CHUNK = GROUP * TASKS
SETS = 2
PHASES = 16
AHEAD = 6
DEPTH = 256
LOG2E = math.log2(math.e)
MIB = 1024 * 1024


def params(mib):
    return pltpu.CompilerParams(vmem_limit_bytes=mib * MIB)


def vmem_spec():
    return pl.BlockSpec(memory_space=pltpu.VMEM)


def in_hbm(*arrays):
    return [pltpu.with_memory_space_constraint(x, pltpu.HBM) for x in arrays]


def hbm_spec():
    return pl.BlockSpec(memory_space=pltpu.HBM)


def split3(x):
    high = x.astype(jnp.bfloat16).astype(jnp.float32)
    rest = x - high
    middle = rest.astype(jnp.bfloat16).astype(jnp.float32)
    return high, middle, (rest - middle).astype(jnp.bfloat16).astype(jnp.float32)


def to_column(row, count):
    shape = (count, count)
    eye = lax.broadcasted_iota(jnp.int32, shape, 0) == lax.broadcasted_iota(jnp.int32, shape, 1)
    return jnp.sum(jnp.where(eye, row.astype(jnp.float32), 0.0), axis=1, keepdims=True)


def project_kernel(
    rank,
    tenant_hbm,
    adapter_hbm,
    tenant_row_hbm,
    adapter_row_hbm,
    holder_hbm,
    block_hbm,
    length_hbm,
    hidden_hbm,
    weight_hbm,
    down_hbm,
    up_hbm,
    keep_ref,
    send_ref,
    own_up_ref,
    tenant_ref,
    adapter_ref,
    holder_ref,
    block_ref,
    length_ref,
    hidden_ref,
    weight_ref,
    down_ref,
    total_ref,
    tenant_smem,
    adapter_smem,
    sems,
    up_sems,
    small_sems,
):
    chips, own, _ = keep_ref.shape
    rows, depth = hidden_ref.shape
    width = weight_ref.shape[1]
    spans = [slice(i, min(i + DEPTH, depth)) for i in range(0, depth, DEPTH)]
    first = [
        pltpu.make_async_copy(hidden_hbm, hidden_ref, sems.at[0]),
        pltpu.make_async_copy(down_hbm, down_ref, sems.at[1]),
    ]
    chunks = [
        pltpu.make_async_copy(weight_hbm.at[span], weight_ref.at[span], sems.at[2 + i])
        for i, span in enumerate(spans)
    ]
    scalars = [
        pltpu.make_async_copy(tenant_hbm, tenant_smem, up_sems.at[own]),
        pltpu.make_async_copy(adapter_hbm, adapter_smem, up_sems.at[own + 1]),
    ]
    small = [
        pltpu.make_async_copy(hbm, ref, small_sems.at[i])
        for i, (hbm, ref) in enumerate(
            (
                (tenant_row_hbm, tenant_ref),
                (adapter_row_hbm, adapter_ref),
                (holder_hbm, holder_ref),
                (block_hbm, block_ref),
                (length_hbm, length_ref),
            )
        )
    ]
    for copy in scalars + small + first + chunks:
        copy.start()
    for copy in small:
        copy.wait()

    slots = holder_ref.shape[1]
    numbers = [holder_ref[...], block_ref[...], length_ref[...], jnp.zeros((own, LANES - 3 * slots), jnp.int32)]
    numbers = jnp.concatenate(numbers, axis=1).astype(jnp.float32)
    tenants = adapter_ref.shape[1]
    tenant = to_column(tenant_ref[...], rows)
    pick = lax.broadcasted_iota(jnp.int32, (rows, tenants), 1).astype(jnp.float32) == tenant
    adapter = jnp.sum(jnp.where(pick, adapter_ref[...].astype(jnp.float32), 0.0), axis=1, keepdims=True).astype(
        jnp.int32
    )
    me = lax.axis_index("kv")
    even = me % PAIR == 0
    for copy in scalars:
        copy.wait()
    ups = [
        pltpu.make_async_copy(
            up_hbm.at[adapter_smem[tenant_smem[me * own + r]]], own_up_ref.at[r], up_sems.at[r]
        )
        for r in range(own)
    ]
    for copy in ups:
        copy.start()

    def store(columns, total):
        total = total.reshape(chips, PAIR, own, total.shape[1])
        keep_ref[:, :, columns] = jnp.where(even, total[:, 0], total[:, 1])
        send_ref[:, :, columns] = jnp.where(even, total[:, 1], total[:, 0])

    for copy in first:
        copy.wait()
    hidden = hidden_ref[...]
    low = lax.dot_general(hidden, down_ref[...], (((1,), (1,)), ((), ())), preferred_element_type=jnp.float32)
    column = lax.broadcasted_iota(jnp.int32, low.shape, 1)
    low = jnp.where((column >= adapter * rank) & (column < adapter * rank + rank), low, 0.0)
    low = sum(low[:, i : i + LANES] for i in range(LANES, low.shape[1], LANES)) + low[:, :LANES]
    shift = LANES // 2
    while shift >= rank:
        low = low + pltpu.roll(low, shift, 1)
        shift //= 2
    lane = lax.broadcasted_iota(jnp.int32, (rows, LANES), 1)
    numbers = jnp.concatenate([numbers] * (rows // own), axis=0)
    store(slice(width, width + LANES), jnp.where(lane < 3 * slots, numbers, low))
    for i, (span, copy) in enumerate(zip(spans, chunks)):
        copy.wait()
        for start in range(0, width, COLUMN_TILE):
            tile = slice(start, start + COLUMN_TILE)
            total = jnp.dot(hidden[:, span], weight_ref[span, tile], preferred_element_type=jnp.float32)
            if i > 0:
                total = total_ref[:, tile] + total
            if i < len(chunks) - 1:
                total_ref[:, tile] = total
            else:
                store(tile, total)
    for copy in ups:
        copy.wait()


def project(tenant, tenant_adapter, holder, block, length, hidden, query_weight, down, up, rank, chips):
    rows, depth = hidden.shape
    width = query_weight.shape[1]
    own = rows // chips // PAIR
    out = jax.ShapeDtypeStruct((chips, own, width + LANES), jnp.float32)
    tables = [x.reshape(1, -1) for x in (tenant, tenant_adapter)]
    operands = in_hbm(tenant, tenant_adapter, *tables, holder, block, length, hidden, query_weight, down, up)
    local = operands[2:10]
    return pl.pallas_call(
        functools.partial(project_kernel, rank),
        in_specs=[hbm_spec()] * len(operands),
        out_specs=[vmem_spec()] * 3,
        out_shape=[out, out, jax.ShapeDtypeStruct((own, *up.shape[1:]), up.dtype)],
        scratch_shapes=[pltpu.VMEM(x.shape, x.dtype) for x in local]
        + [
            pltpu.VMEM((rows, width), jnp.float32),
            pltpu.SMEM(tenant.shape, tenant.dtype),
            pltpu.SMEM(tenant_adapter.shape, tenant_adapter.dtype),
            pltpu.SemaphoreType.DMA((2 + pl.cdiv(depth, DEPTH),)),
            pltpu.SemaphoreType.DMA((own + 2,)),
            pltpu.SemaphoreType.DMA((5,)),
        ],
        compiler_params=params(16),
        name="project",
    )(*operands)


def pair_kernel(number_lanes, keep_ref, got_ref, *out_refs):
    chips, own, width = keep_ref.shape
    width = width - LANES
    chip = lax.axis_index("kv") // PAIR
    lane = lax.broadcasted_iota(jnp.int32, (own, LANES), 1)
    for s, ref in enumerate(out_refs):
        c = jnp.bitwise_xor(chip, s)
        ref[:, :width] = keep_ref[c, :, :width] + got_ref[c, :, :width]
        keep = keep_ref[c, :, width:]
        ref[:, width : width + LANES] = jnp.where(lane < number_lanes, keep, keep + got_ref[c, :, width:])
        ref[:, width + LANES :] = got_ref[c, :, width:]


def add_pair(keep, got, number_lanes):
    chips, own, width = keep.shape
    return pl.pallas_call(
        functools.partial(pair_kernel, number_lanes),
        in_specs=[vmem_spec()] * 2,
        out_specs=[vmem_spec()] * chips,
        out_shape=[jax.ShapeDtypeStruct((own, width + LANES), jnp.float32)] * chips,
        compiler_params=params(16),
        name="add_pair",
    )(keep, got)


def queries_kernel(number_lanes, *refs):
    parts, (up_ref, cosine_ref, sine_ref, gain_ref, out_ref, turned_ref) = refs[:-6], refs[-6:]
    own, rank, width = up_ref.shape
    heads = turned_ref.shape[1]

    def whole(columns):
        total = parts[0][:, columns]
        for part in parts[1:]:
            total = total + part[:, columns]
        return total

    low = whole(slice(width, width + LANES)) * ADAPTER_SCALE
    line = lax.broadcasted_iota(jnp.int32, (rank, LANES), 0)
    lane = lax.broadcasted_iota(jnp.int32, (rank, LANES), 1)
    low = [
        jnp.sum(jnp.where(lane == line + number_lanes, low[r : r + 1], 0.0), axis=1, keepdims=True)
        for r in range(own)
    ]
    row = lax.broadcasted_iota(jnp.int32, (own, LANES), 0)
    cosine, sine, gain = cosine_ref[...], sine_ref[...], gain_ref[...]
    for h in range(heads):
        columns = slice(h * LANES, (h + 1) * LANES)
        query = whole(columns)
        adapted = jnp.zeros((own, LANES), jnp.float32)
        for r in range(own):
            adapted = jnp.where(row == r, jnp.sum(up_ref[r, :, columns] * low[r], axis=0, keepdims=True), adapted)
        query = query + adapted
        square = jnp.mean(query * query, axis=-1, keepdims=True)
        query = query * lax.rsqrt(square + EPSILON) * gain
        turned_ref[:, h, :] = query * cosine + pltpu.roll(query, LANES // 2, 1) * sine
    out_ref[...] = turned_ref[...].astype(jnp.bfloat16)


def make_queries(parts, up, cosine, sine, gain, heads, number_lanes):
    own = parts[0].shape[0]
    shape = (own, heads, LANES)
    return pl.pallas_call(
        functools.partial(queries_kernel, number_lanes),
        in_specs=[vmem_spec()] * (len(parts) + 4),
        out_specs=vmem_spec(),
        out_shape=jax.ShapeDtypeStruct(shape, jnp.bfloat16),
        scratch_shapes=[pltpu.VMEM(shape, jnp.float32)],
        compiler_params=params(16),
        name="queries",
    )(*parts, up, cosine, sine, gain)


def place_kernel(blocks, block_size, slots, *refs):
    pieces, (place_ref, value_ref, bound_ref) = refs[:-3], refs[-3:]
    rows = place_ref.shape[0]
    me = lax.axis_index("kv").astype(jnp.float32)
    numbers = jnp.concatenate([p[:, i * LANES : (i + 1) * LANES] for p in pieces for i in range(PAIR)], axis=0)
    holder, block, length = (numbers[:, i * slots : (i + 1) * slots] for i in range(3))
    row = lax.broadcasted_iota(jnp.int32, (rows, slots), 0).astype(jnp.float32)
    spare = float(rows * blocks * block_size)
    value_ref[...] = (row * blocks + block) * block_size + (length - 1.0) - spare
    mine = holder == me
    key = jnp.where(mine, block, -1.0)

    def before(count, axis):
        first = lax.broadcasted_iota(jnp.int32, (count, count), axis)
        return jnp.where(first < lax.broadcasted_iota(jnp.int32, (count, count), 1 - axis), 1.0, 0.0).astype(
            jnp.bfloat16
        )

    lane = lax.broadcasted_iota(jnp.int32, (rows, blocks), 1).astype(jnp.float32)
    picks = [jnp.where(key[:, j : j + 1] == lane, 1.0, 0.0) for j in range(slots)]
    count = jnp.sum(functools.reduce(jnp.add, picks), axis=0, keepdims=True)
    tasks = jnp.floor((count + (GROUP - 1)) * (1.0 / GROUP))
    earlier = jnp.dot(
        jnp.broadcast_to(tasks, (8, blocks)).astype(jnp.bfloat16),
        before(blocks, 0),
        preferred_element_type=jnp.float32,
    )[:1]
    base = earlier * GROUP
    row_before = before(rows, 1)
    slot = lax.broadcasted_iota(jnp.int32, (rows, slots), 1)
    place = jnp.full((rows, slots), -1.0, jnp.float32)
    for j in range(slots):
        above = jnp.dot(row_before, picks[j].astype(jnp.bfloat16), preferred_element_type=jnp.float32)
        here = jnp.sum(picks[j] * (above + base), axis=1, keepdims=True)
        place = jnp.where((slot == j) & mine, here, place)
        base = base + jnp.sum(picks[j], axis=0, keepdims=True)
    place_ref[...] = place
    size = blocks // PHASES
    end = earlier + tasks
    block_lane = lax.broadcasted_iota(jnp.int32, (1, blocks), 1)
    bound_lane = lax.broadcasted_iota(jnp.int32, (1, LANES), 1)
    bounds = jnp.zeros((1, LANES), jnp.float32)
    for part in range(PHASES):
        done = jnp.sum(jnp.where(block_lane == (part + 1) * size - 1, end, 0.0), axis=1, keepdims=True)
        done = done * (1.0 / TASKS)
        done = jnp.ceil(done) if part == PHASES - 1 else jnp.floor(done)
        bounds = jnp.where(bound_lane == part + 1, done, bounds)
    bound_ref[...] = bounds.astype(jnp.int32)


def list_kernel(spare, place_ref, value_ref, list_ref):
    rows, slots = place_ref.shape
    capacity = list_ref.shape[1]
    target = lax.broadcasted_iota(jnp.int32, (8, capacity), 1).astype(jnp.float32)

    def tile(t, total):
        here = pl.ds(pl.multiple_of(t * 8, 8), 8)
        places, values = place_ref[here, :], value_ref[here, :]
        for j in range(slots):
            total = total + jnp.where(places[:, j : j + 1] == target, values[:, j : j + 1], 0.0)
        return total

    total = lax.fori_loop(0, rows // 8, tile, jnp.zeros((8, capacity), jnp.float32))
    list_ref[...] = (jnp.sum(total, axis=0, keepdims=True) + spare).astype(jnp.int32)


def make_places(parts, slots, blocks, block_size, count):
    own, width = parts[0].shape
    rows = count * own
    last = width // (PAIR * LANES) - 1
    table = jax.ShapeDtypeStruct((rows, slots), jnp.float32)
    bounds = jax.ShapeDtypeStruct((1, LANES), jnp.int32)
    return pl.pallas_call(
        functools.partial(place_kernel, blocks, block_size, slots),
        grid=(1,),
        in_specs=[pl.BlockSpec((own, PAIR * LANES), lambda i: (0, last))] * len(parts),
        out_specs=[pl.BlockSpec(x.shape, lambda i: (0, 0)) for x in (table, table, bounds)],
        out_shape=[table, table, bounds],
        compiler_params=params(16),
        cost_estimate=pl.CostEstimate(flops=10**8, bytes_accessed=4 * 10**6, transcendentals=0),
        name="slot_places",
    )(*parts)


def make_list(places, values, blocks, block_size, count):
    rows, slots = places.shape
    most = 2 * rows * slots // count // count * count + (GROUP - 1) * blocks + 3 * CHUNK
    capacity = -(-most // LANES) * LANES
    return pl.pallas_call(
        functools.partial(list_kernel, float(rows * blocks * block_size)),
        in_specs=[vmem_spec()] * 2,
        out_specs=vmem_spec(),
        out_shape=jax.ShapeDtypeStruct((1, capacity), jnp.int32),
        compiler_params=params(16),
        cost_estimate=pl.CostEstimate(flops=10**8, bytes_accessed=4 * 10**6, transcendentals=0),
        name="slot_list",
    )(places, values)


def join_kernel(own_ref, other_ref, places_ref, out_ref):
    own = own_ref.shape[0]
    out_ref[:own] = own_ref[...]
    out_ref[own:] = other_ref[...]


def join_pair(own, other, places):
    return pl.pallas_call(
        join_kernel,
        in_specs=[vmem_spec()] * 3,
        out_specs=vmem_spec(),
        out_shape=jax.ShapeDtypeStruct((PAIR * own.shape[0], *own.shape[1:]), own.dtype),
        compiler_params=params(16),
        name="join_pair",
    )(own, other, places)


def attend_kernel(scale, kv_local, count, list_vmem, bound_vmem, *refs):
    queries, refs = refs[: count // PAIR], refs[count // PAIR :]
    (key_hbm, value_hbm, keep_ref, send_ref, list_ref, bound_ref, query_ref, key_ref, value_ref) = refs[:9]
    (score_ref, part_top_ref, part_total_ref, part_sum_ref, number_sems, sems) = refs[9:15]
    states = [refs[15 + 3 * k : 18 + 3 * k] for k in range(SETS)]
    heads = query_ref.shape[1]
    rows = query_ref.shape[0] - 1
    own = rows // count
    blocks, tokens, _ = key_ref.shape
    block_size = tokens // kv_local
    length_bits = (block_size - 1).bit_length()
    block_bits = (blocks - 1).bit_length()
    numbers = (
        pltpu.make_async_copy(list_vmem, list_ref, number_sems.at[0]),
        pltpu.make_async_copy(bound_vmem, bound_ref, number_sems.at[1]),
    )
    size = blocks // PHASES
    spans = [pl.ds(part * size, size) for part in range(PHASES)]
    copies = [
        (
            pltpu.make_async_copy(key_hbm.at[span], key_ref.at[span], sems.at[0, part]),
            pltpu.make_async_copy(value_hbm.at[span], value_ref.at[span], sems.at[1, part]),
        )
        for part, span in enumerate(spans)
    ]
    for pair in (copies[0], numbers, *copies[1:AHEAD]):
        for copy in pair:
            copy.start()

    factor = scale * LOG2E
    for s, piece in enumerate(queries):
        for t in range(PAIR):
            start = (PAIR * s + t) * own
            query_ref[start : start + own] = piece[t]
    query_ref[rows] = jnp.zeros((heads, LANES), jnp.bfloat16)
    for state in states:
        for ref, value in zip(state, (NEG_FILL, 0.0, 0.0)):
            ref[...] = jnp.full(ref.shape, value, jnp.float32)
    for ref in (score_ref, part_top_ref, part_total_ref, part_sum_ref):
        ref[...] = jnp.zeros(ref.shape, jnp.float32)
    group = heads // kv_local
    column = lax.broadcasted_iota(jnp.int32, (group, tokens), 1)
    first = column % kv_local == 0
    wide = (heads, LANES)
    narrow = (group, LANES)

    def entries(chunk):
        return [list_ref[0, chunk * CHUNK + j] for j in range(CHUNK)]

    def row_of(entry):
        return entry >> (length_bits + block_bits)

    def block_of(entry):
        return (entry >> length_bits) & (blocks - 1)

    def merge_slots(row, start):
        before = [[ref[r] for ref in state] for r, state in zip(row, states)]
        after = []
        for k, (top, total, acc) in enumerate(before):
            t, place = divmod(start + k, GROUP)
            part_top = part_top_ref[start + k]
            share = jnp.exp2(-jnp.abs(top - part_top) * factor)
            lower = top < part_top
            old, new = jnp.where(lower, share, 1.0), jnp.where(lower, 1.0, share)
            after.append(
                (
                    jnp.maximum(top, part_top),
                    total * old + part_total_ref[start + k] * new,
                    acc * old + part_sum_ref[t, place * heads : (place + 1) * heads] * new,
                )
            )
        for r, state, new in zip(row, states, after):
            for ref, value in zip(state, new):
                ref[r] = value

    def weigh_item(entry, t, k):
        j = t * GROUP + k
        start = k * heads
        scores = jnp.where(
            first, score_ref[t, start : start + group], score_ref[t, start + group : start + heads]
        )
        length = (entry & (block_size - 1)) + 1
        scores = jnp.where(column < length * kv_local, scores, NEG_FILL)
        tops = [
            jnp.max(x, axis=1, keepdims=True)
            for x in (jnp.where(first, scores, NEG_FILL), jnp.where(first, NEG_FILL, scores))
        ]
        weights = jnp.exp2((scores - jnp.where(first, tops[0], tops[1])) * factor)
        weights = (jnp.where(first, weights, 0.0), jnp.where(first, 0.0, weights))
        for a in range(kv_local):
            here = slice(a * group, (a + 1) * group)
            part_top_ref[j, here] = jnp.broadcast_to(tops[a], narrow)
            part_total_ref[j, here] = jnp.broadcast_to(jnp.sum(weights[a], axis=1, keepdims=True), narrow)
        return jnp.concatenate(weights, axis=0).astype(jnp.bfloat16)

    def turn(stages, i, carry):
        merged, weighed, scored = (entries(jnp.maximum(i - back, 0)) for back in (2, 1, 0))
        for t in range(TASKS):
            task = slice(t * GROUP, (t + 1) * GROUP)
            for start in range(t * GROUP, (t + 1) * GROUP, SETS):
                merge_slots(
                    [jnp.where(i >= 2, row_of(entry), rows) for entry in merged[start : start + SETS]], start
                )
            if stages > 1:
                weights = [weigh_item(entry, t, k) for k, entry in enumerate(weighed[task])]
                part_sum_ref[t] = jnp.dot(
                    jnp.concatenate(weights, axis=0),
                    value_ref[block_of(weighed[task][0])],
                    preferred_element_type=jnp.float32,
                )
            if stages > 2:
                score_ref[t] = lax.dot_general(
                    jnp.concatenate([query_ref[row_of(entry)] for entry in scored[task]], axis=0),
                    key_ref[block_of(scored[task][0])],
                    (((1,), (1,)), ((), ())),
                    preferred_element_type=jnp.float32,
                )
        return carry

    for copy in numbers:
        copy.wait()
    for part in range(PHASES):
        for copy in copies[part]:
            copy.wait()
        for pair in copies[part + AHEAD : part + AHEAD + 1]:
            for copy in pair:
                copy.start()
        lax.fori_loop(bound_ref[0, part], bound_ref[0, part + 1], functools.partial(turn, 3), 0)
    last = bound_ref[0, PHASES]
    turn(2, last, 0)
    turn(1, last + 1, 0)

    square = (own * heads, LANES)
    eye = lax.broadcasted_iota(jnp.int32, square, 0) == lax.broadcasted_iota(jnp.int32, square, 1)
    line = lax.broadcasted_iota(jnp.int32, wide, 0)
    for q in range(count):
        ref = (keep_ref, send_ref)[q % PAIR]
        mine = slice(q * own, (q + 1) * own)
        tops = [top_ref[mine] for top_ref, _, _ in states]
        high = functools.reduce(jnp.maximum, tops)
        shares = [jnp.exp2((top - high) * factor) for top in tops]
        total = sum(total_ref[mine] * share for (_, total_ref, _), share in zip(states, shares))
        ref[q // PAIR, :own] = sum(sum_ref[mine] * share for (_, _, sum_ref), share in zip(states, shares))
        high, total = (
            jnp.sum(jnp.where(eye, x.reshape(square), 0.0), axis=0, keepdims=True) for x in (high, total)
        )
        ref[q // PAIR, own] = jnp.where(line == 0, high, jnp.where(line == 1, total, 0.0))


def attend(items, bounds, queries, keys, values, kv_local, scale):
    _, own, heads, _ = queries[0].shape
    count = len(queries) * PAIR
    rows = count * own
    tokens = keys.shape[1]
    keys, values = in_hbm(keys, values)
    state = pltpu.VMEM((rows + 1, heads, LANES), jnp.float32)
    part = pltpu.VMEM((CHUNK, heads, LANES), jnp.float32)
    return pl.pallas_call(
        functools.partial(attend_kernel, scale, kv_local, count),
        in_specs=[vmem_spec()] * (2 + len(queries)) + [hbm_spec()] * 2,
        out_specs=[vmem_spec()] * PAIR,
        out_shape=[jax.ShapeDtypeStruct((count // PAIR, own + 1, heads, LANES), jnp.float32)] * PAIR,
        scratch_shapes=[
            pltpu.SMEM(items.shape, items.dtype),
            pltpu.SMEM(bounds.shape, bounds.dtype),
            pltpu.VMEM((rows + 1, heads, LANES), jnp.bfloat16),
            pltpu.VMEM(keys.shape, keys.dtype),
            pltpu.VMEM(values.shape, values.dtype),
            pltpu.VMEM((TASKS, GROUP * heads, tokens), jnp.float32),
            part,
            part,
            pltpu.VMEM((TASKS, GROUP * heads, LANES), jnp.float32),
            pltpu.SemaphoreType.DMA((2,)),
            pltpu.SemaphoreType.DMA((2, PHASES)),
        ]
        + [state] * (3 * SETS),
        compiler_params=params(28 + 3 * SETS * rows * heads * LANES * 4 // MIB),
        name="attend",
    )(items, bounds, *queries, keys, values)


def merge_pair_kernel(scale, keep_ref, got_ref, out_ref):
    chips, sections, heads, _ = keep_ref.shape
    own = sections - 1
    factor = scale * LOG2E
    line = lax.broadcasted_iota(jnp.int32, (heads, LANES), 0)
    shares, stats = [], []
    for s in range(chips):
        keep, got = keep_ref[s, own], got_ref[s, own]
        high = jnp.maximum(keep[0:1], got[0:1])
        pair = [jnp.exp2((x[0:1] - high) * factor) for x in (keep, got)]
        shares += pair
        total = pair[0] * keep[1:2] + pair[1] * got[1:2]
        stat = jnp.zeros((heads, LANES), jnp.float32)
        for position, piece in enumerate(split3(high) + split3(total)):
            stat = jnp.where(line == position, piece, stat)
        stats.append(stat)
    columns = jnp.concatenate(shares, axis=0).T
    flat = (own * heads, LANES)
    for s in range(chips):
        total = keep_ref[s, :own].reshape(flat) * columns[:, PAIR * s : PAIR * s + 1]
        total = total + got_ref[s, :own].reshape(flat) * columns[:, PAIR * s + 1 : PAIR * s + 2]
        out_ref[s, :own] = total.astype(jnp.bfloat16).reshape(own, heads, LANES)
        out_ref[s, own] = stats[s].astype(jnp.bfloat16)


def merge_pair(keep, got, scale):
    return pl.pallas_call(
        functools.partial(merge_pair_kernel, scale),
        in_specs=[vmem_spec()] * 2,
        out_specs=vmem_spec(),
        out_shape=jax.ShapeDtypeStruct(keep.shape, jnp.bfloat16),
        compiler_params=params(16),
        name="merge_pair",
    )(keep, got)


def merge_kernel(scale, *refs):
    pieces, (out_ref, wide_ref) = refs[:-2], refs[-2:]
    chips, sections, heads, _ = pieces[0].shape
    own = sections - 1
    factor = scale * LOG2E
    shares = []
    for s in range(chips):
        stats = [pieces[j][s ^ j, own].astype(jnp.float32) for j in range(chips)]
        tops = jnp.concatenate([x[0:1] + x[1:2] + x[2:3] for x in stats], axis=0)
        totals = jnp.concatenate([x[3:4] + x[4:5] + x[5:6] for x in stats], axis=0)
        weights = jnp.exp2((tops - jnp.max(tops, axis=0, keepdims=True)) * factor)
        shares.append(weights / jnp.sum(weights * totals, axis=0, keepdims=True))
    columns = jnp.concatenate(shares, axis=0).T
    flat = own * heads
    for s in range(chips):
        total = jnp.zeros((flat, LANES), jnp.float32)
        for j in range(chips):
            part = pieces[j][s ^ j, :own].astype(jnp.float32).reshape(flat, LANES)
            total = total + part * columns[:, s * chips + j : s * chips + j + 1]
        wide_ref[s * flat : (s + 1) * flat, :] = total
    rows = [wide_ref[pl.ds(h, chips * own, stride=heads), :] for h in range(heads)]
    out_ref[...] = jnp.concatenate(rows, axis=1).astype(jnp.bfloat16)


def merge(pieces, scale):
    chips, sections, heads, _ = pieces[0].shape
    own = sections - 1
    return pl.pallas_call(
        functools.partial(merge_kernel, scale),
        in_specs=[vmem_spec()] * chips,
        out_specs=vmem_spec(),
        out_shape=jax.ShapeDtypeStruct((chips * own, heads * LANES), jnp.bfloat16),
        scratch_shapes=[pltpu.VMEM((chips * own * heads, LANES), jnp.float32)],
        compiler_params=params(32),
        name="merge",
    )(*pieces)


def output_kernel(own, *refs):
    pieces, weight_ref = refs[:PAIR], refs[PAIR]
    outs, (rows_ref, terms_ref) = refs[PAIR + 1 : -2], refs[-2:]
    me = lax.axis_index("kv")
    for t in range(PAIR):
        piece = pieces[t][...].astype(jnp.float32)
        for s in range(piece.shape[0] // own):
            start = pl.multiple_of(jnp.bitwise_xor(me, PAIR * s + t) * own, own)
            rows_ref[pl.ds(start, own), :] = piece[s * own : (s + 1) * own]
    terms_ref[...] = jnp.dot(
        rows_ref[...].astype(jnp.bfloat16), weight_ref[...], preferred_element_type=jnp.float32
    )
    me = lax.axis_index("row")
    part = outs[0].shape[0]
    for s, ref in enumerate(outs):
        start = pl.multiple_of(jnp.bitwise_xor(me, s) * part, part)
        ref[...] = terms_ref[pl.ds(start, part), :].astype(ref.dtype)


def project_out(pieces, weight, own, row_count):
    half, width = pieces[0].shape
    rows, columns = PAIR * half, weight.shape[1]
    shape = (rows // row_count, columns)
    send = jax.ShapeDtypeStruct(shape, jnp.bfloat16)
    return pl.pallas_call(
        functools.partial(output_kernel, own),
        in_specs=[vmem_spec()] * (PAIR + 1),
        out_specs=[vmem_spec()] * row_count,
        out_shape=[jax.ShapeDtypeStruct(shape, jnp.float32)] + [send] * (row_count - 1),
        scratch_shapes=[pltpu.VMEM((rows, width), jnp.float32), pltpu.VMEM((rows, columns), jnp.float32)],
        compiler_params=params(24),
        name="project_out",
    )(*pieces, weight)


def exchange(x, axis, s):
    count = lax.axis_size(axis)
    return lax.ppermute(x, axis, [(i, i ^ s) for i in range(count)])


def gather_chips(x):
    return [x] + [exchange(x, "kv", s) for s in range(PAIR, lax.axis_size("kv"), PAIR)]


def local(
    hidden,
    query_weight,
    adapter_down_weight,
    adapter_up_weight,
    query_norm_gain,
    paged_key_cache,
    paged_value_cache,
    output_weight,
    holder,
    holder_block_index,
    block_used_length,
    tenant,
    tenant_adapter,
):
    own, slots = holder.shape
    rows, depth = hidden.shape
    kv_count = lax.axis_size("kv")
    row_count = lax.axis_size("row")
    adapters, _, rank = adapter_down_weight.shape
    width = query_weight.shape[1]
    head_size = query_norm_gain.shape[0]
    heads = width // head_size
    blocks, block_size, kv_local, _ = paged_key_cache.shape
    scale = 1.0 / math.sqrt(head_size)

    chips = kv_count // PAIR
    keep, send, up = project(
        tenant,
        tenant_adapter,
        holder,
        holder_block_index,
        block_used_length,
        hidden,
        query_weight,
        jnp.swapaxes(adapter_down_weight, 1, 2).reshape(adapters * rank, depth),
        adapter_up_weight,
        rank,
        chips,
    )
    parts = add_pair(keep, exchange(send, "kv", 1), 3 * slots)
    parts = [parts[0]] + [exchange(parts[s], "kv", PAIR * s) for s in range(1, chips)]

    position = (jnp.sum(block_used_length, axis=1) - 1).astype(jnp.float32)
    half = head_size // 2
    frequency = ROPE_BASE ** (-(jnp.arange(half, dtype=jnp.float32) * 2.0) / head_size)
    angles = position[:, None] * frequency[None, :]
    cosine = jnp.concatenate([jnp.cos(angles), jnp.cos(angles)], axis=-1)
    sine = jnp.concatenate([-jnp.sin(angles), jnp.sin(angles)], axis=-1)
    queries = make_queries(parts, up, cosine, sine, query_norm_gain.reshape(1, head_size), heads, 3 * slots)
    places, slot_values, bounds = make_places(parts, slots, blocks, block_size, kv_count)
    queries = gather_chips(join_pair(queries, exchange(queries, "kv", 1), places))
    queries = [q.reshape(PAIR, own, heads, head_size) for q in queries]
    items = make_list(places, slot_values, blocks, block_size, kv_count)

    keys = paged_key_cache.reshape(blocks, block_size * kv_local, head_size)
    values = paged_value_cache.reshape(blocks, block_size * kv_local, head_size)
    keep, send = attend(items, bounds, queries, keys, values, kv_local, scale)
    merged = merge_pair(keep, exchange(send, "kv", 1), scale)
    attention = merge(gather_chips(merged), scale)
    terms = project_out([attention, exchange(attention, "kv", 1)], output_weight, own, row_count)
    total = terms[0]
    for s in range(1, row_count):
        total = total + exchange(terms[s], "row", s).astype(jnp.float32)
    return total.astype(jnp.bfloat16)


def solution(mesh):
    return jax.shard_map(
        local,
        mesh=mesh,
        in_specs=(
            P(None, "kv"),
            P("kv", "row"),
            P(None, "kv", None),
            P(None, None, "row"),
            P(),
            P("kv", None, "row", None),
            P("kv", None, "row", None),
            P("row", "kv"),
            P("kv", None),
            P("kv", None),
            P("kv", None),
            P(),
            P(),
        ),
        out_specs=P("row", "kv"),
        check_vma=False,
    )
```

```python
import functools
import math

import jax
import jax.numpy as jnp
from jax import lax
from jax.experimental import pallas as pl
from jax.experimental.pallas import tpu as pltpu
from jax.sharding import PartitionSpec as P

ADAPTER_SCALE = 0.5
ROPE_BASE = 1000000.0
EPSILON = 1e-06
NEG_FILL = -1e30
LANES = 128
COLUMN_TILE = 256
PAIR = 2
GROUP = 4
TASKS = 8
CHUNK = GROUP * TASKS
SETS = 2
PHASES = 16
AHEAD = 6
DEPTH = 256
LOG2E = math.log2(math.e)
MIB = 1024 * 1024


def params(mib):
    return pltpu.CompilerParams(vmem_limit_bytes=mib * MIB)


def vmem_spec():
    return pl.BlockSpec(memory_space=pltpu.VMEM)


def in_hbm(*arrays):
    return [pltpu.with_memory_space_constraint(x, pltpu.HBM) for x in arrays]


def hbm_spec():
    return pl.BlockSpec(memory_space=pltpu.HBM)


def split3(x):
    high = x.astype(jnp.bfloat16).astype(jnp.float32)
    rest = x - high
    middle = rest.astype(jnp.bfloat16).astype(jnp.float32)
    return high, middle, (rest - middle).astype(jnp.bfloat16).astype(jnp.float32)


def to_column(row, count):
    shape = (count, count)
    eye = lax.broadcasted_iota(jnp.int32, shape, 0) == lax.broadcasted_iota(jnp.int32, shape, 1)
    return jnp.sum(jnp.where(eye, row.astype(jnp.float32), 0.0), axis=1, keepdims=True)


def project_kernel(
    rank,
    tenant_hbm,
    adapter_hbm,
    tenant_row_hbm,
    adapter_row_hbm,
    holder_hbm,
    block_hbm,
    length_hbm,
    hidden_hbm,
    weight_hbm,
    down_hbm,
    up_hbm,
    keep_ref,
    send_ref,
    own_up_ref,
    tenant_ref,
    adapter_ref,
    holder_ref,
    block_ref,
    length_ref,
    hidden_ref,
    weight_ref,
    down_ref,
    total_ref,
    tenant_smem,
    adapter_smem,
    sems,
    up_sems,
    small_sems,
):
    chips, own, _ = keep_ref.shape
    rows, depth = hidden_ref.shape
    width = weight_ref.shape[1]
    spans = [slice(i, min(i + DEPTH, depth)) for i in range(0, depth, DEPTH)]
    first = [
        pltpu.make_async_copy(hidden_hbm, hidden_ref, sems.at[0]),
        pltpu.make_async_copy(down_hbm, down_ref, sems.at[1]),
    ]
    chunks = [
        pltpu.make_async_copy(weight_hbm.at[span], weight_ref.at[span], sems.at[2 + i])
        for i, span in enumerate(spans)
    ]
    scalars = [
        pltpu.make_async_copy(tenant_hbm, tenant_smem, up_sems.at[own]),
        pltpu.make_async_copy(adapter_hbm, adapter_smem, up_sems.at[own + 1]),
    ]
    small = [
        pltpu.make_async_copy(hbm, ref, small_sems.at[i])
        for i, (hbm, ref) in enumerate(
            (
                (tenant_row_hbm, tenant_ref),
                (adapter_row_hbm, adapter_ref),
                (holder_hbm, holder_ref),
                (block_hbm, block_ref),
                (length_hbm, length_ref),
            )
        )
    ]
    for copy in scalars + small + first + chunks:
        copy.start()
    for copy in small:
        copy.wait()

    slots = holder_ref.shape[1]
    numbers = [holder_ref[...], block_ref[...], length_ref[...], jnp.zeros((own, LANES - 3 * slots), jnp.int32)]
    numbers = jnp.concatenate(numbers, axis=1).astype(jnp.float32)
    tenants = adapter_ref.shape[1]
    tenant = to_column(tenant_ref[...], rows)
    pick = lax.broadcasted_iota(jnp.int32, (rows, tenants), 1).astype(jnp.float32) == tenant
    adapter = jnp.sum(jnp.where(pick, adapter_ref[...].astype(jnp.float32), 0.0), axis=1, keepdims=True).astype(
        jnp.int32
    )
    me = lax.axis_index("kv")
    even = me % PAIR == 0
    for copy in scalars:
        copy.wait()
    ups = [
        pltpu.make_async_copy(
            up_hbm.at[adapter_smem[tenant_smem[me * own + r]]], own_up_ref.at[r], up_sems.at[r]
        )
        for r in range(own)
    ]
    for copy in ups:
        copy.start()

    def store(columns, total):
        total = total.reshape(chips, PAIR, own, total.shape[1])
        keep_ref[:, :, columns] = jnp.where(even, total[:, 0], total[:, 1])
        send_ref[:, :, columns] = jnp.where(even, total[:, 1], total[:, 0])

    for copy in first:
        copy.wait()
    hidden = hidden_ref[...]
    low = lax.dot_general(hidden, down_ref[...], (((1,), (1,)), ((), ())), preferred_element_type=jnp.float32)
    column = lax.broadcasted_iota(jnp.int32, low.shape, 1)
    low = jnp.where((column >= adapter * rank) & (column < adapter * rank + rank), low, 0.0)
    low = sum(low[:, i : i + LANES] for i in range(LANES, low.shape[1], LANES)) + low[:, :LANES]
    shift = LANES // 2
    while shift >= rank:
        low = low + pltpu.roll(low, shift, 1)
        shift //= 2
    lane = lax.broadcasted_iota(jnp.int32, (rows, LANES), 1)
    numbers = jnp.concatenate([numbers] * (rows // own), axis=0)
    store(slice(width, width + LANES), jnp.where(lane < 3 * slots, numbers, low))
    for i, (span, copy) in enumerate(zip(spans, chunks)):
        copy.wait()
        for start in range(0, width, COLUMN_TILE):
            tile = slice(start, start + COLUMN_TILE)
            total = jnp.dot(hidden[:, span], weight_ref[span, tile], preferred_element_type=jnp.float32)
            if i > 0:
                total = total_ref[:, tile] + total
            if i < len(chunks) - 1:
                total_ref[:, tile] = total
            else:
                store(tile, total)
    for copy in ups:
        copy.wait()


def project(tenant, tenant_adapter, holder, block, length, hidden, query_weight, down, up, rank, chips):
    rows, depth = hidden.shape
    width = query_weight.shape[1]
    own = rows // chips // PAIR
    out = jax.ShapeDtypeStruct((chips, own, width + LANES), jnp.float32)
    tables = [x.reshape(1, -1) for x in (tenant, tenant_adapter)]
    operands = in_hbm(tenant, tenant_adapter, *tables, holder, block, length, hidden, query_weight, down, up)
    local = operands[2:10]
    return pl.pallas_call(
        functools.partial(project_kernel, rank),
        in_specs=[hbm_spec()] * len(operands),
        out_specs=[vmem_spec()] * 3,
        out_shape=[out, out, jax.ShapeDtypeStruct((own, *up.shape[1:]), up.dtype)],
        scratch_shapes=[pltpu.VMEM(x.shape, x.dtype) for x in local]
        + [
            pltpu.VMEM((rows, width), jnp.float32),
            pltpu.SMEM(tenant.shape, tenant.dtype),
            pltpu.SMEM(tenant_adapter.shape, tenant_adapter.dtype),
            pltpu.SemaphoreType.DMA((2 + pl.cdiv(depth, DEPTH),)),
            pltpu.SemaphoreType.DMA((own + 2,)),
            pltpu.SemaphoreType.DMA((5,)),
        ],
        compiler_params=params(16),
        name="project",
    )(*operands)


def pair_kernel(number_lanes, keep_ref, got_ref, *out_refs):
    chips, own, width = keep_ref.shape
    width = width - LANES
    chip = lax.axis_index("kv") // PAIR
    lane = lax.broadcasted_iota(jnp.int32, (own, LANES), 1)
    for s, ref in enumerate(out_refs):
        c = jnp.bitwise_xor(chip, s)
        ref[:, :width] = keep_ref[c, :, :width] + got_ref[c, :, :width]
        keep = keep_ref[c, :, width:]
        ref[:, width : width + LANES] = jnp.where(lane < number_lanes, keep, keep + got_ref[c, :, width:])
        ref[:, width + LANES :] = got_ref[c, :, width:]


def add_pair(keep, got, number_lanes):
    chips, own, width = keep.shape
    return pl.pallas_call(
        functools.partial(pair_kernel, number_lanes),
        in_specs=[vmem_spec()] * 2,
        out_specs=[vmem_spec()] * chips,
        out_shape=[jax.ShapeDtypeStruct((own, width + LANES), jnp.float32)] * chips,
        compiler_params=params(16),
        name="add_pair",
    )(keep, got)


def queries_kernel(number_lanes, *refs):
    parts, (up_ref, cosine_ref, sine_ref, gain_ref, out_ref, turned_ref) = refs[:-6], refs[-6:]
    own, rank, width = up_ref.shape
    heads = turned_ref.shape[1]

    def whole(columns):
        total = parts[0][:, columns]
        for part in parts[1:]:
            total = total + part[:, columns]
        return total

    low = whole(slice(width, width + LANES)) * ADAPTER_SCALE
    line = lax.broadcasted_iota(jnp.int32, (rank, LANES), 0)
    lane = lax.broadcasted_iota(jnp.int32, (rank, LANES), 1)
    low = [
        jnp.sum(jnp.where(lane == line + number_lanes, low[r : r + 1], 0.0), axis=1, keepdims=True)
        for r in range(own)
    ]
    row = lax.broadcasted_iota(jnp.int32, (own, LANES), 0)
    cosine, sine, gain = cosine_ref[...], sine_ref[...], gain_ref[...]
    for h in range(heads):
        columns = slice(h * LANES, (h + 1) * LANES)
        query = whole(columns)
        adapted = jnp.zeros((own, LANES), jnp.float32)
        for r in range(own):
            adapted = jnp.where(row == r, jnp.sum(up_ref[r, :, columns] * low[r], axis=0, keepdims=True), adapted)
        query = query + adapted
        square = jnp.mean(query * query, axis=-1, keepdims=True)
        query = query * lax.rsqrt(square + EPSILON) * gain
        turned_ref[:, h, :] = query * cosine + pltpu.roll(query, LANES // 2, 1) * sine
    out_ref[...] = turned_ref[...].astype(jnp.bfloat16)


def make_queries(parts, up, cosine, sine, gain, heads, number_lanes):
    own = parts[0].shape[0]
    shape = (own, heads, LANES)
    return pl.pallas_call(
        functools.partial(queries_kernel, number_lanes),
        in_specs=[vmem_spec()] * (len(parts) + 4),
        out_specs=vmem_spec(),
        out_shape=jax.ShapeDtypeStruct(shape, jnp.bfloat16),
        scratch_shapes=[pltpu.VMEM(shape, jnp.float32)],
        compiler_params=params(16),
        name="queries",
    )(*parts, up, cosine, sine, gain)


def place_kernel(blocks, block_size, slots, *refs):
    pieces, (place_ref, value_ref, bound_ref) = refs[:-3], refs[-3:]
    rows = place_ref.shape[0]
    me = lax.axis_index("kv").astype(jnp.float32)
    numbers = jnp.concatenate([p[:, i * LANES : (i + 1) * LANES] for p in pieces for i in range(PAIR)], axis=0)
    holder, block, length = (numbers[:, i * slots : (i + 1) * slots] for i in range(3))
    row = lax.broadcasted_iota(jnp.int32, (rows, slots), 0).astype(jnp.float32)
    spare = float(rows * blocks * block_size)
    value_ref[...] = (row * blocks + block) * block_size + (length - 1.0) - spare
    mine = holder == me
    key = jnp.where(mine, block, -1.0)

    def before(count, axis):
        first = lax.broadcasted_iota(jnp.int32, (count, count), axis)
        return jnp.where(first < lax.broadcasted_iota(jnp.int32, (count, count), 1 - axis), 1.0, 0.0).astype(
            jnp.bfloat16
        )

    lane = lax.broadcasted_iota(jnp.int32, (rows, blocks), 1).astype(jnp.float32)
    picks = [jnp.where(key[:, j : j + 1] == lane, 1.0, 0.0) for j in range(slots)]
    count = jnp.sum(functools.reduce(jnp.add, picks), axis=0, keepdims=True)
    tasks = jnp.floor((count + (GROUP - 1)) * (1.0 / GROUP))
    earlier = jnp.dot(
        jnp.broadcast_to(tasks, (8, blocks)).astype(jnp.bfloat16),
        before(blocks, 0),
        preferred_element_type=jnp.float32,
    )[:1]
    base = earlier * GROUP
    row_before = before(rows, 1)
    slot = lax.broadcasted_iota(jnp.int32, (rows, slots), 1)
    place = jnp.full((rows, slots), -1.0, jnp.float32)
    for j in range(slots):
        above = jnp.dot(row_before, picks[j].astype(jnp.bfloat16), preferred_element_type=jnp.float32)
        here = jnp.sum(picks[j] * (above + base), axis=1, keepdims=True)
        place = jnp.where((slot == j) & mine, here, place)
        base = base + jnp.sum(picks[j], axis=0, keepdims=True)
    place_ref[...] = place
    size = blocks // PHASES
    end = earlier + tasks
    block_lane = lax.broadcasted_iota(jnp.int32, (1, blocks), 1)
    bound_lane = lax.broadcasted_iota(jnp.int32, (1, LANES), 1)
    bounds = jnp.zeros((1, LANES), jnp.float32)
    for part in range(PHASES):
        done = jnp.sum(jnp.where(block_lane == (part + 1) * size - 1, end, 0.0), axis=1, keepdims=True)
        done = done * (1.0 / TASKS)
        done = jnp.ceil(done) if part == PHASES - 1 else jnp.floor(done)
        bounds = jnp.where(bound_lane == part + 1, done, bounds)
    bound_ref[...] = bounds.astype(jnp.int32)


def list_kernel(spare, place_ref, value_ref, joined_ref, list_ref):
    rows, slots = place_ref.shape
    capacity = list_ref.shape[1]
    target = lax.broadcasted_iota(jnp.int32, (8, capacity), 1).astype(jnp.float32)

    def tile(t, total):
        here = pl.ds(pl.multiple_of(t * 8, 8), 8)
        places, values = place_ref[here, :], value_ref[here, :]
        for j in range(slots):
            total = total + jnp.where(places[:, j : j + 1] == target, values[:, j : j + 1], 0.0)
        return total

    total = lax.fori_loop(0, rows // 8, tile, jnp.zeros((8, capacity), jnp.float32))
    list_ref[...] = (jnp.sum(total, axis=0, keepdims=True) + spare).astype(jnp.int32)


def make_places(parts, slots, blocks, block_size, count):
    own, width = parts[0].shape
    rows = count * own
    last = width // (PAIR * LANES) - 1
    table = jax.ShapeDtypeStruct((rows, slots), jnp.float32)
    bounds = jax.ShapeDtypeStruct((1, LANES), jnp.int32)
    return pl.pallas_call(
        functools.partial(place_kernel, blocks, block_size, slots),
        grid=(1,),
        in_specs=[pl.BlockSpec((own, PAIR * LANES), lambda i: (0, last))] * len(parts),
        out_specs=[pl.BlockSpec(x.shape, lambda i: (0, 0)) for x in (table, table, bounds)],
        out_shape=[table, table, bounds],
        compiler_params=params(16),
        cost_estimate=pl.CostEstimate(flops=10**8, bytes_accessed=4 * 10**6, transcendentals=0),
        name="slot_places",
    )(*parts)


def make_list(places, values, joined, blocks, block_size, count):
    rows, slots = places.shape
    most = 2 * rows * slots // count // count * count + (GROUP - 1) * blocks + 3 * CHUNK
    capacity = -(-most // LANES) * LANES
    return pl.pallas_call(
        functools.partial(list_kernel, float(rows * blocks * block_size)),
        in_specs=[vmem_spec()] * 3,
        out_specs=vmem_spec(),
        out_shape=jax.ShapeDtypeStruct((1, capacity), jnp.int32),
        compiler_params=params(16),
        cost_estimate=pl.CostEstimate(flops=10**8, bytes_accessed=4 * 10**6, transcendentals=0),
        name="slot_list",
    )(places, values, joined)


def join_kernel(*refs):
    pieces, out_ref = refs[:-2], refs[-1]
    for s, piece in enumerate(pieces):
        out_ref[s] = piece[...]


def join(pieces, places):
    return pl.pallas_call(
        join_kernel,
        in_specs=[vmem_spec()] * (len(pieces) + 1),
        out_specs=vmem_spec(),
        out_shape=jax.ShapeDtypeStruct((len(pieces), *pieces[0].shape), pieces[0].dtype),
        compiler_params=params(16),
        name="join",
    )(*pieces, places)


def attend_kernel(scale, kv_local, count, list_vmem, bound_vmem, *refs):
    queries, refs = refs[:PAIR], refs[PAIR:]
    (key_hbm, value_hbm, keep_ref, send_ref, list_ref, bound_ref, query_ref, key_ref, value_ref) = refs[:9]
    (score_ref, part_top_ref, part_total_ref, part_sum_ref, number_sems, sems) = refs[9:15]
    states = [refs[15 + 3 * k : 18 + 3 * k] for k in range(SETS)]
    heads = query_ref.shape[1]
    rows = query_ref.shape[0] - 1
    own = rows // count
    blocks, tokens, _ = key_ref.shape
    block_size = tokens // kv_local
    length_bits = (block_size - 1).bit_length()
    block_bits = (blocks - 1).bit_length()
    numbers = (
        pltpu.make_async_copy(list_vmem, list_ref, number_sems.at[0]),
        pltpu.make_async_copy(bound_vmem, bound_ref, number_sems.at[1]),
    )
    size = blocks // PHASES
    spans = [pl.ds(part * size, size) for part in range(PHASES)]
    copies = [
        (
            pltpu.make_async_copy(key_hbm.at[span], key_ref.at[span], sems.at[0, part]),
            pltpu.make_async_copy(value_hbm.at[span], value_ref.at[span], sems.at[1, part]),
        )
        for part, span in enumerate(spans)
    ]
    for pair in (copies[0], numbers, *copies[1:AHEAD]):
        for copy in pair:
            copy.start()

    factor = scale * LOG2E
    for t, piece in enumerate(queries):
        for s in range(count // PAIR):
            start = (PAIR * s + t) * own
            query_ref[start : start + own] = piece[s]
    query_ref[rows] = jnp.zeros((heads, LANES), jnp.bfloat16)
    for state in states:
        for ref, value in zip(state, (NEG_FILL, 0.0, 0.0)):
            ref[...] = jnp.full(ref.shape, value, jnp.float32)
    for ref in (score_ref, part_top_ref, part_total_ref, part_sum_ref):
        ref[...] = jnp.zeros(ref.shape, jnp.float32)
    group = heads // kv_local
    column = lax.broadcasted_iota(jnp.int32, (group, tokens), 1)
    first = column % kv_local == 0
    wide = (heads, LANES)
    narrow = (group, LANES)

    def entries(chunk):
        return [list_ref[0, chunk * CHUNK + j] for j in range(CHUNK)]

    def row_of(entry):
        return entry >> (length_bits + block_bits)

    def block_of(entry):
        return (entry >> length_bits) & (blocks - 1)

    def merge_slots(row, start):
        before = [[ref[r] for ref in state] for r, state in zip(row, states)]
        after = []
        for k, (top, total, acc) in enumerate(before):
            t, place = divmod(start + k, GROUP)
            part_top = part_top_ref[start + k]
            share = jnp.exp2(-jnp.abs(top - part_top) * factor)
            lower = top < part_top
            old, new = jnp.where(lower, share, 1.0), jnp.where(lower, 1.0, share)
            after.append(
                (
                    jnp.maximum(top, part_top),
                    total * old + part_total_ref[start + k] * new,
                    acc * old + part_sum_ref[t, place * heads : (place + 1) * heads] * new,
                )
            )
        for r, state, new in zip(row, states, after):
            for ref, value in zip(state, new):
                ref[r] = value

    def weigh_item(entry, t, k):
        j = t * GROUP + k
        start = k * heads
        scores = jnp.where(
            first, score_ref[t, start : start + group], score_ref[t, start + group : start + heads]
        )
        length = (entry & (block_size - 1)) + 1
        scores = jnp.where(column < length * kv_local, scores, NEG_FILL)
        tops = [
            jnp.max(x, axis=1, keepdims=True)
            for x in (jnp.where(first, scores, NEG_FILL), jnp.where(first, NEG_FILL, scores))
        ]
        weights = jnp.exp2((scores - jnp.where(first, tops[0], tops[1])) * factor)
        weights = (jnp.where(first, weights, 0.0), jnp.where(first, 0.0, weights))
        for a in range(kv_local):
            here = slice(a * group, (a + 1) * group)
            part_top_ref[j, here] = jnp.broadcast_to(tops[a], narrow)
            part_total_ref[j, here] = jnp.broadcast_to(jnp.sum(weights[a], axis=1, keepdims=True), narrow)
        return jnp.concatenate(weights, axis=0).astype(jnp.bfloat16)

    def turn(stages, i, carry):
        merged, weighed, scored = (entries(jnp.maximum(i - back, 0)) for back in (2, 1, 0))
        for t in range(TASKS):
            task = slice(t * GROUP, (t + 1) * GROUP)
            for start in range(t * GROUP, (t + 1) * GROUP, SETS):
                merge_slots(
                    [jnp.where(i >= 2, row_of(entry), rows) for entry in merged[start : start + SETS]], start
                )
            if stages > 1:
                weights = [weigh_item(entry, t, k) for k, entry in enumerate(weighed[task])]
                part_sum_ref[t] = jnp.dot(
                    jnp.concatenate(weights, axis=0),
                    value_ref[block_of(weighed[task][0])],
                    preferred_element_type=jnp.float32,
                )
            if stages > 2:
                score_ref[t] = lax.dot_general(
                    jnp.concatenate([query_ref[row_of(entry)] for entry in scored[task]], axis=0),
                    key_ref[block_of(scored[task][0])],
                    (((1,), (1,)), ((), ())),
                    preferred_element_type=jnp.float32,
                )
        return carry

    for copy in numbers:
        copy.wait()
    for part in range(PHASES):
        for copy in copies[part]:
            copy.wait()
        for pair in copies[part + AHEAD : part + AHEAD + 1]:
            for copy in pair:
                copy.start()
        lax.fori_loop(bound_ref[0, part], bound_ref[0, part + 1], functools.partial(turn, 3), 0)
    last = bound_ref[0, PHASES]
    turn(2, last, 0)
    turn(1, last + 1, 0)

    square = (own * heads, LANES)
    eye = lax.broadcasted_iota(jnp.int32, square, 0) == lax.broadcasted_iota(jnp.int32, square, 1)
    line = lax.broadcasted_iota(jnp.int32, wide, 0)
    for q in range(count):
        ref = (keep_ref, send_ref)[q % PAIR]
        mine = slice(q * own, (q + 1) * own)
        tops = [top_ref[mine] for top_ref, _, _ in states]
        high = functools.reduce(jnp.maximum, tops)
        shares = [jnp.exp2((top - high) * factor) for top in tops]
        total = sum(total_ref[mine] * share for (_, total_ref, _), share in zip(states, shares))
        ref[q // PAIR, :own] = sum(sum_ref[mine] * share for (_, _, sum_ref), share in zip(states, shares))
        high, total = (
            jnp.sum(jnp.where(eye, x.reshape(square), 0.0), axis=0, keepdims=True) for x in (high, total)
        )
        ref[q // PAIR, own] = jnp.where(line == 0, high, jnp.where(line == 1, total, 0.0))


def attend(items, bounds, queries, keys, values, kv_local, scale):
    chips, own, heads, _ = queries[0].shape
    count = chips * PAIR
    rows = count * own
    tokens = keys.shape[1]
    keys, values = in_hbm(keys, values)
    state = pltpu.VMEM((rows + 1, heads, LANES), jnp.float32)
    part = pltpu.VMEM((CHUNK, heads, LANES), jnp.float32)
    return pl.pallas_call(
        functools.partial(attend_kernel, scale, kv_local, count),
        in_specs=[vmem_spec()] * (2 + len(queries)) + [hbm_spec()] * 2,
        out_specs=[vmem_spec()] * PAIR,
        out_shape=[jax.ShapeDtypeStruct((count // PAIR, own + 1, heads, LANES), jnp.float32)] * PAIR,
        scratch_shapes=[
            pltpu.SMEM(items.shape, items.dtype),
            pltpu.SMEM(bounds.shape, bounds.dtype),
            pltpu.VMEM((rows + 1, heads, LANES), jnp.bfloat16),
            pltpu.VMEM(keys.shape, keys.dtype),
            pltpu.VMEM(values.shape, values.dtype),
            pltpu.VMEM((TASKS, GROUP * heads, tokens), jnp.float32),
            part,
            part,
            pltpu.VMEM((TASKS, GROUP * heads, LANES), jnp.float32),
            pltpu.SemaphoreType.DMA((2,)),
            pltpu.SemaphoreType.DMA((2, PHASES)),
        ]
        + [state] * (3 * SETS),
        compiler_params=params(28 + 3 * SETS * rows * heads * LANES * 4 // MIB),
        name="attend",
    )(items, bounds, *queries, keys, values)


def merge_pair_kernel(scale, keep_ref, got_ref, out_ref):
    chips, sections, heads, _ = keep_ref.shape
    own = sections - 1
    factor = scale * LOG2E
    line = lax.broadcasted_iota(jnp.int32, (heads, LANES), 0)
    shares, stats = [], []
    for s in range(chips):
        keep, got = keep_ref[s, own], got_ref[s, own]
        high = jnp.maximum(keep[0:1], got[0:1])
        pair = [jnp.exp2((x[0:1] - high) * factor) for x in (keep, got)]
        shares += pair
        total = pair[0] * keep[1:2] + pair[1] * got[1:2]
        stat = jnp.zeros((heads, LANES), jnp.float32)
        for position, piece in enumerate(split3(high) + split3(total)):
            stat = jnp.where(line == position, piece, stat)
        stats.append(stat)
    columns = jnp.concatenate(shares, axis=0).T
    flat = (own * heads, LANES)
    for s in range(chips):
        total = keep_ref[s, :own].reshape(flat) * columns[:, PAIR * s : PAIR * s + 1]
        total = total + got_ref[s, :own].reshape(flat) * columns[:, PAIR * s + 1 : PAIR * s + 2]
        out_ref[s, :own] = total.astype(jnp.bfloat16).reshape(own, heads, LANES)
        out_ref[s, own] = stats[s].astype(jnp.bfloat16)


def merge_pair(keep, got, scale):
    return pl.pallas_call(
        functools.partial(merge_pair_kernel, scale),
        in_specs=[vmem_spec()] * 2,
        out_specs=vmem_spec(),
        out_shape=jax.ShapeDtypeStruct(keep.shape, jnp.bfloat16),
        compiler_params=params(16),
        name="merge_pair",
    )(keep, got)


def merge_kernel(scale, *refs):
    pieces, (out_ref, wide_ref) = refs[:-2], refs[-2:]
    chips, sections, heads, _ = pieces[0].shape
    own = sections - 1
    factor = scale * LOG2E
    shares = []
    for s in range(chips):
        stats = [pieces[j][s ^ j, own].astype(jnp.float32) for j in range(chips)]
        tops = jnp.concatenate([x[0:1] + x[1:2] + x[2:3] for x in stats], axis=0)
        totals = jnp.concatenate([x[3:4] + x[4:5] + x[5:6] for x in stats], axis=0)
        weights = jnp.exp2((tops - jnp.max(tops, axis=0, keepdims=True)) * factor)
        shares.append(weights / jnp.sum(weights * totals, axis=0, keepdims=True))
    columns = jnp.concatenate(shares, axis=0).T
    flat = own * heads
    for s in range(chips):
        total = jnp.zeros((flat, LANES), jnp.float32)
        for j in range(chips):
            part = pieces[j][s ^ j, :own].astype(jnp.float32).reshape(flat, LANES)
            total = total + part * columns[:, s * chips + j : s * chips + j + 1]
        wide_ref[s * flat : (s + 1) * flat, :] = total
    rows = [wide_ref[pl.ds(h, chips * own, stride=heads), :] for h in range(heads)]
    out_ref[...] = jnp.concatenate(rows, axis=1).astype(jnp.bfloat16)


def merge(pieces, scale):
    chips, sections, heads, _ = pieces[0].shape
    own = sections - 1
    return pl.pallas_call(
        functools.partial(merge_kernel, scale),
        in_specs=[vmem_spec()] * chips,
        out_specs=vmem_spec(),
        out_shape=jax.ShapeDtypeStruct((chips * own, heads * LANES), jnp.bfloat16),
        scratch_shapes=[pltpu.VMEM((chips * own * heads, LANES), jnp.float32)],
        compiler_params=params(32),
        name="merge",
    )(*pieces)


def output_kernel(own, *refs):
    pieces, weight_ref = refs[:PAIR], refs[PAIR]
    outs, (rows_ref, terms_ref) = refs[PAIR + 1 : -2], refs[-2:]
    me = lax.axis_index("kv")
    for t in range(PAIR):
        piece = pieces[t][...].astype(jnp.float32)
        for s in range(piece.shape[0] // own):
            start = pl.multiple_of(jnp.bitwise_xor(me, PAIR * s + t) * own, own)
            rows_ref[pl.ds(start, own), :] = piece[s * own : (s + 1) * own]
    terms_ref[...] = jnp.dot(
        rows_ref[...].astype(jnp.bfloat16), weight_ref[...], preferred_element_type=jnp.float32
    )
    me = lax.axis_index("row")
    part = outs[0].shape[0]
    for s, ref in enumerate(outs):
        start = pl.multiple_of(jnp.bitwise_xor(me, s) * part, part)
        ref[...] = terms_ref[pl.ds(start, part), :].astype(ref.dtype)


def project_out(pieces, weight, own, row_count):
    half, width = pieces[0].shape
    rows, columns = PAIR * half, weight.shape[1]
    shape = (rows // row_count, columns)
    send = jax.ShapeDtypeStruct(shape, jnp.bfloat16)
    return pl.pallas_call(
        functools.partial(output_kernel, own),
        in_specs=[vmem_spec()] * (PAIR + 1),
        out_specs=[vmem_spec()] * row_count,
        out_shape=[jax.ShapeDtypeStruct(shape, jnp.float32)] + [send] * (row_count - 1),
        scratch_shapes=[pltpu.VMEM((rows, width), jnp.float32), pltpu.VMEM((rows, columns), jnp.float32)],
        compiler_params=params(24),
        name="project_out",
    )(*pieces, weight)


def exchange(x, axis, s):
    count = lax.axis_size(axis)
    return lax.ppermute(x, axis, [(i, i ^ s) for i in range(count)])


def gather_chips(x):
    return [x] + [exchange(x, "kv", s) for s in range(PAIR, lax.axis_size("kv"), PAIR)]


def local(
    hidden,
    query_weight,
    adapter_down_weight,
    adapter_up_weight,
    query_norm_gain,
    paged_key_cache,
    paged_value_cache,
    output_weight,
    holder,
    holder_block_index,
    block_used_length,
    tenant,
    tenant_adapter,
):
    own, slots = holder.shape
    rows, depth = hidden.shape
    kv_count = lax.axis_size("kv")
    row_count = lax.axis_size("row")
    adapters, _, rank = adapter_down_weight.shape
    width = query_weight.shape[1]
    head_size = query_norm_gain.shape[0]
    heads = width // head_size
    blocks, block_size, kv_local, _ = paged_key_cache.shape
    scale = 1.0 / math.sqrt(head_size)

    chips = kv_count // PAIR
    keep, send, up = project(
        tenant,
        tenant_adapter,
        holder,
        holder_block_index,
        block_used_length,
        hidden,
        query_weight,
        jnp.swapaxes(adapter_down_weight, 1, 2).reshape(adapters * rank, depth),
        adapter_up_weight,
        rank,
        chips,
    )
    parts = add_pair(keep, exchange(send, "kv", 1), 3 * slots)
    parts = [parts[0]] + [exchange(parts[s], "kv", PAIR * s) for s in range(1, chips)]

    position = (jnp.sum(block_used_length, axis=1) - 1).astype(jnp.float32)
    half = head_size // 2
    frequency = ROPE_BASE ** (-(jnp.arange(half, dtype=jnp.float32) * 2.0) / head_size)
    angles = position[:, None] * frequency[None, :]
    cosine = jnp.concatenate([jnp.cos(angles), jnp.cos(angles)], axis=-1)
    sine = jnp.concatenate([-jnp.sin(angles), jnp.sin(angles)], axis=-1)
    queries = make_queries(parts, up, cosine, sine, query_norm_gain.reshape(1, head_size), heads, 3 * slots)
    places, slot_values, bounds = make_places(parts, slots, blocks, block_size, kv_count)
    queries = join(gather_chips(queries), places)
    items = make_list(places, slot_values, queries, blocks, block_size, kv_count)
    queries = [queries, exchange(queries, "kv", 1)]

    keys = paged_key_cache.reshape(blocks, block_size * kv_local, head_size)
    values = paged_value_cache.reshape(blocks, block_size * kv_local, head_size)
    keep, send = attend(items, bounds, queries, keys, values, kv_local, scale)
    merged = merge_pair(keep, exchange(send, "kv", 1), scale)
    attention = merge(gather_chips(merged), scale)
    terms = project_out([attention, exchange(attention, "kv", 1)], output_weight, own, row_count)
    total = terms[0]
    for s in range(1, row_count):
        total = total + exchange(terms[s], "row", s).astype(jnp.float32)
    return total.astype(jnp.bfloat16)


def solution(mesh):
    return jax.shard_map(
        local,
        mesh=mesh,
        in_specs=(
            P(None, "kv"),
            P("kv", "row"),
            P(None, "kv", None),
            P(None, None, "row"),
            P(),
            P("kv", None, "row", None),
            P("kv", None, "row", None),
            P("row", "kv"),
            P("kv", None),
            P("kv", None),
            P("kv", None),
            P(),
            P(),
        ),
        out_specs=P("row", "kv"),
        check_vma=False,
    )
```

```python
import functools
import math

import jax
import jax.numpy as jnp
from jax import lax
from jax.experimental import pallas as pl
from jax.experimental.pallas import tpu as pltpu
from jax.sharding import PartitionSpec as P

ADAPTER_SCALE = 0.5
ROPE_BASE = 1000000.0
EPSILON = 1e-06
NEG_FILL = -1e30
LANES = 128
COLUMN_TILE = 256
PAIR = 2
GROUP = 4
TASKS = 8
CHUNK = GROUP * TASKS
SETS = 2
PHASES = 8
AHEAD = 4
DEPTH = 256
LOG2E = math.log2(math.e)
MIB = 1024 * 1024


def params(mib):
    return pltpu.CompilerParams(vmem_limit_bytes=mib * MIB)


def vmem_spec():
    return pl.BlockSpec(memory_space=pltpu.VMEM)


def in_hbm(*arrays):
    return [pltpu.with_memory_space_constraint(x, pltpu.HBM) for x in arrays]


def hbm_spec():
    return pl.BlockSpec(memory_space=pltpu.HBM)


def split3(x):
    high = x.astype(jnp.bfloat16).astype(jnp.float32)
    rest = x - high
    middle = rest.astype(jnp.bfloat16).astype(jnp.float32)
    return high, middle, (rest - middle).astype(jnp.bfloat16).astype(jnp.float32)


def to_column(row, count):
    shape = (count, count)
    eye = lax.broadcasted_iota(jnp.int32, shape, 0) == lax.broadcasted_iota(jnp.int32, shape, 1)
    return jnp.sum(jnp.where(eye, row.astype(jnp.float32), 0.0), axis=1, keepdims=True)


def project_kernel(
    rank,
    tenant_hbm,
    adapter_hbm,
    tenant_row_hbm,
    adapter_row_hbm,
    holder_hbm,
    block_hbm,
    length_hbm,
    hidden_hbm,
    weight_hbm,
    down_hbm,
    up_hbm,
    keep_ref,
    send_ref,
    own_up_ref,
    tenant_ref,
    adapter_ref,
    holder_ref,
    block_ref,
    length_ref,
    hidden_ref,
    weight_ref,
    down_ref,
    total_ref,
    tenant_smem,
    adapter_smem,
    sems,
    up_sems,
    small_sems,
):
    chips, own, _ = keep_ref.shape
    rows, depth = hidden_ref.shape
    width = weight_ref.shape[1]
    spans = [slice(i, min(i + DEPTH, depth)) for i in range(0, depth, DEPTH)]
    first = [
        pltpu.make_async_copy(hidden_hbm, hidden_ref, sems.at[0]),
        pltpu.make_async_copy(down_hbm, down_ref, sems.at[1]),
    ]
    chunks = [
        pltpu.make_async_copy(weight_hbm.at[span], weight_ref.at[span], sems.at[2 + i])
        for i, span in enumerate(spans)
    ]
    scalars = [
        pltpu.make_async_copy(tenant_hbm, tenant_smem, up_sems.at[own]),
        pltpu.make_async_copy(adapter_hbm, adapter_smem, up_sems.at[own + 1]),
    ]
    small = [
        pltpu.make_async_copy(hbm, ref, small_sems.at[i])
        for i, (hbm, ref) in enumerate(
            (
                (tenant_row_hbm, tenant_ref),
                (adapter_row_hbm, adapter_ref),
                (holder_hbm, holder_ref),
                (block_hbm, block_ref),
                (length_hbm, length_ref),
            )
        )
    ]
    for copy in scalars + small + first + chunks:
        copy.start()
    for copy in small:
        copy.wait()

    slots = holder_ref.shape[1]
    numbers = [holder_ref[...], block_ref[...], length_ref[...], jnp.zeros((own, LANES - 3 * slots), jnp.int32)]
    numbers = jnp.concatenate(numbers, axis=1).astype(jnp.float32)
    tenants = adapter_ref.shape[1]
    tenant = to_column(tenant_ref[...], rows)
    pick = lax.broadcasted_iota(jnp.int32, (rows, tenants), 1).astype(jnp.float32) == tenant
    adapter = jnp.sum(jnp.where(pick, adapter_ref[...].astype(jnp.float32), 0.0), axis=1, keepdims=True).astype(
        jnp.int32
    )
    me = lax.axis_index("kv")
    even = me % PAIR == 0
    for copy in scalars:
        copy.wait()
    ups = [
        pltpu.make_async_copy(
            up_hbm.at[adapter_smem[tenant_smem[me * own + r]]], own_up_ref.at[r], up_sems.at[r]
        )
        for r in range(own)
    ]
    for copy in ups:
        copy.start()

    def store(columns, total):
        total = total.reshape(chips, PAIR, own, total.shape[1])
        keep_ref[:, :, columns] = jnp.where(even, total[:, 0], total[:, 1])
        send_ref[:, :, columns] = jnp.where(even, total[:, 1], total[:, 0])

    for copy in first:
        copy.wait()
    hidden = hidden_ref[...]
    low = lax.dot_general(hidden, down_ref[...], (((1,), (1,)), ((), ())), preferred_element_type=jnp.float32)
    column = lax.broadcasted_iota(jnp.int32, low.shape, 1)
    low = jnp.where((column >= adapter * rank) & (column < adapter * rank + rank), low, 0.0)
    low = sum(low[:, i : i + LANES] for i in range(LANES, low.shape[1], LANES)) + low[:, :LANES]
    shift = LANES // 2
    while shift >= rank:
        low = low + pltpu.roll(low, shift, 1)
        shift //= 2
    lane = lax.broadcasted_iota(jnp.int32, (rows, LANES), 1)
    numbers = jnp.concatenate([numbers] * (rows // own), axis=0)
    store(slice(width, width + LANES), jnp.where(lane < 3 * slots, numbers, low))
    for i, (span, copy) in enumerate(zip(spans, chunks)):
        copy.wait()
        for start in range(0, width, COLUMN_TILE):
            tile = slice(start, start + COLUMN_TILE)
            total = jnp.dot(hidden[:, span], weight_ref[span, tile], preferred_element_type=jnp.float32)
            if i > 0:
                total = total_ref[:, tile] + total
            if i < len(chunks) - 1:
                total_ref[:, tile] = total
            else:
                store(tile, total)
    for copy in ups:
        copy.wait()


def project(tenant, tenant_adapter, holder, block, length, hidden, query_weight, down, up, rank, chips):
    rows, depth = hidden.shape
    width = query_weight.shape[1]
    own = rows // chips // PAIR
    out = jax.ShapeDtypeStruct((chips, own, width + LANES), jnp.float32)
    tables = [x.reshape(1, -1) for x in (tenant, tenant_adapter)]
    operands = in_hbm(tenant, tenant_adapter, *tables, holder, block, length, hidden, query_weight, down, up)
    local = operands[2:10]
    return pl.pallas_call(
        functools.partial(project_kernel, rank),
        in_specs=[hbm_spec()] * len(operands),
        out_specs=[vmem_spec()] * 3,
        out_shape=[out, out, jax.ShapeDtypeStruct((own, *up.shape[1:]), up.dtype)],
        scratch_shapes=[pltpu.VMEM(x.shape, x.dtype) for x in local]
        + [
            pltpu.VMEM((rows, width), jnp.float32),
            pltpu.SMEM(tenant.shape, tenant.dtype),
            pltpu.SMEM(tenant_adapter.shape, tenant_adapter.dtype),
            pltpu.SemaphoreType.DMA((2 + pl.cdiv(depth, DEPTH),)),
            pltpu.SemaphoreType.DMA((own + 2,)),
            pltpu.SemaphoreType.DMA((5,)),
        ],
        compiler_params=params(16),
        name="project",
    )(*operands)


def pair_kernel(number_lanes, keep_ref, got_ref, *out_refs):
    chips, own, width = keep_ref.shape
    width = width - LANES
    chip = lax.axis_index("kv") // PAIR
    lane = lax.broadcasted_iota(jnp.int32, (own, LANES), 1)
    for s, ref in enumerate(out_refs):
        c = jnp.bitwise_xor(chip, s)
        ref[:, :width] = keep_ref[c, :, :width] + got_ref[c, :, :width]
        keep = keep_ref[c, :, width:]
        ref[:, width : width + LANES] = jnp.where(lane < number_lanes, keep, keep + got_ref[c, :, width:])
        ref[:, width + LANES :] = got_ref[c, :, width:]


def add_pair(keep, got, number_lanes):
    chips, own, width = keep.shape
    return pl.pallas_call(
        functools.partial(pair_kernel, number_lanes),
        in_specs=[vmem_spec()] * 2,
        out_specs=[vmem_spec()] * chips,
        out_shape=[jax.ShapeDtypeStruct((own, width + LANES), jnp.float32)] * chips,
        compiler_params=params(16),
        name="add_pair",
    )(keep, got)


def queries_kernel(number_lanes, *refs):
    parts, (up_ref, cosine_ref, sine_ref, gain_ref, out_ref, turned_ref) = refs[:-6], refs[-6:]
    own, rank, width = up_ref.shape
    heads = turned_ref.shape[1]

    def whole(columns):
        total = parts[0][:, columns]
        for part in parts[1:]:
            total = total + part[:, columns]
        return total

    low = whole(slice(width, width + LANES)) * ADAPTER_SCALE
    line = lax.broadcasted_iota(jnp.int32, (rank, LANES), 0)
    lane = lax.broadcasted_iota(jnp.int32, (rank, LANES), 1)
    low = [
        jnp.sum(jnp.where(lane == line + number_lanes, low[r : r + 1], 0.0), axis=1, keepdims=True)
        for r in range(own)
    ]
    row = lax.broadcasted_iota(jnp.int32, (own, LANES), 0)
    cosine, sine, gain = cosine_ref[...], sine_ref[...], gain_ref[...]
    for h in range(heads):
        columns = slice(h * LANES, (h + 1) * LANES)
        query = whole(columns)
        adapted = jnp.zeros((own, LANES), jnp.float32)
        for r in range(own):
            adapted = jnp.where(row == r, jnp.sum(up_ref[r, :, columns] * low[r], axis=0, keepdims=True), adapted)
        query = query + adapted
        square = jnp.mean(query * query, axis=-1, keepdims=True)
        query = query * lax.rsqrt(square + EPSILON) * gain
        turned_ref[:, h, :] = query * cosine + pltpu.roll(query, LANES // 2, 1) * sine
    out_ref[...] = turned_ref[...].astype(jnp.bfloat16)


def make_queries(parts, up, cosine, sine, gain, heads, number_lanes):
    own = parts[0].shape[0]
    shape = (own, heads, LANES)
    return pl.pallas_call(
        functools.partial(queries_kernel, number_lanes),
        in_specs=[vmem_spec()] * (len(parts) + 4),
        out_specs=vmem_spec(),
        out_shape=jax.ShapeDtypeStruct(shape, jnp.bfloat16),
        scratch_shapes=[pltpu.VMEM(shape, jnp.float32)],
        compiler_params=params(16),
        name="queries",
    )(*parts, up, cosine, sine, gain)


def place_kernel(blocks, block_size, slots, *refs):
    pieces, (place_ref, value_ref, bound_ref) = refs[:-3], refs[-3:]
    rows = place_ref.shape[0]
    me = lax.axis_index("kv").astype(jnp.float32)
    numbers = jnp.concatenate([p[:, i * LANES : (i + 1) * LANES] for p in pieces for i in range(PAIR)], axis=0)
    holder, block, length = (numbers[:, i * slots : (i + 1) * slots] for i in range(3))
    row = lax.broadcasted_iota(jnp.int32, (rows, slots), 0).astype(jnp.float32)
    spare = float(rows * blocks * block_size)
    value_ref[...] = (row * blocks + block) * block_size + (length - 1.0) - spare
    mine = holder == me
    key = jnp.where(mine, block, -1.0)

    def before(count, axis):
        first = lax.broadcasted_iota(jnp.int32, (count, count), axis)
        return jnp.where(first < lax.broadcasted_iota(jnp.int32, (count, count), 1 - axis), 1.0, 0.0).astype(
            jnp.bfloat16
        )

    lane = lax.broadcasted_iota(jnp.int32, (rows, blocks), 1).astype(jnp.float32)
    picks = [jnp.where(key[:, j : j + 1] == lane, 1.0, 0.0) for j in range(slots)]
    count = jnp.sum(functools.reduce(jnp.add, picks), axis=0, keepdims=True)
    tasks = jnp.floor((count + (GROUP - 1)) * (1.0 / GROUP))
    earlier = jnp.dot(
        jnp.broadcast_to(tasks, (8, blocks)).astype(jnp.bfloat16),
        before(blocks, 0),
        preferred_element_type=jnp.float32,
    )[:1]
    base = earlier * GROUP
    row_before = before(rows, 1)
    slot = lax.broadcasted_iota(jnp.int32, (rows, slots), 1)
    place = jnp.full((rows, slots), -1.0, jnp.float32)
    for j in range(slots):
        above = jnp.dot(row_before, picks[j].astype(jnp.bfloat16), preferred_element_type=jnp.float32)
        here = jnp.sum(picks[j] * (above + base), axis=1, keepdims=True)
        place = jnp.where((slot == j) & mine, here, place)
        base = base + jnp.sum(picks[j], axis=0, keepdims=True)
    place_ref[...] = place
    size = blocks // PHASES
    end = earlier + tasks
    block_lane = lax.broadcasted_iota(jnp.int32, (1, blocks), 1)
    bound_lane = lax.broadcasted_iota(jnp.int32, (1, LANES), 1)
    bounds = jnp.zeros((1, LANES), jnp.float32)
    for part in range(PHASES):
        done = jnp.sum(jnp.where(block_lane == (part + 1) * size - 1, end, 0.0), axis=1, keepdims=True)
        done = done * (1.0 / TASKS)
        done = jnp.ceil(done) if part == PHASES - 1 else jnp.floor(done)
        bounds = jnp.where(bound_lane == part + 1, done, bounds)
    bound_ref[...] = bounds.astype(jnp.int32)


def list_kernel(
    spare, place_ref, value_ref, joined_ref, key_hbm, value_hbm, list_ref, first_key_ref, first_value_ref, sems
):
    rows, slots = place_ref.shape
    span = pl.ds(0, first_key_ref.shape[0])
    copies = [
        pltpu.make_async_copy(key_hbm.at[span], first_key_ref, sems.at[0]),
        pltpu.make_async_copy(value_hbm.at[span], first_value_ref, sems.at[1]),
    ]
    for copy in copies:
        copy.start()
    capacity = list_ref.shape[1]
    target = lax.broadcasted_iota(jnp.int32, (8, capacity), 1).astype(jnp.float32)

    def tile(t, total):
        here = pl.ds(pl.multiple_of(t * 8, 8), 8)
        places, values = place_ref[here, :], value_ref[here, :]
        for j in range(slots):
            total = total + jnp.where(places[:, j : j + 1] == target, values[:, j : j + 1], 0.0)
        return total

    total = lax.fori_loop(0, rows // 8, tile, jnp.zeros((8, capacity), jnp.float32))
    list_ref[...] = (jnp.sum(total, axis=0, keepdims=True) + spare).astype(jnp.int32)
    for copy in copies:
        copy.wait()


def make_places(parts, slots, blocks, block_size, count):
    own, width = parts[0].shape
    rows = count * own
    last = width // (PAIR * LANES) - 1
    table = jax.ShapeDtypeStruct((rows, slots), jnp.float32)
    bounds = jax.ShapeDtypeStruct((1, LANES), jnp.int32)
    return pl.pallas_call(
        functools.partial(place_kernel, blocks, block_size, slots),
        grid=(1,),
        in_specs=[pl.BlockSpec((own, PAIR * LANES), lambda i: (0, last))] * len(parts),
        out_specs=[pl.BlockSpec(x.shape, lambda i: (0, 0)) for x in (table, table, bounds)],
        out_shape=[table, table, bounds],
        compiler_params=params(16),
        cost_estimate=pl.CostEstimate(flops=10**8, bytes_accessed=4 * 10**6, transcendentals=0),
        name="slot_places",
    )(*parts)


def make_list(places, slot_values, joined, keys, values, block_size, count):
    blocks = keys.shape[0]
    rows, slots = places.shape
    most = 2 * rows * slots // count // count * count + (GROUP - 1) * blocks + 3 * CHUNK
    capacity = -(-most // LANES) * LANES
    return pl.pallas_call(
        functools.partial(list_kernel, float(rows * blocks * block_size)),
        in_specs=[vmem_spec()] * 3 + [hbm_spec()] * 2,
        out_specs=[vmem_spec()] * 3,
        out_shape=[jax.ShapeDtypeStruct((1, capacity), jnp.int32)]
        + [jax.ShapeDtypeStruct((blocks // PHASES, *x.shape[1:]), x.dtype) for x in (keys, values)],
        scratch_shapes=[pltpu.SemaphoreType.DMA((2,))],
        compiler_params=params(16),
        cost_estimate=pl.CostEstimate(flops=10**8, bytes_accessed=4 * 10**6, transcendentals=0),
        name="slot_list",
    )(places, slot_values, joined, *in_hbm(keys, values))


def join_kernel(*refs):
    pieces, out_ref = refs[:-2], refs[-1]
    for s, piece in enumerate(pieces):
        out_ref[s] = piece[...]


def join(pieces, places):
    return pl.pallas_call(
        join_kernel,
        in_specs=[vmem_spec()] * (len(pieces) + 1),
        out_specs=vmem_spec(),
        out_shape=jax.ShapeDtypeStruct((len(pieces), *pieces[0].shape), pieces[0].dtype),
        compiler_params=params(16),
        name="join",
    )(*pieces, places)


def attend_kernel(scale, kv_local, count, list_vmem, bound_vmem, *refs):
    queries, first_refs, refs = refs[:PAIR], refs[PAIR : PAIR + 2], refs[PAIR + 2 :]
    (key_hbm, value_hbm, keep_ref, send_ref, list_ref, bound_ref, query_ref, key_ref, value_ref) = refs[:9]
    (score_ref, part_top_ref, part_total_ref, part_sum_ref, number_sems, sems) = refs[9:15]
    states = [refs[15 + 3 * k : 18 + 3 * k] for k in range(SETS)]
    heads = query_ref.shape[1]
    rows = query_ref.shape[0] - 1
    own = rows // count
    blocks, tokens, _ = key_ref.shape
    block_size = tokens // kv_local
    length_bits = (block_size - 1).bit_length()
    block_bits = (blocks - 1).bit_length()
    numbers = (
        pltpu.make_async_copy(list_vmem, list_ref, number_sems.at[0]),
        pltpu.make_async_copy(bound_vmem, bound_ref, number_sems.at[1]),
    )
    size = blocks // PHASES
    spans = [pl.ds(part * size, size) for part in range(PHASES)]
    copies = [
        (
            pltpu.make_async_copy(key_hbm.at[span], key_ref.at[span], sems.at[0, part]),
            pltpu.make_async_copy(value_hbm.at[span], value_ref.at[span], sems.at[1, part]),
        )
        for part, span in enumerate(spans)
    ]
    for pair in (numbers, *copies[1 : 1 + AHEAD]):
        for copy in pair:
            copy.start()
    for ref, first_ref in zip((key_ref, value_ref), first_refs):
        ref[:size] = first_ref[...]

    factor = scale * LOG2E
    for t, piece in enumerate(queries):
        for s in range(count // PAIR):
            start = (PAIR * s + t) * own
            query_ref[start : start + own] = piece[s]
    query_ref[rows] = jnp.zeros((heads, LANES), jnp.bfloat16)
    for state in states:
        for ref, value in zip(state, (NEG_FILL, 0.0, 0.0)):
            ref[...] = jnp.full(ref.shape, value, jnp.float32)
    for ref in (score_ref, part_top_ref, part_total_ref, part_sum_ref):
        ref[...] = jnp.zeros(ref.shape, jnp.float32)
    group = heads // kv_local
    column = lax.broadcasted_iota(jnp.int32, (group, tokens), 1)
    first = column % kv_local == 0
    wide = (heads, LANES)
    narrow = (group, LANES)

    def entries(chunk):
        return [list_ref[0, chunk * CHUNK + j] for j in range(CHUNK)]

    def row_of(entry):
        return entry >> (length_bits + block_bits)

    def block_of(entry):
        return (entry >> length_bits) & (blocks - 1)

    def merge_slots(row, start):
        before = [[ref[r] for ref in state] for r, state in zip(row, states)]
        after = []
        for k, (top, total, acc) in enumerate(before):
            t, place = divmod(start + k, GROUP)
            part_top = part_top_ref[start + k]
            share = jnp.exp2(-jnp.abs(top - part_top) * factor)
            lower = top < part_top
            old, new = jnp.where(lower, share, 1.0), jnp.where(lower, 1.0, share)
            after.append(
                (
                    jnp.maximum(top, part_top),
                    total * old + part_total_ref[start + k] * new,
                    acc * old + part_sum_ref[t, place * heads : (place + 1) * heads] * new,
                )
            )
        for r, state, new in zip(row, states, after):
            for ref, value in zip(state, new):
                ref[r] = value

    def weigh_item(entry, t, k):
        j = t * GROUP + k
        start = k * heads
        scores = jnp.where(
            first, score_ref[t, start : start + group], score_ref[t, start + group : start + heads]
        )
        length = (entry & (block_size - 1)) + 1
        scores = jnp.where(column < length * kv_local, scores, NEG_FILL)
        tops = [
            jnp.max(x, axis=1, keepdims=True)
            for x in (jnp.where(first, scores, NEG_FILL), jnp.where(first, NEG_FILL, scores))
        ]
        weights = jnp.exp2((scores - jnp.where(first, tops[0], tops[1])) * factor)
        weights = (jnp.where(first, weights, 0.0), jnp.where(first, 0.0, weights))
        for a in range(kv_local):
            here = slice(a * group, (a + 1) * group)
            part_top_ref[j, here] = jnp.broadcast_to(tops[a], narrow)
            part_total_ref[j, here] = jnp.broadcast_to(jnp.sum(weights[a], axis=1, keepdims=True), narrow)
        return jnp.concatenate(weights, axis=0).astype(jnp.bfloat16)

    def turn(stages, i, carry):
        merged, weighed, scored = (entries(jnp.maximum(i - back, 0)) for back in (2, 1, 0))
        for t in range(TASKS):
            task = slice(t * GROUP, (t + 1) * GROUP)
            for start in range(t * GROUP, (t + 1) * GROUP, SETS):
                merge_slots(
                    [jnp.where(i >= 2, row_of(entry), rows) for entry in merged[start : start + SETS]], start
                )
            if stages > 1:
                weights = [weigh_item(entry, t, k) for k, entry in enumerate(weighed[task])]
                part_sum_ref[t] = jnp.dot(
                    jnp.concatenate(weights, axis=0),
                    value_ref[block_of(weighed[task][0])],
                    preferred_element_type=jnp.float32,
                )
            if stages > 2:
                score_ref[t] = lax.dot_general(
                    jnp.concatenate([query_ref[row_of(entry)] for entry in scored[task]], axis=0),
                    key_ref[block_of(scored[task][0])],
                    (((1,), (1,)), ((), ())),
                    preferred_element_type=jnp.float32,
                )
        return carry

    for copy in numbers:
        copy.wait()
    for part in range(PHASES):
        if part > 0:
            for copy in copies[part]:
                copy.wait()
            for pair in copies[part + AHEAD : part + AHEAD + 1]:
                for copy in pair:
                    copy.start()
        lax.fori_loop(bound_ref[0, part], bound_ref[0, part + 1], functools.partial(turn, 3), 0)
    last = bound_ref[0, PHASES]
    turn(2, last, 0)
    turn(1, last + 1, 0)

    square = (own * heads, LANES)
    eye = lax.broadcasted_iota(jnp.int32, square, 0) == lax.broadcasted_iota(jnp.int32, square, 1)
    line = lax.broadcasted_iota(jnp.int32, wide, 0)
    for q in range(count):
        ref = (keep_ref, send_ref)[q % PAIR]
        mine = slice(q * own, (q + 1) * own)
        tops = [top_ref[mine] for top_ref, _, _ in states]
        high = functools.reduce(jnp.maximum, tops)
        shares = [jnp.exp2((top - high) * factor) for top in tops]
        total = sum(total_ref[mine] * share for (_, total_ref, _), share in zip(states, shares))
        ref[q // PAIR, :own] = sum(sum_ref[mine] * share for (_, _, sum_ref), share in zip(states, shares))
        high, total = (
            jnp.sum(jnp.where(eye, x.reshape(square), 0.0), axis=0, keepdims=True) for x in (high, total)
        )
        ref[q // PAIR, own] = jnp.where(line == 0, high, jnp.where(line == 1, total, 0.0))


def attend(items, bounds, queries, first, keys, values, kv_local, scale):
    chips, own, heads, _ = queries[0].shape
    count = chips * PAIR
    rows = count * own
    tokens = keys.shape[1]
    keys, values = in_hbm(keys, values)
    state = pltpu.VMEM((rows + 1, heads, LANES), jnp.float32)
    part = pltpu.VMEM((CHUNK, heads, LANES), jnp.float32)
    return pl.pallas_call(
        functools.partial(attend_kernel, scale, kv_local, count),
        in_specs=[vmem_spec()] * (4 + len(queries)) + [hbm_spec()] * 2,
        out_specs=[vmem_spec()] * PAIR,
        out_shape=[jax.ShapeDtypeStruct((count // PAIR, own + 1, heads, LANES), jnp.float32)] * PAIR,
        scratch_shapes=[
            pltpu.SMEM(items.shape, items.dtype),
            pltpu.SMEM(bounds.shape, bounds.dtype),
            pltpu.VMEM((rows + 1, heads, LANES), jnp.bfloat16),
            pltpu.VMEM(keys.shape, keys.dtype),
            pltpu.VMEM(values.shape, values.dtype),
            pltpu.VMEM((TASKS, GROUP * heads, tokens), jnp.float32),
            part,
            part,
            pltpu.VMEM((TASKS, GROUP * heads, LANES), jnp.float32),
            pltpu.SemaphoreType.DMA((2,)),
            pltpu.SemaphoreType.DMA((2, PHASES)),
        ]
        + [state] * (3 * SETS),
        compiler_params=params(28 + 3 * SETS * rows * heads * LANES * 4 // MIB),
        name="attend",
    )(items, bounds, *queries, *first, keys, values)


def merge_pair_kernel(scale, keep_ref, got_ref, out_ref):
    chips, sections, heads, _ = keep_ref.shape
    own = sections - 1
    factor = scale * LOG2E
    line = lax.broadcasted_iota(jnp.int32, (heads, LANES), 0)
    shares, stats = [], []
    for s in range(chips):
        keep, got = keep_ref[s, own], got_ref[s, own]
        high = jnp.maximum(keep[0:1], got[0:1])
        pair = [jnp.exp2((x[0:1] - high) * factor) for x in (keep, got)]
        shares += pair
        total = pair[0] * keep[1:2] + pair[1] * got[1:2]
        stat = jnp.zeros((heads, LANES), jnp.float32)
        for position, piece in enumerate(split3(high) + split3(total)):
            stat = jnp.where(line == position, piece, stat)
        stats.append(stat)
    columns = jnp.concatenate(shares, axis=0).T
    flat = (own * heads, LANES)
    for s in range(chips):
        total = keep_ref[s, :own].reshape(flat) * columns[:, PAIR * s : PAIR * s + 1]
        total = total + got_ref[s, :own].reshape(flat) * columns[:, PAIR * s + 1 : PAIR * s + 2]
        out_ref[s, :own] = total.astype(jnp.bfloat16).reshape(own, heads, LANES)
        out_ref[s, own] = stats[s].astype(jnp.bfloat16)


def merge_pair(keep, got, scale):
    return pl.pallas_call(
        functools.partial(merge_pair_kernel, scale),
        in_specs=[vmem_spec()] * 2,
        out_specs=vmem_spec(),
        out_shape=jax.ShapeDtypeStruct(keep.shape, jnp.bfloat16),
        compiler_params=params(16),
        name="merge_pair",
    )(keep, got)


def merge_kernel(scale, *refs):
    pieces, (out_ref, wide_ref) = refs[:-2], refs[-2:]
    chips, sections, heads, _ = pieces[0].shape
    own = sections - 1
    factor = scale * LOG2E
    shares = []
    for s in range(chips):
        stats = [pieces[j][s ^ j, own].astype(jnp.float32) for j in range(chips)]
        tops = jnp.concatenate([x[0:1] + x[1:2] + x[2:3] for x in stats], axis=0)
        totals = jnp.concatenate([x[3:4] + x[4:5] + x[5:6] for x in stats], axis=0)
        weights = jnp.exp2((tops - jnp.max(tops, axis=0, keepdims=True)) * factor)
        shares.append(weights / jnp.sum(weights * totals, axis=0, keepdims=True))
    columns = jnp.concatenate(shares, axis=0).T
    flat = own * heads
    for s in range(chips):
        total = jnp.zeros((flat, LANES), jnp.float32)
        for j in range(chips):
            part = pieces[j][s ^ j, :own].astype(jnp.float32).reshape(flat, LANES)
            total = total + part * columns[:, s * chips + j : s * chips + j + 1]
        wide_ref[s * flat : (s + 1) * flat, :] = total
    rows = [wide_ref[pl.ds(h, chips * own, stride=heads), :] for h in range(heads)]
    out_ref[...] = jnp.concatenate(rows, axis=1).astype(jnp.bfloat16)


def merge(pieces, scale):
    chips, sections, heads, _ = pieces[0].shape
    own = sections - 1
    return pl.pallas_call(
        functools.partial(merge_kernel, scale),
        in_specs=[vmem_spec()] * chips,
        out_specs=vmem_spec(),
        out_shape=jax.ShapeDtypeStruct((chips * own, heads * LANES), jnp.bfloat16),
        scratch_shapes=[pltpu.VMEM((chips * own * heads, LANES), jnp.float32)],
        compiler_params=params(32),
        name="merge",
    )(*pieces)


def output_kernel(own, *refs):
    pieces, weight_ref = refs[:PAIR], refs[PAIR]
    outs, (rows_ref, terms_ref) = refs[PAIR + 1 : -2], refs[-2:]
    me = lax.axis_index("kv")
    for t in range(PAIR):
        piece = pieces[t][...].astype(jnp.float32)
        for s in range(piece.shape[0] // own):
            start = pl.multiple_of(jnp.bitwise_xor(me, PAIR * s + t) * own, own)
            rows_ref[pl.ds(start, own), :] = piece[s * own : (s + 1) * own]
    terms_ref[...] = jnp.dot(
        rows_ref[...].astype(jnp.bfloat16), weight_ref[...], preferred_element_type=jnp.float32
    )
    me = lax.axis_index("row")
    part = outs[0].shape[0]
    for s, ref in enumerate(outs):
        start = pl.multiple_of(jnp.bitwise_xor(me, s) * part, part)
        ref[...] = terms_ref[pl.ds(start, part), :].astype(ref.dtype)


def project_out(pieces, weight, own, row_count):
    half, width = pieces[0].shape
    rows, columns = PAIR * half, weight.shape[1]
    shape = (rows // row_count, columns)
    send = jax.ShapeDtypeStruct(shape, jnp.bfloat16)
    return pl.pallas_call(
        functools.partial(output_kernel, own),
        in_specs=[vmem_spec()] * (PAIR + 1),
        out_specs=[vmem_spec()] * row_count,
        out_shape=[jax.ShapeDtypeStruct(shape, jnp.float32)] + [send] * (row_count - 1),
        scratch_shapes=[pltpu.VMEM((rows, width), jnp.float32), pltpu.VMEM((rows, columns), jnp.float32)],
        compiler_params=params(24),
        name="project_out",
    )(*pieces, weight)


def exchange(x, axis, s):
    count = lax.axis_size(axis)
    return lax.ppermute(x, axis, [(i, i ^ s) for i in range(count)])


def gather_chips(x):
    return [x] + [exchange(x, "kv", s) for s in range(PAIR, lax.axis_size("kv"), PAIR)]


def local(
    hidden,
    query_weight,
    adapter_down_weight,
    adapter_up_weight,
    query_norm_gain,
    paged_key_cache,
    paged_value_cache,
    output_weight,
    holder,
    holder_block_index,
    block_used_length,
    tenant,
    tenant_adapter,
):
    own, slots = holder.shape
    rows, depth = hidden.shape
    kv_count = lax.axis_size("kv")
    row_count = lax.axis_size("row")
    adapters, _, rank = adapter_down_weight.shape
    width = query_weight.shape[1]
    head_size = query_norm_gain.shape[0]
    heads = width // head_size
    blocks, block_size, kv_local, _ = paged_key_cache.shape
    scale = 1.0 / math.sqrt(head_size)

    chips = kv_count // PAIR
    keep, send, up = project(
        tenant,
        tenant_adapter,
        holder,
        holder_block_index,
        block_used_length,
        hidden,
        query_weight,
        jnp.swapaxes(adapter_down_weight, 1, 2).reshape(adapters * rank, depth),
        adapter_up_weight,
        rank,
        chips,
    )
    parts = add_pair(keep, exchange(send, "kv", 1), 3 * slots)
    parts = [parts[0]] + [exchange(parts[s], "kv", PAIR * s) for s in range(1, chips)]

    position = (jnp.sum(block_used_length, axis=1) - 1).astype(jnp.float32)
    half = head_size // 2
    frequency = ROPE_BASE ** (-(jnp.arange(half, dtype=jnp.float32) * 2.0) / head_size)
    angles = position[:, None] * frequency[None, :]
    cosine = jnp.concatenate([jnp.cos(angles), jnp.cos(angles)], axis=-1)
    sine = jnp.concatenate([-jnp.sin(angles), jnp.sin(angles)], axis=-1)
    queries = make_queries(parts, up, cosine, sine, query_norm_gain.reshape(1, head_size), heads, 3 * slots)
    places, slot_values, bounds = make_places(parts, slots, blocks, block_size, kv_count)
    queries = join(gather_chips(queries), places)
    keys = paged_key_cache.reshape(blocks, block_size * kv_local, head_size)
    values = paged_value_cache.reshape(blocks, block_size * kv_local, head_size)
    items, *first = make_list(places, slot_values, queries, keys, values, block_size, kv_count)
    queries = [queries, exchange(queries, "kv", 1)]
    keep, send = attend(items, bounds, queries, first, keys, values, kv_local, scale)
    merged = merge_pair(keep, exchange(send, "kv", 1), scale)
    attention = merge(gather_chips(merged), scale)
    terms = project_out([attention, exchange(attention, "kv", 1)], output_weight, own, row_count)
    total = terms[0]
    for s in range(1, row_count):
        total = total + exchange(terms[s], "row", s).astype(jnp.float32)
    return total.astype(jnp.bfloat16)


def solution(mesh):
    return jax.shard_map(
        local,
        mesh=mesh,
        in_specs=(
            P(None, "kv"),
            P("kv", "row"),
            P(None, "kv", None),
            P(None, None, "row"),
            P(),
            P("kv", None, "row", None),
            P("kv", None, "row", None),
            P("row", "kv"),
            P("kv", None),
            P("kv", None),
            P("kv", None),
            P(),
            P(),
        ),
        out_specs=P("row", "kv"),
        check_vma=False,
    )
```

```python
import functools
import math

import jax
import jax.numpy as jnp
from jax import lax
from jax.experimental import pallas as pl
from jax.experimental.pallas import tpu as pltpu
from jax.sharding import PartitionSpec as P

ADAPTER_SCALE = 0.5
ROPE_BASE = 1000000.0
EPSILON = 1e-06
NEG_FILL = -1e30
LANES = 128
COLUMN_TILE = 256
PAIR = 2
GROUP = 4
TASKS = 16
CHUNK = GROUP * TASKS
SETS = 2
PHASES = 8
AHEAD = 4
DEPTH = 256
LOG2E = math.log2(math.e)
MIB = 1024 * 1024


def params(mib):
    return pltpu.CompilerParams(vmem_limit_bytes=mib * MIB)


def vmem_spec():
    return pl.BlockSpec(memory_space=pltpu.VMEM)


def in_hbm(*arrays):
    return [pltpu.with_memory_space_constraint(x, pltpu.HBM) for x in arrays]


def hbm_spec():
    return pl.BlockSpec(memory_space=pltpu.HBM)


def split3(x):
    high = x.astype(jnp.bfloat16).astype(jnp.float32)
    rest = x - high
    middle = rest.astype(jnp.bfloat16).astype(jnp.float32)
    return high, middle, (rest - middle).astype(jnp.bfloat16).astype(jnp.float32)


def to_column(row, count):
    shape = (count, count)
    eye = lax.broadcasted_iota(jnp.int32, shape, 0) == lax.broadcasted_iota(jnp.int32, shape, 1)
    return jnp.sum(jnp.where(eye, row.astype(jnp.float32), 0.0), axis=1, keepdims=True)


def project_kernel(
    rank,
    tenant_hbm,
    adapter_hbm,
    tenant_row_hbm,
    adapter_row_hbm,
    holder_hbm,
    block_hbm,
    length_hbm,
    hidden_hbm,
    weight_hbm,
    down_hbm,
    up_hbm,
    keep_ref,
    send_ref,
    own_up_ref,
    tenant_ref,
    adapter_ref,
    holder_ref,
    block_ref,
    length_ref,
    hidden_ref,
    weight_ref,
    down_ref,
    total_ref,
    tenant_smem,
    adapter_smem,
    sems,
    up_sems,
    small_sems,
):
    chips, own, _ = keep_ref.shape
    rows, depth = hidden_ref.shape
    width = weight_ref.shape[1]
    spans = [slice(i, min(i + DEPTH, depth)) for i in range(0, depth, DEPTH)]
    first = [
        pltpu.make_async_copy(hidden_hbm, hidden_ref, sems.at[0]),
        pltpu.make_async_copy(down_hbm, down_ref, sems.at[1]),
    ]
    chunks = [
        pltpu.make_async_copy(weight_hbm.at[span], weight_ref.at[span], sems.at[2 + i])
        for i, span in enumerate(spans)
    ]
    scalars = [
        pltpu.make_async_copy(tenant_hbm, tenant_smem, up_sems.at[own]),
        pltpu.make_async_copy(adapter_hbm, adapter_smem, up_sems.at[own + 1]),
    ]
    small = [
        pltpu.make_async_copy(hbm, ref, small_sems.at[i])
        for i, (hbm, ref) in enumerate(
            (
                (tenant_row_hbm, tenant_ref),
                (adapter_row_hbm, adapter_ref),
                (holder_hbm, holder_ref),
                (block_hbm, block_ref),
                (length_hbm, length_ref),
            )
        )
    ]
    for copy in scalars + small + first + chunks:
        copy.start()
    for copy in small:
        copy.wait()

    slots = holder_ref.shape[1]
    numbers = [holder_ref[...], block_ref[...], length_ref[...], jnp.zeros((own, LANES - 3 * slots), jnp.int32)]
    numbers = jnp.concatenate(numbers, axis=1).astype(jnp.float32)
    tenants = adapter_ref.shape[1]
    tenant = to_column(tenant_ref[...], rows)
    pick = lax.broadcasted_iota(jnp.int32, (rows, tenants), 1).astype(jnp.float32) == tenant
    adapter = jnp.sum(jnp.where(pick, adapter_ref[...].astype(jnp.float32), 0.0), axis=1, keepdims=True).astype(
        jnp.int32
    )
    me = lax.axis_index("kv")
    even = me % PAIR == 0
    for copy in scalars:
        copy.wait()
    ups = [
        pltpu.make_async_copy(
            up_hbm.at[adapter_smem[tenant_smem[me * own + r]]], own_up_ref.at[r], up_sems.at[r]
        )
        for r in range(own)
    ]
    for copy in ups:
        copy.start()

    def store(columns, total):
        total = total.reshape(chips, PAIR, own, total.shape[1])
        keep_ref[:, :, columns] = jnp.where(even, total[:, 0], total[:, 1])
        send_ref[:, :, columns] = jnp.where(even, total[:, 1], total[:, 0])

    for copy in first:
        copy.wait()
    hidden = hidden_ref[...]
    low = lax.dot_general(hidden, down_ref[...], (((1,), (1,)), ((), ())), preferred_element_type=jnp.float32)
    column = lax.broadcasted_iota(jnp.int32, low.shape, 1)
    low = jnp.where((column >= adapter * rank) & (column < adapter * rank + rank), low, 0.0)
    low = sum(low[:, i : i + LANES] for i in range(LANES, low.shape[1], LANES)) + low[:, :LANES]
    shift = LANES // 2
    while shift >= rank:
        low = low + pltpu.roll(low, shift, 1)
        shift //= 2
    lane = lax.broadcasted_iota(jnp.int32, (rows, LANES), 1)
    numbers = jnp.concatenate([numbers] * (rows // own), axis=0)
    store(slice(width, width + LANES), jnp.where(lane < 3 * slots, numbers, low))
    for i, (span, copy) in enumerate(zip(spans, chunks)):
        copy.wait()
        for start in range(0, width, COLUMN_TILE):
            tile = slice(start, start + COLUMN_TILE)
            total = jnp.dot(hidden[:, span], weight_ref[span, tile], preferred_element_type=jnp.float32)
            if i > 0:
                total = total_ref[:, tile] + total
            if i < len(chunks) - 1:
                total_ref[:, tile] = total
            else:
                store(tile, total)
    for copy in ups:
        copy.wait()


def project(tenant, tenant_adapter, holder, block, length, hidden, query_weight, down, up, rank, chips):
    rows, depth = hidden.shape
    width = query_weight.shape[1]
    own = rows // chips // PAIR
    out = jax.ShapeDtypeStruct((chips, own, width + LANES), jnp.float32)
    tables = [x.reshape(1, -1) for x in (tenant, tenant_adapter)]
    operands = in_hbm(tenant, tenant_adapter, *tables, holder, block, length, hidden, query_weight, down, up)
    local = operands[2:10]
    return pl.pallas_call(
        functools.partial(project_kernel, rank),
        in_specs=[hbm_spec()] * len(operands),
        out_specs=[vmem_spec()] * 3,
        out_shape=[out, out, jax.ShapeDtypeStruct((own, *up.shape[1:]), up.dtype)],
        scratch_shapes=[pltpu.VMEM(x.shape, x.dtype) for x in local]
        + [
            pltpu.VMEM((rows, width), jnp.float32),
            pltpu.SMEM(tenant.shape, tenant.dtype),
            pltpu.SMEM(tenant_adapter.shape, tenant_adapter.dtype),
            pltpu.SemaphoreType.DMA((2 + pl.cdiv(depth, DEPTH),)),
            pltpu.SemaphoreType.DMA((own + 2,)),
            pltpu.SemaphoreType.DMA((5,)),
        ],
        compiler_params=params(16),
        name="project",
    )(*operands)


def pair_kernel(number_lanes, keep_ref, got_ref, *out_refs):
    chips, own, width = keep_ref.shape
    width = width - LANES
    chip = lax.axis_index("kv") // PAIR
    lane = lax.broadcasted_iota(jnp.int32, (own, LANES), 1)
    for s, ref in enumerate(out_refs):
        c = jnp.bitwise_xor(chip, s)
        ref[:, :width] = keep_ref[c, :, :width] + got_ref[c, :, :width]
        keep = keep_ref[c, :, width:]
        ref[:, width : width + LANES] = jnp.where(lane < number_lanes, keep, keep + got_ref[c, :, width:])
        ref[:, width + LANES :] = got_ref[c, :, width:]


def add_pair(keep, got, number_lanes):
    chips, own, width = keep.shape
    return pl.pallas_call(
        functools.partial(pair_kernel, number_lanes),
        in_specs=[vmem_spec()] * 2,
        out_specs=[vmem_spec()] * chips,
        out_shape=[jax.ShapeDtypeStruct((own, width + LANES), jnp.float32)] * chips,
        compiler_params=params(16),
        name="add_pair",
    )(keep, got)


def queries_kernel(number_lanes, *refs):
    parts, (up_ref, cosine_ref, sine_ref, gain_ref, out_ref, turned_ref) = refs[:-6], refs[-6:]
    own, rank, width = up_ref.shape
    heads = turned_ref.shape[1]

    def whole(columns):
        total = parts[0][:, columns]
        for part in parts[1:]:
            total = total + part[:, columns]
        return total

    low = whole(slice(width, width + LANES)) * ADAPTER_SCALE
    line = lax.broadcasted_iota(jnp.int32, (rank, LANES), 0)
    lane = lax.broadcasted_iota(jnp.int32, (rank, LANES), 1)
    low = [
        jnp.sum(jnp.where(lane == line + number_lanes, low[r : r + 1], 0.0), axis=1, keepdims=True)
        for r in range(own)
    ]
    row = lax.broadcasted_iota(jnp.int32, (own, LANES), 0)
    cosine, sine, gain = cosine_ref[...], sine_ref[...], gain_ref[...]
    for h in range(heads):
        columns = slice(h * LANES, (h + 1) * LANES)
        query = whole(columns)
        adapted = jnp.zeros((own, LANES), jnp.float32)
        for r in range(own):
            adapted = jnp.where(row == r, jnp.sum(up_ref[r, :, columns] * low[r], axis=0, keepdims=True), adapted)
        query = query + adapted
        square = jnp.mean(query * query, axis=-1, keepdims=True)
        query = query * lax.rsqrt(square + EPSILON) * gain
        turned_ref[:, h, :] = query * cosine + pltpu.roll(query, LANES // 2, 1) * sine
    out_ref[...] = turned_ref[...].astype(jnp.bfloat16)


def make_queries(parts, up, cosine, sine, gain, heads, number_lanes):
    own = parts[0].shape[0]
    shape = (own, heads, LANES)
    return pl.pallas_call(
        functools.partial(queries_kernel, number_lanes),
        in_specs=[vmem_spec()] * (len(parts) + 4),
        out_specs=vmem_spec(),
        out_shape=jax.ShapeDtypeStruct(shape, jnp.bfloat16),
        scratch_shapes=[pltpu.VMEM(shape, jnp.float32)],
        compiler_params=params(16),
        name="queries",
    )(*parts, up, cosine, sine, gain)


def place_kernel(blocks, block_size, slots, *refs):
    pieces, (place_ref, value_ref, bound_ref) = refs[:-3], refs[-3:]
    rows = place_ref.shape[0]
    me = lax.axis_index("kv").astype(jnp.float32)
    numbers = jnp.concatenate([p[:, i * LANES : (i + 1) * LANES] for p in pieces for i in range(PAIR)], axis=0)
    holder, block, length = (numbers[:, i * slots : (i + 1) * slots] for i in range(3))
    row = lax.broadcasted_iota(jnp.int32, (rows, slots), 0).astype(jnp.float32)
    spare = float(rows * blocks * block_size)
    value_ref[...] = (row * blocks + block) * block_size + (length - 1.0) - spare
    mine = holder == me
    key = jnp.where(mine, block, -1.0)

    def before(count, axis):
        first = lax.broadcasted_iota(jnp.int32, (count, count), axis)
        return jnp.where(first < lax.broadcasted_iota(jnp.int32, (count, count), 1 - axis), 1.0, 0.0).astype(
            jnp.bfloat16
        )

    lane = lax.broadcasted_iota(jnp.int32, (rows, blocks), 1).astype(jnp.float32)
    picks = [jnp.where(key[:, j : j + 1] == lane, 1.0, 0.0) for j in range(slots)]
    count = jnp.sum(functools.reduce(jnp.add, picks), axis=0, keepdims=True)
    tasks = jnp.floor((count + (GROUP - 1)) * (1.0 / GROUP))
    earlier = jnp.dot(
        jnp.broadcast_to(tasks, (8, blocks)).astype(jnp.bfloat16),
        before(blocks, 0),
        preferred_element_type=jnp.float32,
    )[:1]
    base = earlier * GROUP
    row_before = before(rows, 1)
    slot = lax.broadcasted_iota(jnp.int32, (rows, slots), 1)
    place = jnp.full((rows, slots), -1.0, jnp.float32)
    for j in range(slots):
        above = jnp.dot(row_before, picks[j].astype(jnp.bfloat16), preferred_element_type=jnp.float32)
        here = jnp.sum(picks[j] * (above + base), axis=1, keepdims=True)
        place = jnp.where((slot == j) & mine, here, place)
        base = base + jnp.sum(picks[j], axis=0, keepdims=True)
    place_ref[...] = place
    size = blocks // PHASES
    end = earlier + tasks
    block_lane = lax.broadcasted_iota(jnp.int32, (1, blocks), 1)
    bound_lane = lax.broadcasted_iota(jnp.int32, (1, LANES), 1)
    bounds = jnp.zeros((1, LANES), jnp.float32)
    for part in range(PHASES):
        done = jnp.sum(jnp.where(block_lane == (part + 1) * size - 1, end, 0.0), axis=1, keepdims=True)
        done = done * (1.0 / TASKS)
        done = jnp.ceil(done) if part == PHASES - 1 else jnp.floor(done)
        bounds = jnp.where(bound_lane == part + 1, done, bounds)
    bound_ref[...] = bounds.astype(jnp.int32)


def list_kernel(
    spare, place_ref, value_ref, joined_ref, key_hbm, value_hbm, list_ref, first_key_ref, first_value_ref, sems
):
    rows, slots = place_ref.shape
    span = pl.ds(0, first_key_ref.shape[0])
    copies = [
        pltpu.make_async_copy(key_hbm.at[span], first_key_ref, sems.at[0]),
        pltpu.make_async_copy(value_hbm.at[span], first_value_ref, sems.at[1]),
    ]
    for copy in copies:
        copy.start()
    capacity = list_ref.shape[1]
    target = lax.broadcasted_iota(jnp.int32, (8, capacity), 1).astype(jnp.float32)

    def tile(t, total):
        here = pl.ds(pl.multiple_of(t * 8, 8), 8)
        places, values = place_ref[here, :], value_ref[here, :]
        for j in range(slots):
            total = total + jnp.where(places[:, j : j + 1] == target, values[:, j : j + 1], 0.0)
        return total

    total = lax.fori_loop(0, rows // 8, tile, jnp.zeros((8, capacity), jnp.float32))
    list_ref[...] = (jnp.sum(total, axis=0, keepdims=True) + spare).astype(jnp.int32)
    for copy in copies:
        copy.wait()


def make_places(parts, slots, blocks, block_size, count):
    own, width = parts[0].shape
    rows = count * own
    last = width // (PAIR * LANES) - 1
    table = jax.ShapeDtypeStruct((rows, slots), jnp.float32)
    bounds = jax.ShapeDtypeStruct((1, LANES), jnp.int32)
    return pl.pallas_call(
        functools.partial(place_kernel, blocks, block_size, slots),
        grid=(1,),
        in_specs=[pl.BlockSpec((own, PAIR * LANES), lambda i: (0, last))] * len(parts),
        out_specs=[pl.BlockSpec(x.shape, lambda i: (0, 0)) for x in (table, table, bounds)],
        out_shape=[table, table, bounds],
        compiler_params=params(16),
        cost_estimate=pl.CostEstimate(flops=10**8, bytes_accessed=4 * 10**6, transcendentals=0),
        name="slot_places",
    )(*parts)


def make_list(places, slot_values, joined, keys, values, block_size, count):
    blocks = keys.shape[0]
    rows, slots = places.shape
    most = 2 * rows * slots // count // count * count + (GROUP - 1) * blocks + 3 * CHUNK
    capacity = -(-most // LANES) * LANES
    return pl.pallas_call(
        functools.partial(list_kernel, float(rows * blocks * block_size)),
        in_specs=[vmem_spec()] * 3 + [hbm_spec()] * 2,
        out_specs=[vmem_spec()] * 3,
        out_shape=[jax.ShapeDtypeStruct((1, capacity), jnp.int32)]
        + [jax.ShapeDtypeStruct((blocks // PHASES, *x.shape[1:]), x.dtype) for x in (keys, values)],
        scratch_shapes=[pltpu.SemaphoreType.DMA((2,))],
        compiler_params=params(16),
        cost_estimate=pl.CostEstimate(flops=10**8, bytes_accessed=4 * 10**6, transcendentals=0),
        name="slot_list",
    )(places, slot_values, joined, *in_hbm(keys, values))


def join_kernel(*refs):
    pieces, out_ref = refs[:-2], refs[-1]
    for s, piece in enumerate(pieces):
        out_ref[s] = piece[...]


def join(pieces, places):
    return pl.pallas_call(
        join_kernel,
        in_specs=[vmem_spec()] * (len(pieces) + 1),
        out_specs=vmem_spec(),
        out_shape=jax.ShapeDtypeStruct((len(pieces), *pieces[0].shape), pieces[0].dtype),
        compiler_params=params(16),
        name="join",
    )(*pieces, places)


def attend_kernel(scale, kv_local, count, list_vmem, bound_vmem, *refs):
    queries, first_refs, refs = refs[:PAIR], refs[PAIR : PAIR + 2], refs[PAIR + 2 :]
    (key_hbm, value_hbm, keep_ref, send_ref, list_ref, bound_ref, query_ref, key_ref, value_ref) = refs[:9]
    (score_ref, part_top_ref, part_total_ref, part_sum_ref, number_sems, sems) = refs[9:15]
    states = [refs[15 + 3 * k : 18 + 3 * k] for k in range(SETS)]
    heads = query_ref.shape[1]
    rows = query_ref.shape[0] - 1
    own = rows // count
    blocks, tokens, _ = key_ref.shape
    block_size = tokens // kv_local
    length_bits = (block_size - 1).bit_length()
    block_bits = (blocks - 1).bit_length()
    numbers = (
        pltpu.make_async_copy(list_vmem, list_ref, number_sems.at[0]),
        pltpu.make_async_copy(bound_vmem, bound_ref, number_sems.at[1]),
    )
    size = blocks // PHASES
    spans = [pl.ds(part * size, size) for part in range(PHASES)]
    copies = [
        (
            pltpu.make_async_copy(key_hbm.at[span], key_ref.at[span], sems.at[0, part]),
            pltpu.make_async_copy(value_hbm.at[span], value_ref.at[span], sems.at[1, part]),
        )
        for part, span in enumerate(spans)
    ]
    for pair in (numbers, *copies[1 : 1 + AHEAD]):
        for copy in pair:
            copy.start()
    for ref, first_ref in zip((key_ref, value_ref), first_refs):
        ref[:size] = first_ref[...]

    factor = scale * LOG2E
    for t, piece in enumerate(queries):
        for s in range(count // PAIR):
            start = (PAIR * s + t) * own
            query_ref[start : start + own] = piece[s]
    query_ref[rows] = jnp.zeros((heads, LANES), jnp.bfloat16)
    for state in states:
        for ref, value in zip(state, (NEG_FILL, 0.0, 0.0)):
            ref[...] = jnp.full(ref.shape, value, jnp.float32)
    for ref in (score_ref, part_top_ref, part_total_ref, part_sum_ref):
        ref[...] = jnp.zeros(ref.shape, jnp.float32)
    group = heads // kv_local
    column = lax.broadcasted_iota(jnp.int32, (group, tokens), 1)
    first = column % kv_local == 0
    wide = (heads, LANES)
    narrow = (group, LANES)

    def entries(chunk):
        return [list_ref[0, chunk * CHUNK + j] for j in range(CHUNK)]

    def row_of(entry):
        return entry >> (length_bits + block_bits)

    def block_of(entry):
        return (entry >> length_bits) & (blocks - 1)

    def merge_slots(row, start):
        before = [[ref[r] for ref in state] for r, state in zip(row, states)]
        after = []
        for k, (top, total, acc) in enumerate(before):
            t, place = divmod(start + k, GROUP)
            part_top = part_top_ref[start + k]
            share = jnp.exp2(-jnp.abs(top - part_top) * factor)
            lower = top < part_top
            old, new = jnp.where(lower, share, 1.0), jnp.where(lower, 1.0, share)
            after.append(
                (
                    jnp.maximum(top, part_top),
                    total * old + part_total_ref[start + k] * new,
                    acc * old + part_sum_ref[t, place * heads : (place + 1) * heads] * new,
                )
            )
        for r, state, new in zip(row, states, after):
            for ref, value in zip(state, new):
                ref[r] = value

    def weigh_item(entry, t, k):
        j = t * GROUP + k
        start = k * heads
        scores = jnp.where(
            first, score_ref[t, start : start + group], score_ref[t, start + group : start + heads]
        )
        length = (entry & (block_size - 1)) + 1
        scores = jnp.where(column < length * kv_local, scores, NEG_FILL)
        tops = [
            jnp.max(x, axis=1, keepdims=True)
            for x in (jnp.where(first, scores, NEG_FILL), jnp.where(first, NEG_FILL, scores))
        ]
        weights = jnp.exp2((scores - jnp.where(first, tops[0], tops[1])) * factor)
        weights = (jnp.where(first, weights, 0.0), jnp.where(first, 0.0, weights))
        for a in range(kv_local):
            here = slice(a * group, (a + 1) * group)
            part_top_ref[j, here] = jnp.broadcast_to(tops[a], narrow)
            part_total_ref[j, here] = jnp.broadcast_to(jnp.sum(weights[a], axis=1, keepdims=True), narrow)
        return jnp.concatenate(weights, axis=0).astype(jnp.bfloat16)

    def turn(stages, i, carry):
        merged, weighed, scored = (entries(jnp.maximum(i - back, 0)) for back in (2, 1, 0))
        for t in range(TASKS):
            task = slice(t * GROUP, (t + 1) * GROUP)
            for start in range(t * GROUP, (t + 1) * GROUP, SETS):
                merge_slots(
                    [jnp.where(i >= 2, row_of(entry), rows) for entry in merged[start : start + SETS]], start
                )
            if stages > 1:
                weights = [weigh_item(entry, t, k) for k, entry in enumerate(weighed[task])]
                part_sum_ref[t] = jnp.dot(
                    jnp.concatenate(weights, axis=0),
                    value_ref[block_of(weighed[task][0])],
                    preferred_element_type=jnp.float32,
                )
            if stages > 2:
                score_ref[t] = lax.dot_general(
                    jnp.concatenate([query_ref[row_of(entry)] for entry in scored[task]], axis=0),
                    key_ref[block_of(scored[task][0])],
                    (((1,), (1,)), ((), ())),
                    preferred_element_type=jnp.float32,
                )
        return carry

    for copy in numbers:
        copy.wait()
    for part in range(PHASES):
        if part > 0:
            for copy in copies[part]:
                copy.wait()
            for pair in copies[part + AHEAD : part + AHEAD + 1]:
                for copy in pair:
                    copy.start()
        lax.fori_loop(bound_ref[0, part], bound_ref[0, part + 1], functools.partial(turn, 3), 0)
    last = bound_ref[0, PHASES]
    turn(2, last, 0)
    turn(1, last + 1, 0)

    square = (own * heads, LANES)
    eye = lax.broadcasted_iota(jnp.int32, square, 0) == lax.broadcasted_iota(jnp.int32, square, 1)
    line = lax.broadcasted_iota(jnp.int32, wide, 0)
    for q in range(count):
        ref = (keep_ref, send_ref)[q % PAIR]
        mine = slice(q * own, (q + 1) * own)
        tops = [top_ref[mine] for top_ref, _, _ in states]
        high = functools.reduce(jnp.maximum, tops)
        shares = [jnp.exp2((top - high) * factor) for top in tops]
        total = sum(total_ref[mine] * share for (_, total_ref, _), share in zip(states, shares))
        ref[q // PAIR, :own] = sum(sum_ref[mine] * share for (_, _, sum_ref), share in zip(states, shares))
        high, total = (
            jnp.sum(jnp.where(eye, x.reshape(square), 0.0), axis=0, keepdims=True) for x in (high, total)
        )
        ref[q // PAIR, own] = jnp.where(line == 0, high, jnp.where(line == 1, total, 0.0))


def attend(items, bounds, queries, first, keys, values, kv_local, scale):
    chips, own, heads, _ = queries[0].shape
    count = chips * PAIR
    rows = count * own
    tokens = keys.shape[1]
    keys, values = in_hbm(keys, values)
    state = pltpu.VMEM((rows + 1, heads, LANES), jnp.float32)
    part = pltpu.VMEM((CHUNK, heads, LANES), jnp.float32)
    return pl.pallas_call(
        functools.partial(attend_kernel, scale, kv_local, count),
        in_specs=[vmem_spec()] * (4 + len(queries)) + [hbm_spec()] * 2,
        out_specs=[vmem_spec()] * PAIR,
        out_shape=[jax.ShapeDtypeStruct((count // PAIR, own + 1, heads, LANES), jnp.float32)] * PAIR,
        scratch_shapes=[
            pltpu.SMEM(items.shape, items.dtype),
            pltpu.SMEM(bounds.shape, bounds.dtype),
            pltpu.VMEM((rows + 1, heads, LANES), jnp.bfloat16),
            pltpu.VMEM(keys.shape, keys.dtype),
            pltpu.VMEM(values.shape, values.dtype),
            pltpu.VMEM((TASKS, GROUP * heads, tokens), jnp.float32),
            part,
            part,
            pltpu.VMEM((TASKS, GROUP * heads, LANES), jnp.float32),
            pltpu.SemaphoreType.DMA((2,)),
            pltpu.SemaphoreType.DMA((2, PHASES)),
        ]
        + [state] * (3 * SETS),
        compiler_params=params(28 + 3 * SETS * rows * heads * LANES * 4 // MIB),
        name="attend",
    )(items, bounds, *queries, *first, keys, values)


def merge_pair_kernel(scale, keep_ref, got_ref, out_ref):
    chips, sections, heads, _ = keep_ref.shape
    own = sections - 1
    factor = scale * LOG2E
    line = lax.broadcasted_iota(jnp.int32, (heads, LANES), 0)
    shares, stats = [], []
    for s in range(chips):
        keep, got = keep_ref[s, own], got_ref[s, own]
        high = jnp.maximum(keep[0:1], got[0:1])
        pair = [jnp.exp2((x[0:1] - high) * factor) for x in (keep, got)]
        shares += pair
        total = pair[0] * keep[1:2] + pair[1] * got[1:2]
        stat = jnp.zeros((heads, LANES), jnp.float32)
        for position, piece in enumerate(split3(high) + split3(total)):
            stat = jnp.where(line == position, piece, stat)
        stats.append(stat)
    columns = jnp.concatenate(shares, axis=0).T
    flat = (own * heads, LANES)
    for s in range(chips):
        total = keep_ref[s, :own].reshape(flat) * columns[:, PAIR * s : PAIR * s + 1]
        total = total + got_ref[s, :own].reshape(flat) * columns[:, PAIR * s + 1 : PAIR * s + 2]
        out_ref[s, :own] = total.astype(jnp.bfloat16).reshape(own, heads, LANES)
        out_ref[s, own] = stats[s].astype(jnp.bfloat16)


def merge_pair(keep, got, scale):
    return pl.pallas_call(
        functools.partial(merge_pair_kernel, scale),
        in_specs=[vmem_spec()] * 2,
        out_specs=vmem_spec(),
        out_shape=jax.ShapeDtypeStruct(keep.shape, jnp.bfloat16),
        compiler_params=params(16),
        name="merge_pair",
    )(keep, got)


def merge_kernel(scale, *refs):
    pieces, (out_ref, wide_ref) = refs[:-2], refs[-2:]
    chips, sections, heads, _ = pieces[0].shape
    own = sections - 1
    factor = scale * LOG2E
    shares = []
    for s in range(chips):
        stats = [pieces[j][s ^ j, own].astype(jnp.float32) for j in range(chips)]
        tops = jnp.concatenate([x[0:1] + x[1:2] + x[2:3] for x in stats], axis=0)
        totals = jnp.concatenate([x[3:4] + x[4:5] + x[5:6] for x in stats], axis=0)
        weights = jnp.exp2((tops - jnp.max(tops, axis=0, keepdims=True)) * factor)
        shares.append(weights / jnp.sum(weights * totals, axis=0, keepdims=True))
    columns = jnp.concatenate(shares, axis=0).T
    flat = own * heads
    for s in range(chips):
        total = jnp.zeros((flat, LANES), jnp.float32)
        for j in range(chips):
            part = pieces[j][s ^ j, :own].astype(jnp.float32).reshape(flat, LANES)
            total = total + part * columns[:, s * chips + j : s * chips + j + 1]
        wide_ref[s * flat : (s + 1) * flat, :] = total
    rows = [wide_ref[pl.ds(h, chips * own, stride=heads), :] for h in range(heads)]
    out_ref[...] = jnp.concatenate(rows, axis=1).astype(jnp.bfloat16)


def merge(pieces, scale):
    chips, sections, heads, _ = pieces[0].shape
    own = sections - 1
    return pl.pallas_call(
        functools.partial(merge_kernel, scale),
        in_specs=[vmem_spec()] * chips,
        out_specs=vmem_spec(),
        out_shape=jax.ShapeDtypeStruct((chips * own, heads * LANES), jnp.bfloat16),
        scratch_shapes=[pltpu.VMEM((chips * own * heads, LANES), jnp.float32)],
        compiler_params=params(32),
        name="merge",
    )(*pieces)


def own_output_kernel(piece_ref, weight_ref, out_ref):
    out_ref[...] = jnp.dot(piece_ref[...], weight_ref[...], preferred_element_type=jnp.float32)


def output_kernel(own, done_ref, piece_ref, weight_ref, *refs):
    outs, terms_ref = refs[:-1], refs[-1]
    me = lax.axis_index("kv")
    products = (done_ref[...], jnp.dot(piece_ref[...], weight_ref[...], preferred_element_type=jnp.float32))
    for t, product in enumerate(products):
        for s in range(product.shape[0] // own):
            start = pl.multiple_of(jnp.bitwise_xor(me, PAIR * s + t) * own, own)
            terms_ref[pl.ds(start, own), :] = product[s * own : (s + 1) * own]
    me = lax.axis_index("row")
    part = outs[0].shape[0]
    for s, ref in enumerate(outs):
        start = pl.multiple_of(jnp.bitwise_xor(me, s) * part, part)
        ref[...] = terms_ref[pl.ds(start, part), :].astype(ref.dtype)


def project_own(piece, weight):
    half, width = piece.shape
    columns = weight.shape[1]
    return pl.pallas_call(
        own_output_kernel,
        in_specs=[vmem_spec()] * 2,
        out_specs=vmem_spec(),
        out_shape=jax.ShapeDtypeStruct((half, columns), jnp.float32),
        compiler_params=params(16),
        cost_estimate=pl.CostEstimate(
            flops=2 * half * width * columns, bytes_accessed=2 * width * columns, transcendentals=0
        ),
        name="project_own",
    )(piece, weight)


def project_out(done, piece, weight, own, row_count):
    half, columns = done.shape
    rows = PAIR * half
    shape = (rows // row_count, columns)
    send = jax.ShapeDtypeStruct(shape, jnp.bfloat16)
    return pl.pallas_call(
        functools.partial(output_kernel, own),
        in_specs=[vmem_spec()] * 3,
        out_specs=[vmem_spec()] * row_count,
        out_shape=[jax.ShapeDtypeStruct(shape, jnp.float32)] + [send] * (row_count - 1),
        scratch_shapes=[pltpu.VMEM((rows, columns), jnp.float32)],
        compiler_params=params(16),
        name="project_out",
    )(done, piece, weight)


def exchange(x, axis, s):
    count = lax.axis_size(axis)
    return lax.ppermute(x, axis, [(i, i ^ s) for i in range(count)])


def gather_chips(x):
    return [x] + [exchange(x, "kv", s) for s in range(PAIR, lax.axis_size("kv"), PAIR)]


def local(
    hidden,
    query_weight,
    adapter_down_weight,
    adapter_up_weight,
    query_norm_gain,
    paged_key_cache,
    paged_value_cache,
    output_weight,
    holder,
    holder_block_index,
    block_used_length,
    tenant,
    tenant_adapter,
):
    own, slots = holder.shape
    rows, depth = hidden.shape
    kv_count = lax.axis_size("kv")
    row_count = lax.axis_size("row")
    adapters, _, rank = adapter_down_weight.shape
    width = query_weight.shape[1]
    head_size = query_norm_gain.shape[0]
    heads = width // head_size
    blocks, block_size, kv_local, _ = paged_key_cache.shape
    scale = 1.0 / math.sqrt(head_size)

    chips = kv_count // PAIR
    keep, send, up = project(
        tenant,
        tenant_adapter,
        holder,
        holder_block_index,
        block_used_length,
        hidden,
        query_weight,
        jnp.swapaxes(adapter_down_weight, 1, 2).reshape(adapters * rank, depth),
        adapter_up_weight,
        rank,
        chips,
    )
    parts = add_pair(keep, exchange(send, "kv", 1), 3 * slots)
    parts = [parts[0]] + [exchange(parts[s], "kv", PAIR * s) for s in range(1, chips)]

    position = (jnp.sum(block_used_length, axis=1) - 1).astype(jnp.float32)
    half = head_size // 2
    frequency = ROPE_BASE ** (-(jnp.arange(half, dtype=jnp.float32) * 2.0) / head_size)
    angles = position[:, None] * frequency[None, :]
    cosine = jnp.concatenate([jnp.cos(angles), jnp.cos(angles)], axis=-1)
    sine = jnp.concatenate([-jnp.sin(angles), jnp.sin(angles)], axis=-1)
    queries = make_queries(parts, up, cosine, sine, query_norm_gain.reshape(1, head_size), heads, 3 * slots)
    places, slot_values, bounds = make_places(parts, slots, blocks, block_size, kv_count)
    queries = join(gather_chips(queries), places)
    keys = paged_key_cache.reshape(blocks, block_size * kv_local, head_size)
    values = paged_value_cache.reshape(blocks, block_size * kv_local, head_size)
    items, *first = make_list(places, slot_values, queries, keys, values, block_size, kv_count)
    queries = [queries, exchange(queries, "kv", 1)]
    keep, send = attend(items, bounds, queries, first, keys, values, kv_local, scale)
    merged = merge_pair(keep, exchange(send, "kv", 1), scale)
    attention = merge(gather_chips(merged), scale)
    done = project_own(attention, output_weight)
    terms = project_out(done, exchange(attention, "kv", 1), output_weight, own, row_count)
    total = terms[0]
    for s in range(1, row_count):
        total = total + exchange(terms[s], "row", s).astype(jnp.float32)
    return total.astype(jnp.bfloat16)


def solution(mesh):
    return jax.shard_map(
        local,
        mesh=mesh,
        in_specs=(
            P(None, "kv"),
            P("kv", "row"),
            P(None, "kv", None),
            P(None, None, "row"),
            P(),
            P("kv", None, "row", None),
            P("kv", None, "row", None),
            P("row", "kv"),
            P("kv", None),
            P("kv", None),
            P("kv", None),
            P(),
            P(),
        ),
        out_specs=P("row", "kv"),
        check_vma=False,
    )
```
